128 devices in a mesh: dp: 32 (over x, y, z_hi), ctx: 4 (over z_lo, core).
Axes of the slice: x: 4, y: 4, z: 4 (z_hi: 2, z_lo: 2; z = z_hi * 2 + z_lo), core: 2. Of those that a mesh axis runs over, the one named last changes fastest.
Arguments:
- tokens: bfloat16 [32768, 4096], P(('dp', 'ctx')), may hold values from -28 to 28
- projection: bfloat16 [4096, 3072], P('dp'), may hold values from -0.09375 to 0.09375
- placement: int32 [128, 128], P(('dp', 'ctx')), may hold values from 0 to 127, each once within a row
- doc_lengths: int32 [32, 8], P('dp'), may hold values from 1 to 512, 1024 in all within a row
Outputs:
- attended: bfloat16 [32768, 2048], P(('dp', 'ctx'))
The draws below stay inside these ranges and needn't reach their ends.
Inputs may be any that keep to these rules, and one draw needn't show every extreme that they name: `placement`: row i lists for each of the 2-row pieces of loader block i the device that computes it; every device appears once in each row. `doc_lengths`: each row holds the documents of one packed sequence of 1024 tokens in order, one of exactly 512 tokens.
All inputs are finite; a program needn't handle non-finite values.
Results may differ from the reference program's by a relative error of at most 0.006.
The reference program's roundings to bfloat16 on the way count: a program that leaves them out, or rounds other values in their place, can miss the bound.
Values may be sent and summed in bfloat16 or wider, within the bound.
No kernel may reach another device: no remote copies, remote signals or barrier semaphores. Data moves between devices by JAX's collectives and lax.ppermute only.
A program may use at most 128 MiB of HBM per device.

```python
import math
from functools import partial
import jax
import jax.numpy as jnp
import numpy as np
from jax import lax

D = 4096
HEAD_DIM = 128
HEADS = 16
KV_HEADS = 4
DOCS = 8
SEQS = 32
SEQ = 1024
MOST = 512
PIECE = 2
TOKENS = 32768
QKV_W = 3072
DEVICES = 128


def draw_tokens(key, part):
    key = jax.random.fold_in(key, 11)
    former = jax.random.fold_in(key, 0)
    values = jnp.clip(jax.random.normal(former, (TOKENS, D), jnp.float32), -6.0, 6.0)
    return values.astype(jnp.bfloat16)


def shard_levels(rng, extent, cuts, low, largest):
    loudness = 1.0
    for axis_at, blocks in cuts:
        steps = jax.random.uniform(jax.random.fold_in(jax.random.fold_in(rng, 6), axis_at), (blocks,), jnp.float32, low / len(cuts), largest / len(cuts))
        loudness = loudness * jnp.repeat(jnp.exp(steps), extent[axis_at] // blocks).reshape((-1,) + (1,) * (len(extent) - 1 - axis_at))
    return loudness


def split_up(number_of, total, most, lean):
    weights = [(1 << 20) // math.isqrt(standing ** lean) + 1 for standing in range(2, number_of + 1)]
    spare, holding = total - most - (number_of - 1), [1] * (number_of - 1)
    while spare > 0:
        candidates = [i for i in range(number_of - 1) if holding[i] < most]
        pool, budget = sum([weights[i] for i in candidates]), spare
        for i in candidates:
            extra = min(most - holding[i], max(1, budget * weights[i] // pool), spare)
            holding[i] = holding[i] + extra
            spare = spare - extra
    return np.array([most] + holding)


def uneven_parts(rng, number_of, total, bound, slope):
    if number_of == 2:
        one = jax.random.randint(rng, (), max(1, total - bound), min(bound, total - 1) + 1)
        return jnp.stack([one, total - one])
    tallies = jnp.asarray(split_up(number_of, total, bound, slope), jnp.int32)
    twos = (number_of - 1) // 2
    source_of, receiver = tallies[1:1 + 2 * twos:2], tallies[2:2 + 2 * twos:2]
    margin = jnp.minimum(source_of - 1, bound - receiver)
    moved = jax.random.randint(jax.random.fold_in(rng, 1), (twos,), 0, 1 << 20) % (margin + 1)
    tallies = tallies.at[1:1 + 2 * twos:2].set(source_of - moved).at[2:2 + 2 * twos:2].set(receiver + moved)
    return tallies[jax.random.permutation(jax.random.fold_in(rng, 2), number_of)]


def bell_draw(rng, shape, scale, most, shards=(), held_as=jnp.bfloat16):
    level = shard_levels(rng, shape, shards, -0.22, 0.18) if shards else 1.0
    values = jax.random.normal(rng, shape, jnp.float32) * scale * level
    return jnp.minimum(jnp.maximum(values, -most), most).astype(held_as)


def setup_inputs(seed: int = 0) -> dict:
    keys = jax.random.split(jax.random.key(seed), 5)
    tokens = draw_tokens(jax.random.fold_in(keys[4], 71), 0)
    projection = bell_draw(keys[1], (D, QKV_W), D ** -0.5, 0.09375, ((0, 32),))
    placement = jax.vmap(lambda own: jax.random.permutation(own, DEVICES))(jax.random.split(keys[2], DEVICES)).reshape((DEVICES, DEVICES)).astype(jnp.int32)
    doc_lengths = jax.vmap(lambda own: uneven_parts(own, DOCS, SEQ, MOST, 2))(jax.random.split(keys[3], SEQS)).reshape((SEQS, DOCS)).astype(jnp.int32)
    return {"tokens": tokens, "projection": projection, "placement": placement, "doc_lengths": doc_lengths}


theta_base = 500000.0


def doc_tables(lengths, position):
    doc_ends = jnp.cumsum(lengths).astype(jnp.int32)
    doc_starts = doc_ends - lengths
    segment = jnp.sum((position[:, None] >= doc_ends[None, :]).astype(jnp.int32), axis=1)
    one_hot = segment[:, None] == jnp.arange(lengths.shape[0], dtype=jnp.int32)[None, :]
    begins = jnp.sum(jnp.where(one_hot, doc_starts[None, :], 0), axis=1).astype(jnp.int32)
    return segment, position - begins


def rotate(values, offsets, head_count):
    row_count = values.shape[0]
    half_dim = HEAD_DIM // 2
    frequency = theta_base ** (-2.0 * jnp.arange(half_dim, dtype=jnp.float32) / HEAD_DIM)
    angles = offsets.astype(jnp.float32)[:, None] * frequency[None, :]
    cosine = jnp.cos(angles)[:, None, :]
    sine = jnp.sin(angles)[:, None, :]
    halves = values.astype(jnp.float32).reshape(row_count, head_count, 2, half_dim)
    former = halves[:, :, 0]
    latter = halves[:, :, 1]
    result = jnp.stack([former * cosine - latter * sine, latter * cosine + former * sine], axis=2)
    return result.reshape(row_count, head_count * HEAD_DIM).astype(jnp.bfloat16)


def one_sequence(weight_matrix, inputs):
    rows_in, lengths = inputs
    projected = jnp.dot(rows_in, weight_matrix, preferred_element_type=jnp.float32).astype(jnp.bfloat16)
    position = jnp.arange(SEQ, dtype=jnp.int32)
    segment, offsets = doc_tables(lengths, position)
    query_width = HEADS * HEAD_DIM
    key_width = KV_HEADS * HEAD_DIM
    queries = rotate(projected[:, :query_width], offsets, HEADS)
    key_rows = rotate(projected[:, query_width:query_width + key_width], offsets, KV_HEADS)
    value_rows = projected[:, query_width + key_width:]
    group_size = HEADS // KV_HEADS
    query_heads = queries.astype(jnp.float32).reshape(SEQ, KV_HEADS, group_size, HEAD_DIM)
    key_heads = key_rows.astype(jnp.float32).reshape(SEQ, KV_HEADS, HEAD_DIM)
    value_heads = value_rows.astype(jnp.float32).reshape(SEQ, KV_HEADS, HEAD_DIM)
    scores = jnp.einsum("tkgd,skd->tkgs", query_heads, key_heads) * (HEAD_DIM ** -0.5)
    allowed = (segment[:, None] == segment[None, :]) & (position[None, :] <= position[:, None])
    scores = jnp.where(allowed[:, None, None, :], scores, -jnp.inf)
    row_max = jnp.max(scores, axis=-1, keepdims=True)
    weights = jnp.exp(scores - row_max)
    row_sum = jnp.sum(weights, axis=-1)
    rounded = lax.optimization_barrier(weights.astype(jnp.bfloat16)).astype(jnp.float32)
    mixed = jnp.einsum("tkgs,skd->tkgd", rounded, value_heads) / row_sum[..., None]
    return mixed.reshape(SEQ, HEADS * HEAD_DIM).astype(jnp.bfloat16)


def reference(tokens, projection, placement, doc_lengths):
    home_rows = tokens.reshape(DEVICES, DEVICES, PIECE, D)
    source = jnp.broadcast_to(jnp.arange(DEVICES, dtype=jnp.int32)[:, None], (DEVICES, DEVICES))
    work_rows = jnp.zeros_like(home_rows).at[placement, source].set(home_rows)
    grouped = work_rows.reshape(SEQS, SEQ, D)
    mixed = lax.map(partial(one_sequence, projection), (grouped, doc_lengths))
    mixed = mixed.reshape(DEVICES, DEVICES, PIECE, HEADS * HEAD_DIM)
    return mixed[placement, source].reshape(TOKENS, HEADS * HEAD_DIM)
```

```python
import functools

import jax
import jax.numpy as jnp
from jax import lax
from jax.experimental import pallas as pl
from jax.experimental.pallas import tpu as pltpu
from jax.sharding import Mesh, PartitionSpec as P

HEAD_DIM = 128
HEADS = 16
KV_HEADS = 4
GROUP = HEADS // KV_HEADS
THETA = 500000.0
MOST = 512
DP = ("x", "y", "zh")
CTX = ("zl", "core")
EVERY = DP + CTX
BLOCK = 256


def frequencies():
    half = HEAD_DIM // 2
    return THETA ** (-2.0 * jnp.arange(half, dtype=jnp.float32) / HEAD_DIM)


def rotary_tables(lengths, count):
    position = jnp.arange(count, dtype=jnp.int32)
    ends = jnp.cumsum(lengths)
    begins = jnp.sum(jnp.where(position[:, None] >= ends[None, :], lengths[None, :], 0), axis=1)
    angles = (position - begins).astype(jnp.float32)[:, None] * frequencies()[None, :]
    cosine, sine = jnp.cos(angles), jnp.sin(angles)
    return jnp.concatenate([cosine, cosine], axis=1), jnp.concatenate([-sine, sine], axis=1)


def sort_kernel(target_ref, rows_ref, out_ref):
    count = rows_ref.shape[0]
    order = lax.broadcasted_iota(jnp.int32, (count, count), 0)
    one_hot = jnp.where(order == target_ref[...], 1.0, 0.0).astype(jnp.bfloat16)
    moved = jnp.dot(one_hot, rows_ref[...], preferred_element_type=jnp.float32).astype(jnp.bfloat16)
    groups, copies, rows, width = out_ref.shape
    for copy in range(copies):
        out_ref[:, copy] = moved.reshape(groups, rows, width)


def sort_rows(tokens, target, groups, copies):
    count, width = tokens.shape
    rows = count // groups
    tile = 1024
    return pl.pallas_call(
        sort_kernel,
        out_shape=jax.ShapeDtypeStruct((groups, copies, rows, width), tokens.dtype),
        grid=(width // tile,),
        in_specs=[
            pl.BlockSpec((1, count), lambda i: (0, 0)),
            pl.BlockSpec((count, tile), lambda i: (0, i)),
        ],
        out_specs=pl.BlockSpec((groups, copies, rows, tile), lambda i: (0, 0, 0, i)),
        compiler_params=pltpu.CompilerParams(vmem_limit_bytes=32 * 2**20),
        name="sort_rows",
    )(target.reshape(1, count), tokens)


def unsort_kernel(target_ref, rows_ref, out_ref):
    count = out_ref.shape[0]
    order = lax.broadcasted_iota(jnp.int32, (count, count), 1)
    one_hot = jnp.where(order == target_ref[...], 1.0, 0.0).astype(jnp.bfloat16)
    rows = rows_ref[...].reshape(count, out_ref.shape[1])
    out_ref[...] = jnp.dot(one_hot, rows, preferred_element_type=jnp.float32).astype(jnp.bfloat16)


def unsort_rows(returned, target):
    groups, blocks, rows, width = returned.shape
    count = groups * rows
    return pl.pallas_call(
        unsort_kernel,
        out_shape=jax.ShapeDtypeStruct((count, blocks * width), returned.dtype),
        grid=(blocks,),
        in_specs=[
            pl.BlockSpec((count, 1), lambda i: (0, 0)),
            pl.BlockSpec((groups, None, rows, width), lambda i: (0, i, 0, 0)),
        ],
        out_specs=pl.BlockSpec((count, width), lambda i: (0, i)),
        compiler_params=pltpu.CompilerParams(vmem_limit_bytes=32 * 2**20),
        name="unsort_rows",
    )(target.reshape(count, 1), returned)


def attention_kernel(core_ref, lengths_ref, own_ref, other_ref, cos_ref, sin_ref, out_ref, queries, keys, values, mixed):
    count = cos_ref.shape[0]
    blocks = count // BLOCK
    part = BLOCK // blocks
    half = HEAD_DIM // 2
    core = core_ref[0]

    taken = lax.broadcasted_iota(jnp.int32, (BLOCK, BLOCK), 1)
    lane, rest = taken // (BLOCK // 2), taken % (BLOCK // 2)
    pair, slot, row = rest // (2 * blocks), (rest // 2) % blocks, rest % 2
    placed = slot * part + (pair * 2 + jnp.where(core == 0, lane, 1 - lane)) * 2 + row
    wanted = lax.broadcasted_iota(jnp.int32, (BLOCK, BLOCK), 0)
    forward = jnp.where(wanted == placed, 1.0, 0.0).astype(jnp.bfloat16)
    for h in range(blocks):
        span = slice(h * BLOCK // 2, (h + 1) * BLOCK // 2)
        chunk = jnp.concatenate([own_ref[span], other_ref[span]], axis=0)
        chunk = jnp.dot(forward, chunk, preferred_element_type=jnp.float32)
        for s in range(blocks):
            rows = slice(s * BLOCK + h * part, s * BLOCK + (h + 1) * part)
            here = chunk[s * part : (s + 1) * part]
            cosine, sine = cos_ref[rows], sin_ref[rows]

            def rotate(x):
                return (x * cosine + pltpu.roll(x, half, 1) * sine).astype(jnp.bfloat16)

            for g in range(GROUP):
                queries[g, rows] = rotate(here[:, g * HEAD_DIM : (g + 1) * HEAD_DIM])
            keys[rows] = rotate(here[:, GROUP * HEAD_DIM : (GROUP + 1) * HEAD_DIM])
            values[rows] = here[:, (GROUP + 1) * HEAD_DIM :].astype(jnp.bfloat16)

    scale = HEAD_DIM ** (-0.5)
    reach = (MOST - 1 + BLOCK - 1) // BLOCK
    for b in range(blocks):
        first = max(0, b - reach)
        width = (b + 1 - first) * BLOCK
        position = b * BLOCK + lax.broadcasted_iota(jnp.int32, (BLOCK, 1), 0)
        begin, end = jnp.zeros_like(position), jnp.int32(0)
        for j in range(lengths_ref.shape[1]):
            end = end + lengths_ref[0, j]
            begin = jnp.where(position >= end, end, begin)
        key_at = first * BLOCK + lax.broadcasted_iota(jnp.int32, (BLOCK, width), 1)
        allowed = (key_at >= begin) & (key_at <= position)
        key_block = keys[first * BLOCK : (b + 1) * BLOCK]
        value_block = values[first * BLOCK : (b + 1) * BLOCK]
        for g in range(GROUP):
            scores = lax.dot_general(
                queries[g, b * BLOCK : (b + 1) * BLOCK],
                key_block,
                (((1,), (1,)), ((), ())),
                preferred_element_type=jnp.float32,
            )
            scores = jnp.where(allowed, scores * scale, -1e30)
            weights = jnp.exp(scores - jnp.max(scores, axis=1, keepdims=True))
            total = jnp.sum(weights, axis=1, keepdims=True)
            weighted = jnp.dot(
                weights.astype(jnp.bfloat16), value_block, preferred_element_type=jnp.float32
            )
            mixed[b * BLOCK : (b + 1) * BLOCK, g * HEAD_DIM : (g + 1) * HEAD_DIM] = (
                weighted / total
            ).astype(jnp.bfloat16)

    left = lax.broadcasted_iota(jnp.int32, (BLOCK, BLOCK), 0)
    source = ((left // 2) % blocks) * part + (left // (2 * blocks)) * 2 + left % 2
    backward = jnp.where(taken == source, 1.0, 0.0).astype(jnp.bfloat16)
    for h in range(blocks):
        chunk = jnp.concatenate(
            [mixed[s * BLOCK + h * part : s * BLOCK + (h + 1) * part] for s in range(blocks)], axis=0
        )
        out_ref[h * BLOCK : (h + 1) * BLOCK] = jnp.dot(
            backward, chunk, preferred_element_type=jnp.float32
        ).astype(jnp.bfloat16)


def attend(core, lengths, own, other, cosine, sine):
    count = cosine.shape[0]
    whole = pl.BlockSpec(memory_space=pltpu.VMEM)
    scalars = pl.BlockSpec(memory_space=pltpu.SMEM)
    return pl.pallas_call(
        attention_kernel,
        out_shape=jax.ShapeDtypeStruct((count, GROUP * HEAD_DIM), jnp.bfloat16),
        in_specs=[scalars, scalars, whole, whole, whole, whole],
        out_specs=whole,
        scratch_shapes=[
            pltpu.VMEM((GROUP, count, HEAD_DIM), jnp.bfloat16),
            pltpu.VMEM((count, HEAD_DIM), jnp.bfloat16),
            pltpu.VMEM((count, HEAD_DIM), jnp.bfloat16),
            pltpu.VMEM((count, GROUP * HEAD_DIM), jnp.bfloat16),
        ],
        compiler_params=pltpu.CompilerParams(vmem_limit_bytes=48 * 2**20),
        name="attend",
    )(core, lengths, own, other, cosine, sine)


def on_device(tokens, projection, placement, doc_lengths):
    row_count, width = tokens.shape
    devices = placement.shape[1]
    members = lax.axis_size(CTX)
    groups = devices // members
    piece = row_count // devices
    member, core = lax.axis_index(CTX), lax.axis_index("core")

    query_width, key_width = HEADS * HEAD_DIM, KV_HEADS * HEAD_DIM
    columns = jnp.concatenate(
        [
            lax.dynamic_slice_in_dim(projection, member * GROUP * HEAD_DIM, GROUP * HEAD_DIM, 1),
            lax.dynamic_slice_in_dim(projection, query_width + member * HEAD_DIM, HEAD_DIM, 1),
            lax.dynamic_slice_in_dim(projection, query_width + key_width + member * HEAD_DIM, HEAD_DIM, 1),
        ],
        axis=1,
    )
    weights = lax.all_gather(columns, DP, axis=0, tiled=True)

    target = (placement[0][:, None] * piece + jnp.arange(piece, dtype=jnp.int32)[None, :]).reshape(row_count)
    outgoing = sort_rows(tokens, target, groups, 2)
    arrived = lax.all_to_all(
        outgoing.reshape(groups * 2, row_count // groups, width), DP + ("zl",), 0, 0, tiled=True
    )
    own_rows = arrived.reshape(2 * row_count, width)
    other_rows = lax.ppermute(own_rows, "core", [(0, 1), (1, 0)])
    own = jnp.dot(own_rows, weights, preferred_element_type=jnp.float32).astype(jnp.bfloat16)
    other = jnp.dot(other_rows, weights, preferred_element_type=jnp.float32).astype(jnp.bfloat16)
    cosine, sine = rotary_tables(doc_lengths[0], members * row_count)
    mixed = attend(core.reshape(1), doc_lengths, own, other, cosine, sine)
    returned = lax.all_to_all(
        mixed.reshape(devices, members * piece, GROUP * HEAD_DIM), EVERY, 0, 0, tiled=True
    )
    return unsort_rows(returned.reshape(groups, members, members * piece, GROUP * HEAD_DIM), target)


def solution(mesh):
    sizes = {"x": 4, "y": 4, "zh": 2, "zl": 2, "core": 2}
    fine = Mesh(mesh.devices.reshape(tuple(sizes.values())), tuple(sizes))
    return jax.shard_map(
        on_device,
        mesh=fine,
        in_specs=(P(EVERY, None), P(DP, None), P(EVERY, None), P(DP, None)),
        out_specs=P(EVERY, None),
        check_vma=False,
    )
```

```python
import functools

import jax
import jax.numpy as jnp
from jax import lax
from jax.experimental import pallas as pl
from jax.experimental.pallas import tpu as pltpu
from jax.sharding import Mesh, PartitionSpec as P

HEAD_DIM = 128
HEADS = 16
KV_HEADS = 4
GROUP = HEADS // KV_HEADS
THETA = 500000.0
MOST = 512
DP = ("x", "y", "zh")
CTX = ("zl", "core")
EVERY = DP + CTX
BLOCK = 256


def frequencies():
    half = HEAD_DIM // 2
    return THETA ** (-2.0 * jnp.arange(half, dtype=jnp.float32) / HEAD_DIM)


def rotary_tables(lengths, count):
    position = jnp.arange(count, dtype=jnp.int32)
    ends = jnp.cumsum(lengths)
    begins = jnp.sum(jnp.where(position[:, None] >= ends[None, :], lengths[None, :], 0), axis=1)
    angles = (position - begins).astype(jnp.float32)[:, None] * frequencies()[None, :]
    cosine, sine = jnp.cos(angles), jnp.sin(angles)
    return jnp.concatenate([cosine, cosine], axis=1), jnp.concatenate([-sine, sine], axis=1)


def sort_kernel(target_ref, rows_ref, out_ref):
    count = rows_ref.shape[0]
    order = lax.broadcasted_iota(jnp.int32, (count, count), 0)
    one_hot = jnp.where(order == target_ref[...], 1.0, 0.0).astype(jnp.bfloat16)
    moved = jnp.dot(one_hot, rows_ref[...], preferred_element_type=jnp.float32).astype(jnp.bfloat16)
    out_ref[...] = moved.reshape(out_ref.shape)


def sort_rows(tokens, target, groups):
    count, width = tokens.shape
    rows = count // groups
    tile = 1024
    return pl.pallas_call(
        sort_kernel,
        out_shape=jax.ShapeDtypeStruct((groups, rows, width), tokens.dtype),
        grid=(width // tile,),
        in_specs=[
            pl.BlockSpec((1, count), lambda i: (0, 0)),
            pl.BlockSpec((count, tile), lambda i: (0, i)),
        ],
        out_specs=pl.BlockSpec((groups, rows, tile), lambda i: (0, 0, i)),
        compiler_params=pltpu.CompilerParams(vmem_limit_bytes=32 * 2**20),
        name="sort_rows",
    )(target.reshape(1, count), tokens)


def unsort_kernel(target_ref, rows_ref, out_ref):
    count = out_ref.shape[0]
    order = lax.broadcasted_iota(jnp.int32, (count, count), 1)
    one_hot = jnp.where(order == target_ref[...], 1.0, 0.0).astype(jnp.bfloat16)
    rows = rows_ref[...].reshape(count, out_ref.shape[1])
    out_ref[...] = jnp.dot(one_hot, rows, preferred_element_type=jnp.float32).astype(jnp.bfloat16)


def unsort_rows(returned, target):
    groups, blocks, rows, width = returned.shape
    count = groups * rows
    return pl.pallas_call(
        unsort_kernel,
        out_shape=jax.ShapeDtypeStruct((count, blocks * width), returned.dtype),
        grid=(blocks,),
        in_specs=[
            pl.BlockSpec((count, 1), lambda i: (0, 0)),
            pl.BlockSpec((groups, None, rows, width), lambda i: (0, i, 0, 0)),
        ],
        out_specs=pl.BlockSpec((count, width), lambda i: (0, i)),
        compiler_params=pltpu.CompilerParams(vmem_limit_bytes=32 * 2**20),
        name="unsort_rows",
    )(target.reshape(count, 1), returned)


def own_columns(projection, member):
    query_width, key_width = HEADS * HEAD_DIM, KV_HEADS * HEAD_DIM
    return jnp.concatenate(
        [
            lax.dynamic_slice_in_dim(projection, member * GROUP * HEAD_DIM, GROUP * HEAD_DIM, 1),
            lax.dynamic_slice_in_dim(projection, query_width + member * HEAD_DIM, HEAD_DIM, 1),
            lax.dynamic_slice_in_dim(projection, query_width + key_width + member * HEAD_DIM, HEAD_DIM, 1),
        ],
        axis=1,
    )


def spread(block, axis):
    up, down = [(i, (i + 1) % 4) for i in range(4)], [(i, (i + 3) % 4) for i in range(4)]
    half = block.shape[0] // 2
    below, above = lax.ppermute(block, axis, up), lax.ppermute(block, axis, down)
    far_low = lax.ppermute(below[:half], axis, up)
    far_high = lax.ppermute(above[half:], axis, down)
    return [block, below, above, far_low, far_high]


RING = (0, 3, 1, 2)
SPAN = ((0, (0, 1, 2, 3)), (3, (0, 1, 2, 3)), (1, (0, 1, 2, 3)), (2, (0, 1)), (2, (2, 3)))


def gather_weights(projection, member):
    x, y, zh = lax.axis_index("x"), lax.axis_index("y"), lax.axis_index("zh")
    rows = projection.shape[0]
    mine = lax.all_gather(own_columns(projection, member), ("x", "y"), axis=0, tiled=True)
    theirs = lax.ppermute(own_columns(projection, member ^ 2), ("zh", "zl"), [(0, 3), (3, 0), (1, 2), (2, 1)])
    half = theirs.shape[1] // 2
    pieces = [mine]
    places = [(i * 2 + zh) * rows for i in range(16)]
    for side, (one, two) in enumerate((("y", "x"), ("x", "y"))):
        block = theirs[:, side * half : (side + 1) * half]
        pieces += spread(jnp.concatenate(spread(block, one), axis=0), two)
        for outer, inners in SPAN:
            for inner in inners:
                near, far = (outer, RING[inner]) if side == 0 else (RING[inner], outer)
                places.append(((x + near) % 4 * 8 + (y + far) % 4 * 2 + 1 - zh) * rows)
    return jnp.stack(places), pieces


def project_kernel(places_ref, rows_ref, *refs):
    pieces, out_ref, ordered = refs[:-2], refs[-2], refs[-1]
    width = out_ref.shape[1]
    half = width // 2
    step = 128

    def take(first, count):
        for i in range(count):
            column = pl.multiple_of(places_ref[first + i], step)
            ordered[:, i * step : (i + 1) * step] = rows_ref[:, pl.ds(column, step)]

    def product(parts):
        total, at = None, 0
        for part in parts:
            depth = part.shape[0]
            term = jnp.dot(ordered[:, at : at + depth], part[...], preferred_element_type=jnp.float32)
            total = term if total is None else total + term
            at += depth
        return total

    take(0, 16)
    out = product(pieces[:1])
    for side in range(2):
        take(16 + side * 16, 16)
        other = product(pieces[1 + side * 5 : 6 + side * 5])
        columns = slice(side * half, (side + 1) * half)
        out_ref[:, columns] = (out[:, columns] + other).astype(jnp.bfloat16)


def project(places, pieces, rows):
    count, depth = rows.shape
    width = pieces[0].shape[1]
    whole = pl.BlockSpec(memory_space=pltpu.VMEM)
    return pl.pallas_call(
        project_kernel,
        out_shape=jax.ShapeDtypeStruct((count, width), jnp.bfloat16),
        in_specs=[pl.BlockSpec(memory_space=pltpu.SMEM)] + [whole] * (1 + len(pieces)),
        out_specs=whole,
        scratch_shapes=[pltpu.VMEM((count, depth // 2), jnp.bfloat16)],
        compiler_params=pltpu.CompilerParams(vmem_limit_bytes=24 * 2**20),
        cost_estimate=pl.CostEstimate(
            flops=2 * count * depth * width, bytes_accessed=2 * depth * (width + count), transcendentals=0
        ),
        name="project",
    )(places, rows, *pieces)


def attention_kernel(member_ref, lengths_ref, *refs):
    lanes = refs[:4]
    cos_ref, sin_ref, out_ref, queries, keys, values, mixed = refs[4:]
    count = cos_ref.shape[0]
    blocks = count // BLOCK
    part = BLOCK // blocks
    half = HEAD_DIM // 2
    member = member_ref[0]

    taken = lax.broadcasted_iota(jnp.int32, (BLOCK, BLOCK), 1)
    lane, rest = taken // part, taken % part
    group, slot, row = rest // (2 * blocks), (rest // 2) % blocks, rest % 2
    placed = slot * part + (group * 4 + (lane ^ member)) * 2 + row
    wanted = lax.broadcasted_iota(jnp.int32, (BLOCK, BLOCK), 0)
    forward = jnp.where(wanted == placed, 1.0, 0.0).astype(jnp.bfloat16)
    for h in range(blocks):
        chunk = jnp.concatenate([lane_ref[h * part : (h + 1) * part] for lane_ref in lanes], axis=0)
        chunk = jnp.dot(forward, chunk, preferred_element_type=jnp.float32)
        for s in range(blocks):
            rows = slice(s * BLOCK + h * part, s * BLOCK + (h + 1) * part)
            here = chunk[s * part : (s + 1) * part]
            cosine, sine = cos_ref[rows], sin_ref[rows]

            def rotate(x):
                return (x * cosine + pltpu.roll(x, half, 1) * sine).astype(jnp.bfloat16)

            for g in range(GROUP):
                queries[g, rows] = rotate(here[:, g * HEAD_DIM : (g + 1) * HEAD_DIM])
            keys[rows] = rotate(here[:, GROUP * HEAD_DIM : (GROUP + 1) * HEAD_DIM])
            values[rows] = here[:, (GROUP + 1) * HEAD_DIM :].astype(jnp.bfloat16)

    scale = HEAD_DIM ** (-0.5)
    reach = (MOST - 1 + BLOCK - 1) // BLOCK
    for b in range(blocks):
        first = max(0, b - reach)
        width = (b + 1 - first) * BLOCK
        position = b * BLOCK + lax.broadcasted_iota(jnp.int32, (BLOCK, 1), 0)
        begin, end = jnp.zeros_like(position), jnp.int32(0)
        for j in range(lengths_ref.shape[1]):
            end = end + lengths_ref[0, j]
            begin = jnp.where(position >= end, end, begin)
        key_at = first * BLOCK + lax.broadcasted_iota(jnp.int32, (BLOCK, width), 1)
        allowed = (key_at >= begin) & (key_at <= position)
        key_block = keys[first * BLOCK : (b + 1) * BLOCK]
        value_block = values[first * BLOCK : (b + 1) * BLOCK]
        for g in range(GROUP):
            scores = lax.dot_general(
                queries[g, b * BLOCK : (b + 1) * BLOCK],
                key_block,
                (((1,), (1,)), ((), ())),
                preferred_element_type=jnp.float32,
            )
            scores = jnp.where(allowed, scores * scale, -1e30)
            weights = jnp.exp(scores - jnp.max(scores, axis=1, keepdims=True))
            total = jnp.sum(weights, axis=1, keepdims=True)
            weighted = jnp.dot(
                weights.astype(jnp.bfloat16), value_block, preferred_element_type=jnp.float32
            )
            mixed[b * BLOCK : (b + 1) * BLOCK, g * HEAD_DIM : (g + 1) * HEAD_DIM] = (
                weighted / total
            ).astype(jnp.bfloat16)

    left = lax.broadcasted_iota(jnp.int32, (BLOCK, BLOCK), 0)
    source = ((left // 2) % blocks) * part + (left // (2 * blocks)) * 2 + left % 2
    backward = jnp.where(taken == source, 1.0, 0.0).astype(jnp.bfloat16)
    for h in range(blocks):
        chunk = jnp.concatenate(
            [mixed[s * BLOCK + h * part : s * BLOCK + (h + 1) * part] for s in range(blocks)], axis=0
        )
        out_ref[h * BLOCK : (h + 1) * BLOCK] = jnp.dot(
            backward, chunk, preferred_element_type=jnp.float32
        ).astype(jnp.bfloat16)


def attend(member, lengths, lanes, cosine, sine):
    count = cosine.shape[0]
    whole = pl.BlockSpec(memory_space=pltpu.VMEM)
    scalars = pl.BlockSpec(memory_space=pltpu.SMEM)
    return pl.pallas_call(
        attention_kernel,
        out_shape=jax.ShapeDtypeStruct((count, GROUP * HEAD_DIM), jnp.bfloat16),
        in_specs=[scalars, scalars] + [whole] * 6,
        out_specs=whole,
        scratch_shapes=[
            pltpu.VMEM((GROUP, count, HEAD_DIM), jnp.bfloat16),
            pltpu.VMEM((count, HEAD_DIM), jnp.bfloat16),
            pltpu.VMEM((count, HEAD_DIM), jnp.bfloat16),
            pltpu.VMEM((count, GROUP * HEAD_DIM), jnp.bfloat16),
        ],
        compiler_params=pltpu.CompilerParams(vmem_limit_bytes=24 * 2**20),
        name="attend",
    )(member, lengths, *lanes, cosine, sine)


def on_device(tokens, projection, placement, doc_lengths):
    row_count, width = tokens.shape
    devices = placement.shape[1]
    members = lax.axis_size(CTX)
    groups = devices // members
    piece = row_count // devices
    member = lax.axis_index(CTX)

    places, pieces = gather_weights(projection, member)
    target = (placement[0][:, None] * piece + jnp.arange(piece, dtype=jnp.int32)[None, :]).reshape(row_count)
    outgoing = sort_rows(tokens, target, groups)
    arrived = lax.all_to_all(outgoing, DP, 0, 0, tiled=True).reshape(row_count, width)
    across = [(0, 1), (1, 0)]
    far = lax.ppermute(arrived, "zl", across)
    near = lax.ppermute(arrived, "core", across)
    lanes = [project(places, pieces, arrived), project(places, pieces, near)]
    tables = rotary_tables(doc_lengths[0], members * row_count)
    far, lanes, tables = lax.optimization_barrier((far, lanes, tables))
    last = lax.ppermute(far, "core", across)
    lanes = lanes + [project(places, pieces, far), project(places, pieces, last)]
    mixed = attend(member.reshape(1), doc_lengths, lanes, *tables)
    returned = lax.all_to_all(
        mixed.reshape(devices, members * piece, GROUP * HEAD_DIM), EVERY, 0, 0, tiled=True
    )
    return unsort_rows(returned.reshape(groups, members, members * piece, GROUP * HEAD_DIM), target)


def solution(mesh):
    sizes = {"x": 4, "y": 4, "zh": 2, "zl": 2, "core": 2}
    fine = Mesh(mesh.devices.reshape(tuple(sizes.values())), tuple(sizes))
    return jax.shard_map(
        on_device,
        mesh=fine,
        in_specs=(P(EVERY, None), P(DP, None), P(EVERY, None), P(DP, None)),
        out_specs=P(EVERY, None),
        check_vma=False,
    )
```

```python
import functools

import jax
import jax.numpy as jnp
from jax import lax
from jax.experimental import pallas as pl
from jax.experimental.pallas import tpu as pltpu
from jax.sharding import Mesh, PartitionSpec as P

HEAD_DIM = 128
HEADS = 16
KV_HEADS = 4
GROUP = HEADS // KV_HEADS
THETA = 500000.0
MOST = 512
DP = ("x", "y", "zh")
CTX = ("zl", "core")
EVERY = DP + CTX
BLOCK = 256


def frequencies():
    half = HEAD_DIM // 2
    return THETA ** (-2.0 * jnp.arange(half, dtype=jnp.float32) / HEAD_DIM)


def rotary_tables(lengths, count):
    position = jnp.arange(count, dtype=jnp.int32)
    ends = jnp.cumsum(lengths)
    begins = jnp.sum(jnp.where(position[:, None] >= ends[None, :], lengths[None, :], 0), axis=1)
    angles = (position - begins).astype(jnp.float32)[:, None] * frequencies()[None, :]
    cosine, sine = jnp.cos(angles), jnp.sin(angles)
    return jnp.concatenate([cosine, cosine], axis=1), jnp.concatenate([-sine, sine], axis=1)


def sort_kernel(placement_ref, rows_ref, out_ref):
    count = rows_ref.shape[0]
    devices = placement_ref.shape[1]
    piece = count // devices
    device = lax.broadcasted_iota(jnp.int32, (devices, devices), 0)
    pieces = jnp.where(device == placement_ref[...], 1.0, 0.0).astype(jnp.bfloat16)
    down = lax.broadcasted_iota(jnp.int32, (count, devices), 0) // piece
    tall = jnp.where(down == lax.broadcasted_iota(jnp.int32, (count, devices), 1), 1.0, 0.0).astype(jnp.bfloat16)
    along = lax.broadcasted_iota(jnp.int32, (devices, count), 1) // piece
    wide = jnp.where(along == lax.broadcasted_iota(jnp.int32, (devices, count), 0), 1.0, 0.0).astype(jnp.bfloat16)
    rows = jnp.dot(tall, pieces, preferred_element_type=jnp.float32).astype(jnp.bfloat16)
    both = jnp.dot(rows, wide, preferred_element_type=jnp.float32)
    same = lax.broadcasted_iota(jnp.int32, (count, count), 0) % piece == lax.broadcasted_iota(jnp.int32, (count, count), 1) % piece
    one_hot = jnp.where(same, both, 0.0).astype(jnp.bfloat16)
    moved = jnp.dot(one_hot, rows_ref[...], preferred_element_type=jnp.float32).astype(jnp.bfloat16)
    out_ref[...] = moved.reshape(out_ref.shape)


def sort_rows(tokens, placement, groups):
    count, width = tokens.shape
    rows = count // groups
    tile = 1024
    return pl.pallas_call(
        sort_kernel,
        out_shape=jax.ShapeDtypeStruct((groups, rows, width), tokens.dtype),
        grid=(width // tile,),
        in_specs=[
            pl.BlockSpec(placement.shape, lambda i: (0, 0)),
            pl.BlockSpec((count, tile), lambda i: (0, i)),
        ],
        out_specs=pl.BlockSpec((groups, rows, tile), lambda i: (0, 0, i)),
        compiler_params=pltpu.CompilerParams(vmem_limit_bytes=60 * 2**20),
        name="sort_rows",
    )(placement, tokens)


def unsort_kernel(target_ref, rows_ref, out_ref):
    count = out_ref.shape[0]
    order = lax.broadcasted_iota(jnp.int32, (count, count), 1)
    one_hot = jnp.where(order == target_ref[...], 1.0, 0.0).astype(jnp.bfloat16)
    rows = rows_ref[...].reshape(count, out_ref.shape[1])
    out_ref[...] = jnp.dot(one_hot, rows, preferred_element_type=jnp.float32).astype(jnp.bfloat16)


def unsort_rows(returned, target):
    groups, blocks, rows, width = returned.shape
    count = groups * rows
    return pl.pallas_call(
        unsort_kernel,
        out_shape=jax.ShapeDtypeStruct((count, blocks * width), returned.dtype),
        grid=(blocks,),
        in_specs=[
            pl.BlockSpec((count, 1), lambda i: (0, 0)),
            pl.BlockSpec((groups, None, rows, width), lambda i: (0, i, 0, 0)),
        ],
        out_specs=pl.BlockSpec((count, width), lambda i: (0, i)),
        compiler_params=pltpu.CompilerParams(vmem_limit_bytes=32 * 2**20),
        name="unsort_rows",
    )(target.reshape(count, 1), returned)


def own_columns(projection, member):
    query_width, key_width = HEADS * HEAD_DIM, KV_HEADS * HEAD_DIM
    return jnp.concatenate(
        [
            lax.dynamic_slice_in_dim(projection, member * GROUP * HEAD_DIM, GROUP * HEAD_DIM, 1),
            lax.dynamic_slice_in_dim(projection, query_width + member * HEAD_DIM, HEAD_DIM, 1),
            lax.dynamic_slice_in_dim(projection, query_width + key_width + member * HEAD_DIM, HEAD_DIM, 1),
        ],
        axis=1,
    )


UP, DOWN, OVER = (tuple((i, (i + d) % 4) for i in range(4)) for d in (1, 3, 2))


def ring_blocks(block, axis):
    others = [lax.ppermute(block, axis, way) for way in (UP, DOWN, OVER)]
    return jnp.concatenate([block] + others, axis=0)


def both_ways(block, axis):
    return [block, lax.ppermute(block, axis, UP), lax.ppermute(block, axis, DOWN)]


def far_halves(blocks, axis):
    half = blocks[0].shape[0] // 2
    return [lax.ppermute(blocks[1][:half], axis, UP), lax.ppermute(blocks[2][half:], axis, DOWN)]


RING = (0, 3, 1, 2)
SPAN = ((0, (0, 1, 2, 3)), (3, (0, 1, 2, 3)), (1, (0, 1, 2, 3)), (2, (0, 1)), (2, (2, 3)))


def weight_places(rows):
    x, y, zh = lax.axis_index("x"), lax.axis_index("y"), lax.axis_index("zh")
    places = [(i * 2 + zh) * rows for i in range(16)]
    for side in range(2):
        for outer, inners in SPAN:
            for inner in inners:
                near, far = (outer, RING[inner]) if side == 0 else (RING[inner], outer)
                places.append(((x + near) % 4 * 8 + (y + far) % 4 * 2 + 1 - zh) * rows)
    return jnp.stack(places)


def project_kernel(parts, places_ref, *refs):
    row_refs, refs = refs[:parts], refs[parts:]
    pieces, out_refs, ordered = refs[: -parts - 1], refs[-parts - 1 : -1], refs[-1]
    half = out_refs[0].shape[1] // 2
    step = 128

    def take(first, count):
        for i in range(count):
            column = pl.multiple_of(places_ref[first + i], step)
            at = 0
            for rows in row_refs:
                ordered[at : at + rows.shape[0], i * step : (i + 1) * step] = rows[:, pl.ds(column, step)]
                at += rows.shape[0]

    def product(pieces):
        total, at = None, 0
        for piece in pieces:
            depth = piece.shape[0]
            term = jnp.dot(ordered[:, at : at + depth], piece[...], preferred_element_type=jnp.float32)
            total = term if total is None else total + term
            at += depth
        return total

    take(0, 16)
    out = product(pieces[:1])
    for side in range(2):
        take(16 + side * 16, 16)
        columns = slice(side * half, (side + 1) * half)
        here = (out[:, columns] + product(pieces[1 + side * 5 : 6 + side * 5])).astype(jnp.bfloat16)
        at = 0
        for out_ref in out_refs:
            out_ref[:, columns] = here[at : at + out_ref.shape[0]]
            at += out_ref.shape[0]


def project(places, pieces, rows):
    count, depth = sum(r.shape[0] for r in rows), rows[0].shape[1]
    width = pieces[0].shape[1]
    whole = pl.BlockSpec(memory_space=pltpu.VMEM)
    return pl.pallas_call(
        functools.partial(project_kernel, len(rows)),
        out_shape=[jax.ShapeDtypeStruct((r.shape[0], width), jnp.bfloat16) for r in rows],
        in_specs=[pl.BlockSpec(memory_space=pltpu.SMEM)] + [whole] * (len(rows) + len(pieces)),
        out_specs=[whole] * len(rows),
        scratch_shapes=[pltpu.VMEM((count, depth // 2), jnp.bfloat16)],
        compiler_params=pltpu.CompilerParams(vmem_limit_bytes=24 * 2**20),
        cost_estimate=pl.CostEstimate(flops=1, bytes_accessed=1, transcendentals=0),
        name="project",
    )(places, *rows, *pieces)


def attention_kernel(late, member_ref, lengths_ref, *refs):
    lanes, (cos_ref, sin_ref) = refs[:4], refs[4:6]
    if late:
        early_keys, early_values, early_mixed, out_ref, queries, keys, values, mixed = refs[6:]
    else:
        keys, values, mixed, queries = refs[6:]
    blocks = 2
    part = BLOCK // 4
    span = BLOCK // blocks
    half = HEAD_DIM // 2
    member = member_ref[0]

    taken = lax.broadcasted_iota(jnp.int32, (BLOCK, BLOCK), 1)
    lane, rest = taken // part, taken % part
    group, block, row = rest // (2 * blocks), (rest // 2) % blocks, rest % 2
    placed = block * span + (group * 4 + (lane ^ member)) * 2 + row
    wanted = lax.broadcasted_iota(jnp.int32, (BLOCK, BLOCK), 0)
    forward = jnp.where(wanted == placed, 1.0, 0.0).astype(jnp.bfloat16)
    first_row = blocks * BLOCK if late else 0
    for h in range(2):
        chunk = jnp.concatenate([lane_ref[h * part : (h + 1) * part] for lane_ref in lanes], axis=0)
        chunk = jnp.dot(forward, chunk, preferred_element_type=jnp.float32)
        for s in range(blocks):
            at = s * BLOCK + h * span
            rows = slice(at, at + span)
            here = chunk[s * span : (s + 1) * span]
            cosine, sine = cos_ref[first_row + at : first_row + at + span], sin_ref[first_row + at : first_row + at + span]

            def rotate(x):
                return (x * cosine + pltpu.roll(x, half, 1) * sine).astype(jnp.bfloat16)

            for g in range(GROUP):
                queries[g, rows] = rotate(here[:, g * HEAD_DIM : (g + 1) * HEAD_DIM])
            keys[rows] = rotate(here[:, GROUP * HEAD_DIM : (GROUP + 1) * HEAD_DIM])
            values[rows] = here[:, (GROUP + 1) * HEAD_DIM :].astype(jnp.bfloat16)

    def reached(early, own, first, stop):
        base = blocks if late else 0
        parts = []
        if first < base:
            parts.append(early[first * BLOCK : base * BLOCK])
        parts.append(own[max(first - base, 0) * BLOCK : (stop - base) * BLOCK])
        return parts[0] if len(parts) == 1 else jnp.concatenate(parts, axis=0)

    scale = HEAD_DIM ** (-0.5)
    reach = (MOST - 1 + BLOCK - 1) // BLOCK
    for local in range(blocks):
        b = local + (blocks if late else 0)
        first = max(0, b - reach)
        width = (b + 1 - first) * BLOCK
        position = b * BLOCK + lax.broadcasted_iota(jnp.int32, (BLOCK, 1), 0)
        begin, end = jnp.zeros_like(position), jnp.int32(0)
        for j in range(lengths_ref.shape[1]):
            end = end + lengths_ref[0, j]
            begin = jnp.where(position >= end, end, begin)
        key_at = first * BLOCK + lax.broadcasted_iota(jnp.int32, (BLOCK, width), 1)
        allowed = (key_at >= begin) & (key_at <= position)
        key_block = reached(early_keys if late else None, keys, first, b + 1)
        value_block = reached(early_values if late else None, values, first, b + 1)
        rows = slice(local * BLOCK, (local + 1) * BLOCK)
        for g in range(GROUP):
            scores = lax.dot_general(
                queries[g, rows], key_block, (((1,), (1,)), ((), ())), preferred_element_type=jnp.float32
            )
            scores = jnp.where(allowed, scores * scale, -1e30)
            weights = jnp.exp(scores - jnp.max(scores, axis=1, keepdims=True))
            total = jnp.sum(weights, axis=1, keepdims=True)
            weighted = jnp.dot(
                weights.astype(jnp.bfloat16), value_block, preferred_element_type=jnp.float32
            )
            mixed[rows, g * HEAD_DIM : (g + 1) * HEAD_DIM] = (weighted / total).astype(jnp.bfloat16)

    if not late:
        return
    slots = 2 * blocks
    left = lax.broadcasted_iota(jnp.int32, (BLOCK, BLOCK), 0)
    source = ((left // 2) % slots) * part + (left // (2 * slots)) * 2 + left % 2
    backward = jnp.where(taken == source, 1.0, 0.0).astype(jnp.bfloat16)
    for h in range(slots):
        chunk = jnp.concatenate(
            [
                held[s * BLOCK + h * part : s * BLOCK + (h + 1) * part]
                for held in (early_mixed, mixed)
                for s in range(blocks)
            ],
            axis=0,
        )
        out_ref[h * BLOCK : (h + 1) * BLOCK] = jnp.dot(
            backward, chunk, preferred_element_type=jnp.float32
        ).astype(jnp.bfloat16)


def attend(member, lengths, lanes, tables, early=None):
    count = 2 * BLOCK
    late = early is not None
    whole = pl.BlockSpec(memory_space=pltpu.VMEM)
    scalars = pl.BlockSpec(memory_space=pltpu.SMEM)
    queries = (GROUP, count, HEAD_DIM)
    held = [(count, HEAD_DIM), (count, HEAD_DIM), (count, GROUP * HEAD_DIM)]
    outs = [(2 * count, GROUP * HEAD_DIM)] if late else held
    scratch = [queries] + held if late else [queries]
    early = list(early) if late else []
    return pl.pallas_call(
        functools.partial(attention_kernel, late),
        out_shape=[jax.ShapeDtypeStruct(shape, jnp.bfloat16) for shape in outs],
        in_specs=[scalars, scalars] + [whole] * (6 + len(early)),
        out_specs=[whole] * len(outs),
        scratch_shapes=[pltpu.VMEM(shape, jnp.bfloat16) for shape in scratch],
        compiler_params=pltpu.CompilerParams(vmem_limit_bytes=24 * 2**20),
        cost_estimate=pl.CostEstimate(flops=1, bytes_accessed=1, transcendentals=0),
        name="attend",
    )(member, lengths, *lanes, *tables, *early)


def on_device(tokens, projection, placement, doc_lengths):
    row_count, width = tokens.shape
    devices = placement.shape[1]
    members = lax.axis_size(CTX)
    groups = devices // members
    piece = row_count // devices
    member = lax.axis_index(CTX)
    across = [(0, 1), (1, 0)]
    depth = projection.shape[0]
    tie = lax.optimization_barrier

    mine = lax.all_gather(own_columns(projection, member), ("x", "y"), axis=0, tiled=True)
    places = weight_places(depth)
    outgoing = sort_rows(tokens, placement, groups)
    arrived = lax.all_to_all(outgoing, DP, 0, 0, tiled=True)

    theirs = lax.ppermute(own_columns(projection, member ^ 2), ("zh", "zl"), [(0, 3), (3, 0), (1, 2), (2, 1)])
    half = theirs.shape[1] // 2
    first, second = ring_blocks(theirs[:, :half], "y"), ring_blocks(theirs[:, half:], "x")
    first, second = both_ways(first, "x"), both_ways(second, "y")
    tables = rotary_tables(doc_lengths[0], members * row_count)
    arrived, first, second, tables, places = tie((arrived, first, second, tables, places))

    rows = members * piece // 2
    early, late = (
        arrived[:, i * rows : (i + 1) * rows].reshape(groups * rows, width) for i in range(2)
    )
    far_early = lax.ppermute(early, "zl", across)
    first_far, second_far = far_halves(first, "x"), far_halves(second, "y")
    far_early, early, late, first_far, second_far = tie((far_early, early, late, first_far, second_far))

    far_late = lax.ppermute(late, "zl", across)
    near_early, near_late, last_early = (lax.ppermute(r, "core", across) for r in (early, late, far_early))
    pieces = [mine, *first, *first_far, *second, *second_far]
    own = project(places, pieces, [early, near_early, late, near_late])
    others = project(places, pieces, [far_early, last_early])
    held = attend(member.reshape(1), doc_lengths, [own[0], own[1], *others], tables)
    far_late, held = tie((far_late, held))
    last_late = lax.ppermute(far_late, "core", across)
    others = project(places, pieces, [far_late, last_late])
    mixed = attend(member.reshape(1), doc_lengths, [own[2], own[3], *others], tables, held)[0]

    returned = lax.all_to_all(
        mixed.reshape(devices, members * piece, GROUP * HEAD_DIM), EVERY, 0, 0, tiled=True
    )
    target = (placement[0][:, None] * piece + jnp.arange(piece, dtype=jnp.int32)[None, :]).reshape(row_count)
    return unsort_rows(returned.reshape(groups, members, members * piece, GROUP * HEAD_DIM), target)


def solution(mesh):
    sizes = {"x": 4, "y": 4, "zh": 2, "zl": 2, "core": 2}
    fine = Mesh(mesh.devices.reshape(tuple(sizes.values())), tuple(sizes))
    return jax.shard_map(
        on_device,
        mesh=fine,
        in_specs=(P(EVERY, None), P(DP, None), P(EVERY, None), P(DP, None)),
        out_specs=P(EVERY, None),
        check_vma=False,
    )
```

```python
import functools

import jax
import jax.numpy as jnp
from jax import lax
from jax.experimental import pallas as pl
from jax.experimental.pallas import tpu as pltpu
from jax.sharding import Mesh, PartitionSpec as P

HEAD_DIM = 128
HEADS = 16
KV_HEADS = 4
GROUP = HEADS // KV_HEADS
THETA = 500000.0
MOST = 512
DP = ("x", "y", "zh")
CTX = ("zl", "core")
EVERY = DP + CTX
BLOCK = 256


def frequencies():
    half = HEAD_DIM // 2
    return THETA ** (-2.0 * jnp.arange(half, dtype=jnp.float32) / HEAD_DIM)


def rotary_tables(lengths, count):
    position = jnp.arange(count, dtype=jnp.int32)
    ends = jnp.cumsum(lengths)
    begins = jnp.sum(jnp.where(position[:, None] >= ends[None, :], lengths[None, :], 0), axis=1)
    angles = (position - begins).astype(jnp.float32)[:, None] * frequencies()[None, :]
    cosine, sine = jnp.cos(angles), jnp.sin(angles)
    return jnp.concatenate([cosine, cosine], axis=1), jnp.concatenate([-sine, sine], axis=1)


def sort_kernel(placement_ref, rows_ref, out_ref, one_hot):
    count = rows_ref.shape[0]
    devices = placement_ref.shape[1]
    piece = count // devices

    @pl.when(pl.program_id(0) == 0)
    def _():
        device = lax.broadcasted_iota(jnp.int32, (devices, devices), 0)
        pieces = jnp.where(device == placement_ref[...], 1.0, 0.0).astype(jnp.bfloat16)
        down = lax.broadcasted_iota(jnp.int32, (count, devices), 0) // piece
        tall = jnp.where(down == lax.broadcasted_iota(jnp.int32, (count, devices), 1), 1.0, 0.0).astype(jnp.bfloat16)
        along = lax.broadcasted_iota(jnp.int32, (devices, count), 1) // piece
        wide = jnp.where(along == lax.broadcasted_iota(jnp.int32, (devices, count), 0), 1.0, 0.0).astype(jnp.bfloat16)
        rows = jnp.dot(tall, pieces, preferred_element_type=jnp.float32).astype(jnp.bfloat16)
        both = jnp.dot(rows, wide, preferred_element_type=jnp.float32)
        row = lax.broadcasted_iota(jnp.int32, (count, count), 0) % piece
        same = row == lax.broadcasted_iota(jnp.int32, (count, count), 1) % piece
        one_hot[...] = jnp.where(same, both, 0.0).astype(jnp.bfloat16)

    moved = jnp.dot(one_hot[...], rows_ref[...], preferred_element_type=jnp.float32).astype(jnp.bfloat16)
    out_ref[...] = moved.reshape(out_ref.shape)


def sort_rows(tokens, placement, groups):
    count, width = tokens.shape
    rows = count // groups
    tile = 512
    return pl.pallas_call(
        sort_kernel,
        out_shape=jax.ShapeDtypeStruct((groups, rows, width), tokens.dtype),
        grid=(width // tile,),
        in_specs=[
            pl.BlockSpec(placement.shape, lambda i: (0, 0)),
            pl.BlockSpec((count, tile), lambda i: (0, i)),
        ],
        out_specs=pl.BlockSpec((groups, rows, tile), lambda i: (0, 0, i)),
        scratch_shapes=[pltpu.VMEM((count, count), jnp.bfloat16)],
        compiler_params=pltpu.CompilerParams(vmem_limit_bytes=60 * 2**20),
        name="sort_rows",
    )(placement, tokens)


def unsort_kernel(target_ref, rows_ref, out_ref):
    count = out_ref.shape[0]
    order = lax.broadcasted_iota(jnp.int32, (count, count), 1)
    one_hot = jnp.where(order == target_ref[...], 1.0, 0.0).astype(jnp.bfloat16)
    rows = rows_ref[...].reshape(count, out_ref.shape[1])
    out_ref[...] = jnp.dot(one_hot, rows, preferred_element_type=jnp.float32).astype(jnp.bfloat16)


def unsort_rows(returned, target):
    groups, blocks, rows, width = returned.shape
    count = groups * rows
    return pl.pallas_call(
        unsort_kernel,
        out_shape=jax.ShapeDtypeStruct((count, blocks * width), returned.dtype),
        grid=(blocks,),
        in_specs=[
            pl.BlockSpec((count, 1), lambda i: (0, 0)),
            pl.BlockSpec((groups, None, rows, width), lambda i: (0, i, 0, 0)),
        ],
        out_specs=pl.BlockSpec((count, width), lambda i: (0, i)),
        compiler_params=pltpu.CompilerParams(vmem_limit_bytes=32 * 2**20),
        name="unsort_rows",
    )(target.reshape(count, 1), returned)


def columns_kernel(members_ref, projection_ref, *refs):
    outs, sems = refs[:-1], refs[-1]
    copies = []
    for i, out in enumerate(outs):
        member, at, source = members_ref[i], 0, 0
        for heads, width in ((KV_HEADS, GROUP * HEAD_DIM), (KV_HEADS, HEAD_DIM), (KV_HEADS, HEAD_DIM)):
            copy = pltpu.make_async_copy(
                projection_ref.at[:, pl.ds(pl.multiple_of(source + member * width, HEAD_DIM), width)],
                out.at[:, pl.ds(at, width)],
                sems.at[len(copies)],
            )
            copy.start()
            copies.append(copy)
            at, source = at + width, source + heads * width
    for copy in copies:
        copy.wait()


def columns_of(projection, members):
    anywhere = pl.BlockSpec(memory_space=pl.ANY)
    shape = jax.ShapeDtypeStruct((projection.shape[0], (GROUP + 2) * HEAD_DIM), projection.dtype)
    return pl.pallas_call(
        columns_kernel,
        out_shape=[shape] * len(members),
        in_specs=[pl.BlockSpec(memory_space=pltpu.SMEM), anywhere],
        out_specs=[anywhere] * len(members),
        scratch_shapes=[pltpu.SemaphoreType.DMA((3 * len(members),))],
        name="columns",
    )(jnp.stack(members), projection)


UP, DOWN, OVER = (tuple((i, (i + d) % 4) for i in range(4)) for d in (1, 3, 2))


def ring_blocks(block, axis):
    others = [lax.ppermute(block, axis, way) for way in (UP, DOWN, OVER)]
    return jnp.concatenate([block] + others, axis=0)


def both_ways(block, axis):
    return [block, lax.ppermute(block, axis, UP), lax.ppermute(block, axis, DOWN)]


def far_halves(blocks, axis):
    half = blocks[0].shape[0] // 2
    return [lax.ppermute(blocks[1][:half], axis, UP), lax.ppermute(blocks[2][half:], axis, DOWN)]


RING = (0, 3, 1, 2)
SPAN = ((0, (0, 1, 2, 3)), (3, (0, 1, 2, 3)), (1, (0, 1, 2, 3)), (2, (0, 1)), (2, (2, 3)))


def weight_places(rows):
    x, y, zh = lax.axis_index("x"), lax.axis_index("y"), lax.axis_index("zh")
    places = [(i * 2 + zh) * rows for i in range(16)]
    for side in range(2):
        for outer, inners in SPAN:
            for inner in inners:
                near, far = (outer, RING[inner]) if side == 0 else (RING[inner], outer)
                places.append(((x + near) % 4 * 8 + (y + far) % 4 * 2 + 1 - zh) * rows)
    return jnp.stack(places)


def project_kernel(parts, places_ref, *refs):
    row_refs, refs = refs[:parts], refs[parts:]
    pieces, out_refs, ordered = refs[: -parts - 1], refs[-parts - 1 : -1], refs[-1]
    half = out_refs[0].shape[1] // 2
    step = 128

    def take(first, count):
        for i in range(count):
            column = pl.multiple_of(places_ref[first + i], step)
            at = 0
            for rows in row_refs:
                ordered[at : at + rows.shape[0], i * step : (i + 1) * step] = rows[:, pl.ds(column, step)]
                at += rows.shape[0]

    def product(pieces):
        total, at = None, 0
        for piece in pieces:
            depth = piece.shape[0]
            term = jnp.dot(ordered[:, at : at + depth], piece[...], preferred_element_type=jnp.float32)
            total = term if total is None else total + term
            at += depth
        return total

    take(0, 16)
    out = product(pieces[:1])
    for side in range(2):
        take(16 + side * 16, 16)
        columns = slice(side * half, (side + 1) * half)
        here = (out[:, columns] + product(pieces[1 + side * 5 : 6 + side * 5])).astype(jnp.bfloat16)
        at = 0
        for out_ref in out_refs:
            out_ref[:, columns] = here[at : at + out_ref.shape[0]]
            at += out_ref.shape[0]


def project(places, pieces, rows):
    count, depth = sum(r.shape[0] for r in rows), rows[0].shape[1]
    width = pieces[0].shape[1]
    whole = pl.BlockSpec(memory_space=pltpu.VMEM)
    return pl.pallas_call(
        functools.partial(project_kernel, len(rows)),
        out_shape=[jax.ShapeDtypeStruct((r.shape[0], width), jnp.bfloat16) for r in rows],
        in_specs=[pl.BlockSpec(memory_space=pltpu.SMEM)] + [whole] * (len(rows) + len(pieces)),
        out_specs=[whole] * len(rows),
        scratch_shapes=[pltpu.VMEM((count, depth // 2), jnp.bfloat16)],
        compiler_params=pltpu.CompilerParams(vmem_limit_bytes=16 * 2**20),
        cost_estimate=pl.CostEstimate(
            flops=2 * count * depth * width, bytes_accessed=2 * depth * (width + count), transcendentals=0
        ),
        name="project",
    )(places, *rows, *pieces)


def attention_kernel(member_ref, lengths_ref, *refs):
    own_ref, near_ref, far_refs, last_refs = refs[0], refs[1], refs[2:6], refs[6:10]
    cos_ref, sin_ref, out_ref, queries, keys, values, mixed = refs[10:]
    count = cos_ref.shape[0]
    blocks = count // BLOCK
    part = BLOCK // blocks
    half = HEAD_DIM // 2
    member = member_ref[0]

    taken = lax.broadcasted_iota(jnp.int32, (BLOCK, BLOCK), 1)
    lane, rest = taken // part, taken % part
    group, slot, row = rest // (2 * blocks), (rest // 2) % blocks, rest % 2
    placed = slot * part + (group * 4 + (lane ^ member)) * 2 + row
    wanted = lax.broadcasted_iota(jnp.int32, (BLOCK, BLOCK), 0)
    forward = jnp.where(wanted == placed, 1.0, 0.0).astype(jnp.bfloat16)
    for h in range(blocks):
        span = slice(h * part, (h + 1) * part)
        chunk = jnp.concatenate([own_ref[span], near_ref[span], far_refs[h][...], last_refs[h][...]], axis=0)
        chunk = jnp.dot(forward, chunk, preferred_element_type=jnp.float32)
        for s in range(blocks):
            rows = slice(s * BLOCK + h * part, s * BLOCK + (h + 1) * part)
            here = chunk[s * part : (s + 1) * part]
            cosine, sine = cos_ref[rows], sin_ref[rows]

            def rotate(x):
                return (x * cosine + pltpu.roll(x, half, 1) * sine).astype(jnp.bfloat16)

            for g in range(GROUP):
                queries[g, rows] = rotate(here[:, g * HEAD_DIM : (g + 1) * HEAD_DIM])
            keys[rows] = rotate(here[:, GROUP * HEAD_DIM : (GROUP + 1) * HEAD_DIM])
            values[rows] = here[:, (GROUP + 1) * HEAD_DIM :].astype(jnp.bfloat16)

    scale = HEAD_DIM ** (-0.5)
    reach = (MOST - 1 + BLOCK - 1) // BLOCK
    for b in range(blocks):
        first = max(0, b - reach)
        width = (b + 1 - first) * BLOCK
        position = b * BLOCK + lax.broadcasted_iota(jnp.int32, (BLOCK, 1), 0)
        begin, end = jnp.zeros_like(position), jnp.int32(0)
        for j in range(lengths_ref.shape[1]):
            end = end + lengths_ref[0, j]
            begin = jnp.where(position >= end, end, begin)
        key_at = first * BLOCK + lax.broadcasted_iota(jnp.int32, (BLOCK, width), 1)
        allowed = (key_at >= begin) & (key_at <= position)
        key_block = keys[first * BLOCK : (b + 1) * BLOCK]
        value_block = values[first * BLOCK : (b + 1) * BLOCK]
        for g in range(GROUP):
            scores = lax.dot_general(
                queries[g, b * BLOCK : (b + 1) * BLOCK],
                key_block,
                (((1,), (1,)), ((), ())),
                preferred_element_type=jnp.float32,
            )
            scores = jnp.where(allowed, scores * scale, -1e30)
            weights = jnp.exp(scores - jnp.max(scores, axis=1, keepdims=True))
            total = jnp.sum(weights, axis=1, keepdims=True)
            weighted = jnp.dot(
                weights.astype(jnp.bfloat16), value_block, preferred_element_type=jnp.float32
            )
            mixed[b * BLOCK : (b + 1) * BLOCK, g * HEAD_DIM : (g + 1) * HEAD_DIM] = (
                weighted / total
            ).astype(jnp.bfloat16)

    left = lax.broadcasted_iota(jnp.int32, (BLOCK, BLOCK), 0)
    source = ((left // 2) % blocks) * part + (left // (2 * blocks)) * 2 + left % 2
    backward = jnp.where(taken == source, 1.0, 0.0).astype(jnp.bfloat16)
    for h in range(blocks):
        chunk = jnp.concatenate(
            [mixed[s * BLOCK + h * part : s * BLOCK + (h + 1) * part] for s in range(blocks)], axis=0
        )
        out_ref[h * BLOCK : (h + 1) * BLOCK] = jnp.dot(
            backward, chunk, preferred_element_type=jnp.float32
        ).astype(jnp.bfloat16)


def attend(member, lengths, lanes, cosine, sine):
    count = cosine.shape[0]
    whole = pl.BlockSpec(memory_space=pltpu.VMEM)
    scalars = pl.BlockSpec(memory_space=pltpu.SMEM)
    return pl.pallas_call(
        attention_kernel,
        out_shape=jax.ShapeDtypeStruct((count, GROUP * HEAD_DIM), jnp.bfloat16),
        in_specs=[scalars, scalars] + [whole] * (2 + len(lanes)),
        out_specs=whole,
        scratch_shapes=[
            pltpu.VMEM((GROUP, count, HEAD_DIM), jnp.bfloat16),
            pltpu.VMEM((count, HEAD_DIM), jnp.bfloat16),
            pltpu.VMEM((count, HEAD_DIM), jnp.bfloat16),
            pltpu.VMEM((count, GROUP * HEAD_DIM), jnp.bfloat16),
        ],
        compiler_params=pltpu.CompilerParams(vmem_limit_bytes=16 * 2**20),
        name="attend",
    )(member, lengths, *lanes, cosine, sine)


def on_device(tokens, projection, placement, doc_lengths):
    row_count, width = tokens.shape
    devices = placement.shape[1]
    members = lax.axis_size(CTX)
    groups = devices // members
    piece = row_count // devices
    member = lax.axis_index(CTX)
    across = [(0, 1), (1, 0)]
    depth = projection.shape[0]
    tie = lax.optimization_barrier

    mine, theirs = columns_of(projection, [member, member ^ 2])
    mine = lax.all_gather(mine, ("x", "y"), axis=0, tiled=True)
    places = weight_places(depth)
    outgoing = sort_rows(tokens, placement, groups)
    arrived = lax.all_to_all(outgoing, DP, 0, 0, tiled=True).reshape(row_count, width)

    theirs = lax.ppermute(theirs, ("zh", "zl"), [(0, 3), (3, 0), (1, 2), (2, 1)])
    tables = rotary_tables(doc_lengths[0], members * row_count)
    arrived, theirs, tables, places = tie((arrived, theirs, tables, places))

    size = row_count // 4
    near, far = [arrived], []

    def exchange(step, *others):
        near[0], sent, *others = tie((near[0], lax.ppermute(near[0][step * size : (step + 1) * size], "zl", across), *others))
        far.append(sent)
        return others

    half = theirs.shape[1] // 2
    first, second = exchange(0, ring_blocks(theirs[:, :half], "y"), ring_blocks(theirs[:, half:], "x"))
    first, second = exchange(1, both_ways(first, "x"), both_ways(second, "y"))
    first_far, second_far = exchange(2, far_halves(first, "x"), far_halves(second, "y"))
    pieces = [mine, *first, *first_far, *second, *second_far]
    own = near[0]
    last_sent = lax.ppermute(own[3 * size :], "zl", across)
    swapped = [lax.ppermute(rows, "core", across) for rows in (own, *far)]
    done = project(places, pieces, [own, *far, *swapped])
    last_sent, done = tie((last_sent, done))
    last = project(places, pieces, [last_sent, lax.ppermute(last_sent, "core", across)])
    lanes = [done[0], done[4], *done[1:4], last[0], *done[5:8], last[1]]
    mixed = attend(member.reshape(1), doc_lengths, lanes, *tables)

    returned = lax.all_to_all(
        mixed.reshape(devices, members * piece, GROUP * HEAD_DIM), EVERY, 0, 0, tiled=True
    )
    target = (placement[0][:, None] * piece + jnp.arange(piece, dtype=jnp.int32)[None, :]).reshape(row_count)
    return unsort_rows(returned.reshape(groups, members, members * piece, GROUP * HEAD_DIM), target)


def solution(mesh):
    sizes = {"x": 4, "y": 4, "zh": 2, "zl": 2, "core": 2}
    fine = Mesh(mesh.devices.reshape(tuple(sizes.values())), tuple(sizes))
    return jax.shard_map(
        on_device,
        mesh=fine,
        in_specs=(P(EVERY, None), P(DP, None), P(EVERY, None), P(DP, None)),
        out_specs=P(EVERY, None),
        check_vma=False,
    )
```

```python
import functools

import jax
import jax.numpy as jnp
from jax import lax
from jax.experimental import pallas as pl
from jax.experimental.pallas import tpu as pltpu
from jax.sharding import Mesh, PartitionSpec as P

HEAD_DIM = 128
HEADS = 16
KV_HEADS = 4
GROUP = HEADS // KV_HEADS
THETA = 500000.0
MOST = 512
DP = ("x", "y", "zh")
CTX = ("zl", "core")
EVERY = DP + CTX
BLOCK = 256


def frequencies():
    half = HEAD_DIM // 2
    return THETA ** (-2.0 * jnp.arange(half, dtype=jnp.float32) / HEAD_DIM)


def rotary_tables(lengths, count):
    position = jnp.arange(count, dtype=jnp.int32)
    ends = jnp.cumsum(lengths)
    begins = jnp.sum(jnp.where(position[:, None] >= ends[None, :], lengths[None, :], 0), axis=1)
    angles = (position - begins).astype(jnp.float32)[:, None] * frequencies()[None, :]
    return jnp.cos(angles), jnp.sin(angles)


def sort_kernel(target_ref, rows_ref, out_ref):
    count = rows_ref.shape[0]
    order = lax.broadcasted_iota(jnp.int32, (count, count), 0)
    one_hot = jnp.where(order == target_ref[...], 1.0, 0.0).astype(jnp.bfloat16)
    moved = jnp.dot(one_hot, rows_ref[...], preferred_element_type=jnp.float32).astype(jnp.bfloat16)
    out_ref[...] = moved.reshape(out_ref.shape)


def sort_rows(tokens, target, groups):
    count, width = tokens.shape
    rows = count // groups
    tile = 1024
    return pl.pallas_call(
        sort_kernel,
        out_shape=jax.ShapeDtypeStruct((groups, rows, width), tokens.dtype),
        grid=(width // tile,),
        in_specs=[
            pl.BlockSpec((1, count), lambda i: (0, 0)),
            pl.BlockSpec((count, tile), lambda i: (0, i)),
        ],
        out_specs=pl.BlockSpec((groups, rows, tile), lambda i: (0, 0, i)),
        compiler_params=pltpu.CompilerParams(vmem_limit_bytes=32 * 2**20),
        name="sort_rows",
    )(target.reshape(1, count), tokens)


def unsort_kernel(target_ref, rows_ref, out_ref):
    count = out_ref.shape[0]
    order = lax.broadcasted_iota(jnp.int32, (count, count), 1)
    one_hot = jnp.where(order == target_ref[...], 1.0, 0.0).astype(jnp.bfloat16)
    rows = rows_ref[...].reshape(count, out_ref.shape[1])
    out_ref[...] = jnp.dot(one_hot, rows, preferred_element_type=jnp.float32).astype(jnp.bfloat16)


def unsort_rows(returned, target):
    groups, blocks, rows, width = returned.shape
    count = groups * rows
    return pl.pallas_call(
        unsort_kernel,
        out_shape=jax.ShapeDtypeStruct((count, blocks * width), returned.dtype),
        grid=(blocks,),
        in_specs=[
            pl.BlockSpec((count, 1), lambda i: (0, 0)),
            pl.BlockSpec((groups, None, rows, width), lambda i: (0, i, 0, 0)),
        ],
        out_specs=pl.BlockSpec((count, width), lambda i: (0, i)),
        compiler_params=pltpu.CompilerParams(vmem_limit_bytes=32 * 2**20),
        name="unsort_rows",
    )(target.reshape(count, 1), returned)


def own_columns(projection, member):
    query_width, key_width = HEADS * HEAD_DIM, KV_HEADS * HEAD_DIM
    return jnp.concatenate(
        [
            lax.dynamic_slice_in_dim(projection, member * GROUP * HEAD_DIM, GROUP * HEAD_DIM, 1),
            lax.dynamic_slice_in_dim(projection, query_width + member * HEAD_DIM, HEAD_DIM, 1),
            lax.dynamic_slice_in_dim(projection, query_width + key_width + member * HEAD_DIM, HEAD_DIM, 1),
        ],
        axis=1,
    )


def ring_blocks(block, axis):
    ways = [[(i, (i + d) % 4) for i in range(4)] for d in (1, 3, 2)]
    return jnp.concatenate([block] + [lax.ppermute(block, axis, way) for way in ways], axis=0)


def spread(block, axis):
    up, down = [(i, (i + 1) % 4) for i in range(4)], [(i, (i + 3) % 4) for i in range(4)]
    half = block.shape[0] // 2
    below, above = lax.ppermute(block, axis, up), lax.ppermute(block, axis, down)
    far_low = lax.ppermute(below[:half], axis, up)
    far_high = lax.ppermute(above[half:], axis, down)
    return [block, below, above, far_low, far_high]


RING = (0, 3, 1, 2)
SPAN = ((0, (0, 1, 2, 3)), (3, (0, 1, 2, 3)), (1, (0, 1, 2, 3)), (2, (0, 1)), (2, (2, 3)))


def gather_weights(mine, theirs, rows):
    x, y, zh = lax.axis_index("x"), lax.axis_index("y"), lax.axis_index("zh")
    half = theirs.shape[1] // 2
    pieces = [mine]
    places = [(i * 2 + zh) * rows for i in range(16)]
    for side, (one, two) in enumerate((("y", "x"), ("x", "y"))):
        block = theirs[:, side * half : (side + 1) * half]
        pieces += spread(ring_blocks(block, one), two)
        for outer, inners in SPAN:
            for inner in inners:
                near, far = (outer, RING[inner]) if side == 0 else (RING[inner], outer)
                places.append(((x + near) % 4 * 8 + (y + far) % 4 * 2 + 1 - zh) * rows)
    return jnp.stack(places), pieces


def project_kernel(parts, places_ref, *refs):
    row_refs, pieces, out_refs = refs[:parts], refs[parts : parts + 11], refs[parts + 11 : 2 * parts + 11]
    held, ordered, weights, row_sems, sems = refs[2 * parts + 11], refs[2 * parts + 12], refs[-5:-2], refs[-2], refs[-1]
    half = out_refs[0].shape[1] // 2
    step = 128

    row_copies, at = [], 0
    for i, rows in enumerate(row_refs):
        row_copies.append(pltpu.make_async_copy(rows, held.at[pl.ds(at, rows.shape[0])], row_sems.at[i]))
        row_copies[-1].start()
        at += rows.shape[0]
    copies = [[], [], []]
    for i, piece in enumerate(pieces):
        which = 0 if i == 0 else 1 + (i - 1) // 5
        at = 0 if i in (0, 1, 6) else at
        for first in range(0, piece.shape[0], 512):
            count = min(512, piece.shape[0] - first)
            copy = pltpu.make_async_copy(
                piece.at[pl.ds(first, count)],
                weights[which].at[pl.ds(at, count)],
                sems.at[sum(len(c) for c in copies)],
            )
            copy.start()
            copies[which].append(copy)
            at += count

    for copy in row_copies:
        copy.wait()
    total = None
    for which in range(3):
        for i in range(16):
            column = pl.multiple_of(places_ref[which * 16 + i], step)
            ordered[:, i * step : (i + 1) * step] = held[:, pl.ds(column, step)]
        for copy in copies[which]:
            copy.wait()
        here = jnp.dot(ordered[...], weights[which][...], preferred_element_type=jnp.float32)
        if which == 0:
            total = here
            continue
        columns = slice((which - 1) * half, which * half)
        here = (total[:, columns] + here).astype(jnp.bfloat16)
        at = 0
        for out_ref in out_refs:
            out_ref[:, columns] = here[at : at + out_ref.shape[0]]
            at += out_ref.shape[0]


def project(places, pieces, rows):
    count, depth = sum(r.shape[0] for r in rows), rows[0].shape[1]
    width = pieces[0].shape[1]
    whole = pl.BlockSpec(memory_space=pltpu.VMEM)
    anywhere = pl.BlockSpec(memory_space=pl.ANY)
    return pl.pallas_call(
        functools.partial(project_kernel, len(rows)),
        out_shape=[jax.ShapeDtypeStruct((r.shape[0], width), jnp.bfloat16) for r in rows],
        in_specs=[pl.BlockSpec(memory_space=pltpu.SMEM)] + [anywhere] * (len(rows) + len(pieces)),
        out_specs=[whole] * len(rows),
        scratch_shapes=[
            pltpu.VMEM((count, depth), jnp.bfloat16),
            pltpu.VMEM((count, depth // 2), jnp.bfloat16),
            pltpu.VMEM((depth // 2, width), jnp.bfloat16),
            pltpu.VMEM((depth // 2, width // 2), jnp.bfloat16),
            pltpu.VMEM((depth // 2, width // 2), jnp.bfloat16),
            pltpu.SemaphoreType.DMA((len(rows),)),
            pltpu.SemaphoreType.DMA((14,)),
        ],
        compiler_params=pltpu.CompilerParams(vmem_limit_bytes=60 * 2**20),
        cost_estimate=pl.CostEstimate(
            flops=2 * count * depth * width, bytes_accessed=2 * depth * (width + count), transcendentals=0
        ),
        name="project",
    )(places, *rows, *pieces)


def attention_kernel(member_ref, lengths_ref, *refs):
    lanes = refs[:4]
    cos_ref, sin_ref, out_ref, queries, keys, values, mixed = refs[4:]
    count = cos_ref.shape[0]
    blocks = count // BLOCK
    part = BLOCK // blocks
    half = HEAD_DIM // 2
    member = member_ref[0]

    taken = lax.broadcasted_iota(jnp.int32, (BLOCK, BLOCK), 1)
    lane, rest = taken // part, taken % part
    group, slot, row = rest // (2 * blocks), (rest // 2) % blocks, rest % 2
    placed = slot * part + (group * 4 + (lane ^ member)) * 2 + row
    wanted = lax.broadcasted_iota(jnp.int32, (BLOCK, BLOCK), 0)
    forward = jnp.where(wanted == placed, 1.0, 0.0).astype(jnp.bfloat16)
    for h in range(blocks):
        chunk = jnp.concatenate([lane_ref[h * part : (h + 1) * part] for lane_ref in lanes], axis=0)
        chunk = jnp.dot(forward, chunk, preferred_element_type=jnp.float32)
        for s in range(blocks):
            rows = slice(s * BLOCK + h * part, s * BLOCK + (h + 1) * part)
            here = chunk[s * part : (s + 1) * part]
            cosine = jnp.concatenate([cos_ref[rows]] * 2, axis=1)
            sine = jnp.concatenate([-sin_ref[rows], sin_ref[rows]], axis=1)

            def rotate(x):
                return (x * cosine + pltpu.roll(x, half, 1) * sine).astype(jnp.bfloat16)

            for g in range(GROUP):
                queries[g, rows] = rotate(here[:, g * HEAD_DIM : (g + 1) * HEAD_DIM])
            keys[rows] = rotate(here[:, GROUP * HEAD_DIM : (GROUP + 1) * HEAD_DIM])
            values[rows] = here[:, (GROUP + 1) * HEAD_DIM :].astype(jnp.bfloat16)

    scale = HEAD_DIM ** (-0.5)
    reach = (MOST - 1 + BLOCK - 1) // BLOCK
    for b in range(blocks):
        first = max(0, b - reach)
        width = (b + 1 - first) * BLOCK
        position = b * BLOCK + lax.broadcasted_iota(jnp.int32, (BLOCK, 1), 0)
        begin, end = jnp.zeros_like(position), jnp.int32(0)
        for j in range(lengths_ref.shape[1]):
            end = end + lengths_ref[0, j]
            begin = jnp.where(position >= end, end, begin)
        key_at = first * BLOCK + lax.broadcasted_iota(jnp.int32, (BLOCK, width), 1)
        allowed = (key_at >= begin) & (key_at <= position)
        key_block = keys[first * BLOCK : (b + 1) * BLOCK]
        value_block = values[first * BLOCK : (b + 1) * BLOCK]
        for g in range(GROUP):
            scores = lax.dot_general(
                queries[g, b * BLOCK : (b + 1) * BLOCK],
                key_block,
                (((1,), (1,)), ((), ())),
                preferred_element_type=jnp.float32,
            )
            scores = jnp.where(allowed, scores * scale, -1e30)
            weights = jnp.exp(scores - jnp.max(scores, axis=1, keepdims=True))
            total = jnp.sum(weights, axis=1, keepdims=True)
            weighted = jnp.dot(
                weights.astype(jnp.bfloat16), value_block, preferred_element_type=jnp.float32
            )
            mixed[b * BLOCK : (b + 1) * BLOCK, g * HEAD_DIM : (g + 1) * HEAD_DIM] = (
                weighted / total
            ).astype(jnp.bfloat16)

    left = lax.broadcasted_iota(jnp.int32, (BLOCK, BLOCK), 0)
    source = ((left // 2) % blocks) * part + (left // (2 * blocks)) * 2 + left % 2
    backward = jnp.where(taken == source, 1.0, 0.0).astype(jnp.bfloat16)
    for h in range(blocks):
        chunk = jnp.concatenate(
            [mixed[s * BLOCK + h * part : s * BLOCK + (h + 1) * part] for s in range(blocks)], axis=0
        )
        out_ref[h * BLOCK : (h + 1) * BLOCK] = jnp.dot(
            backward, chunk, preferred_element_type=jnp.float32
        ).astype(jnp.bfloat16)


def attend(member, lengths, lanes, cosine, sine):
    count = cosine.shape[0]
    whole = pl.BlockSpec(memory_space=pltpu.VMEM)
    scalars = pl.BlockSpec(memory_space=pltpu.SMEM)
    return pl.pallas_call(
        attention_kernel,
        out_shape=jax.ShapeDtypeStruct((count, GROUP * HEAD_DIM), jnp.bfloat16),
        in_specs=[scalars, scalars] + [whole] * 6,
        out_specs=whole,
        scratch_shapes=[
            pltpu.VMEM((GROUP, count, HEAD_DIM), jnp.bfloat16),
            pltpu.VMEM((count, HEAD_DIM), jnp.bfloat16),
            pltpu.VMEM((count, HEAD_DIM), jnp.bfloat16),
            pltpu.VMEM((count, GROUP * HEAD_DIM), jnp.bfloat16),
        ],
        compiler_params=pltpu.CompilerParams(vmem_limit_bytes=24 * 2**20),
        name="attend",
    )(member, lengths, *lanes, cosine, sine)


def on_device(tokens, projection, placement, doc_lengths):
    row_count, width = tokens.shape
    devices = placement.shape[1]
    members = lax.axis_size(CTX)
    groups = devices // members
    piece = row_count // devices
    member = lax.axis_index(CTX)

    mine = lax.all_gather(own_columns(projection, member), ("x", "y"), axis=0, tiled=True)
    theirs = lax.ppermute(own_columns(projection, member ^ 2), ("zh", "zl"), [(0, 3), (3, 0), (1, 2), (2, 1)])
    tables = rotary_tables(doc_lengths[0], members * row_count)
    target = (placement[0][:, None] * piece + jnp.arange(piece, dtype=jnp.int32)[None, :]).reshape(row_count)
    outgoing = sort_rows(tokens, target, groups)
    arrived = lax.all_to_all(outgoing, DP, 0, 0, tiled=True).reshape(row_count, width)
    arrived, theirs, tables = lax.optimization_barrier((arrived, theirs, tables))
    places, pieces = gather_weights(mine, theirs, projection.shape[0])
    across = [(0, 1), (1, 0)]
    far = lax.ppermute(arrived, "zl", across)
    near = lax.ppermute(arrived, "core", across)
    lanes = project(places, pieces, [arrived, near])
    far, lanes = lax.optimization_barrier((far, lanes))
    last = lax.ppermute(far, "core", across)
    lanes = lanes + project(places, pieces, [far]) + project(places, pieces, [last])
    mixed = attend(member.reshape(1), doc_lengths, lanes, *tables)
    returned = lax.all_to_all(
        mixed.reshape(devices, members * piece, GROUP * HEAD_DIM), EVERY, 0, 0, tiled=True
    )
    return unsort_rows(returned.reshape(groups, members, members * piece, GROUP * HEAD_DIM), target)


def solution(mesh):
    sizes = {"x": 4, "y": 4, "zh": 2, "zl": 2, "core": 2}
    fine = Mesh(mesh.devices.reshape(tuple(sizes.values())), tuple(sizes))
    return jax.shard_map(
        on_device,
        mesh=fine,
        in_specs=(P(EVERY, None), P(DP, None), P(EVERY, None), P(DP, None)),
        out_specs=P(EVERY, None),
        check_vma=False,
    )
```

```python
import functools

import jax
import jax.numpy as jnp
from jax import lax
from jax.experimental import pallas as pl
from jax.experimental.pallas import tpu as pltpu
from jax.sharding import Mesh, PartitionSpec as P

HEAD_DIM = 128
HEADS = 16
KV_HEADS = 4
GROUP = HEADS // KV_HEADS
THETA = 500000.0
MOST = 512
DP = ("x", "y", "zh")
CTX = ("zl", "core")
EVERY = DP + CTX
BLOCK = 256


def frequencies():
    half = HEAD_DIM // 2
    return THETA ** (-2.0 * jnp.arange(half, dtype=jnp.float32) / HEAD_DIM)


def rotary_tables(lengths, count):
    position = jnp.arange(count, dtype=jnp.int32)
    ends = jnp.cumsum(lengths)
    begins = jnp.sum(jnp.where(position[:, None] >= ends[None, :], lengths[None, :], 0), axis=1)
    angles = (position - begins).astype(jnp.float32)[:, None] * frequencies()[None, :]
    cosine, sine = jnp.cos(angles), jnp.sin(angles)
    return jnp.concatenate([cosine, cosine], axis=1), jnp.concatenate([-sine, sine], axis=1)


def sort_kernel(target_ref, rows_ref, out_ref):
    count = rows_ref.shape[0]
    order = lax.broadcasted_iota(jnp.int32, (count, count), 0)
    one_hot = jnp.where(order == target_ref[...], 1.0, 0.0).astype(jnp.bfloat16)
    moved = jnp.dot(one_hot, rows_ref[...], preferred_element_type=jnp.float32).astype(jnp.bfloat16)
    out_ref[...] = moved.reshape(out_ref.shape)


def sort_rows(tokens, target, groups):
    count, width = tokens.shape
    rows = count // groups
    tile = 1024
    return pl.pallas_call(
        sort_kernel,
        out_shape=jax.ShapeDtypeStruct((groups, rows, width), tokens.dtype),
        grid=(width // tile,),
        in_specs=[
            pl.BlockSpec((1, count), lambda i: (0, 0)),
            pl.BlockSpec((count, tile), lambda i: (0, i)),
        ],
        out_specs=pl.BlockSpec((groups, rows, tile), lambda i: (0, 0, i)),
        compiler_params=pltpu.CompilerParams(vmem_limit_bytes=32 * 2**20),
        name="sort_rows",
    )(target.reshape(1, count), tokens)


def unsort_kernel(target_ref, rows_ref, out_ref):
    count = out_ref.shape[0]
    order = lax.broadcasted_iota(jnp.int32, (count, count), 1)
    one_hot = jnp.where(order == target_ref[...], 1.0, 0.0).astype(jnp.bfloat16)
    rows = rows_ref[...].reshape(count, out_ref.shape[1])
    out_ref[...] = jnp.dot(one_hot, rows, preferred_element_type=jnp.float32).astype(jnp.bfloat16)


def unsort_rows(returned, target):
    groups, blocks, rows, width = returned.shape
    count = groups * rows
    return pl.pallas_call(
        unsort_kernel,
        out_shape=jax.ShapeDtypeStruct((count, blocks * width), returned.dtype),
        grid=(blocks,),
        in_specs=[
            pl.BlockSpec((count, 1), lambda i: (0, 0)),
            pl.BlockSpec((groups, None, rows, width), lambda i: (0, i, 0, 0)),
        ],
        out_specs=pl.BlockSpec((count, width), lambda i: (0, i)),
        compiler_params=pltpu.CompilerParams(vmem_limit_bytes=32 * 2**20),
        name="unsort_rows",
    )(target.reshape(count, 1), returned)


def own_columns(projection, member):
    query_width, key_width = HEADS * HEAD_DIM, KV_HEADS * HEAD_DIM
    return jnp.concatenate(
        [
            lax.dynamic_slice_in_dim(projection, member * GROUP * HEAD_DIM, GROUP * HEAD_DIM, 1),
            lax.dynamic_slice_in_dim(projection, query_width + member * HEAD_DIM, HEAD_DIM, 1),
            lax.dynamic_slice_in_dim(projection, query_width + key_width + member * HEAD_DIM, HEAD_DIM, 1),
        ],
        axis=1,
    )


def ring_blocks(block, axis):
    ways = [[(i, (i + d) % 4) for i in range(4)] for d in (1, 3, 2)]
    return jnp.concatenate([block] + [lax.ppermute(block, axis, way) for way in ways], axis=0)


def spread(block, axis):
    up, down = [(i, (i + 1) % 4) for i in range(4)], [(i, (i + 3) % 4) for i in range(4)]
    half = block.shape[0] // 2
    below, above = lax.ppermute(block, axis, up), lax.ppermute(block, axis, down)
    far_low = lax.ppermute(below[:half], axis, up)
    far_high = lax.ppermute(above[half:], axis, down)
    return [block, below, above, far_low, far_high]


RING = (0, 3, 1, 2)
SPAN = ((0, (0, 1, 2, 3)), (3, (0, 1, 2, 3)), (1, (0, 1, 2, 3)), (2, (0, 1)), (2, (2, 3)))


def gather_weights(mine, theirs, rows):
    x, y, zh = lax.axis_index("x"), lax.axis_index("y"), lax.axis_index("zh")
    half = theirs.shape[1] // 2
    pieces = [mine]
    places = [(i * 2 + zh) * rows for i in range(16)]
    ready = lax.optimization_barrier([ring_blocks(theirs[:, :half], "y"), ring_blocks(theirs[:, half:], "x")])
    for side, two in enumerate(("x", "y")):
        pieces += spread(ready[side], two)
        for outer, inners in SPAN:
            for inner in inners:
                near, far = (outer, RING[inner]) if side == 0 else (RING[inner], outer)
                places.append(((x + near) % 4 * 8 + (y + far) % 4 * 2 + 1 - zh) * rows)
    return jnp.stack(places), pieces


def project_kernel(places_ref, rows_ref, *refs):
    pieces, out_ref, ordered = refs[:-2], refs[-2], refs[-1]
    width = out_ref.shape[1]
    half = width // 2
    step = 128

    def take(first, count):
        for i in range(count):
            column = pl.multiple_of(places_ref[first + i], step)
            ordered[:, i * step : (i + 1) * step] = rows_ref[:, pl.ds(column, step)]

    def product(parts):
        total, at = None, 0
        for part in parts:
            depth = part.shape[0]
            term = jnp.dot(ordered[:, at : at + depth], part[...], preferred_element_type=jnp.float32)
            total = term if total is None else total + term
            at += depth
        return total

    take(0, 16)
    out = product(pieces[:1])
    for side in range(2):
        take(16 + side * 16, 16)
        other = product(pieces[1 + side * 5 : 6 + side * 5])
        columns = slice(side * half, (side + 1) * half)
        out_ref[:, columns] = (out[:, columns] + other).astype(jnp.bfloat16)


def project(places, pieces, rows):
    count, depth = rows.shape
    width = pieces[0].shape[1]
    whole = pl.BlockSpec(memory_space=pltpu.VMEM)
    return pl.pallas_call(
        project_kernel,
        out_shape=jax.ShapeDtypeStruct((count, width), jnp.bfloat16),
        in_specs=[pl.BlockSpec(memory_space=pltpu.SMEM)] + [whole] * (1 + len(pieces)),
        out_specs=whole,
        scratch_shapes=[pltpu.VMEM((count, depth // 2), jnp.bfloat16)],
        compiler_params=pltpu.CompilerParams(vmem_limit_bytes=24 * 2**20),
        cost_estimate=pl.CostEstimate(
            flops=2 * count * depth * width, bytes_accessed=2 * depth * (width + count), transcendentals=0
        ),
        name="project",
    )(places, rows, *pieces)


def attention_kernel(member_ref, lengths_ref, *refs):
    lanes = refs[:4]
    cos_ref, sin_ref, out_ref, queries, keys, values, mixed = refs[4:]
    count = cos_ref.shape[0]
    blocks = count // BLOCK
    part = BLOCK // blocks
    half = HEAD_DIM // 2
    member = member_ref[0]

    taken = lax.broadcasted_iota(jnp.int32, (BLOCK, BLOCK), 1)
    lane, rest = taken // part, taken % part
    group, slot, row = rest // (2 * blocks), (rest // 2) % blocks, rest % 2
    placed = slot * part + (group * 4 + (lane ^ member)) * 2 + row
    wanted = lax.broadcasted_iota(jnp.int32, (BLOCK, BLOCK), 0)
    forward = jnp.where(wanted == placed, 1.0, 0.0).astype(jnp.bfloat16)
    for h in range(blocks):
        chunk = jnp.concatenate([lane_ref[h * part : (h + 1) * part] for lane_ref in lanes], axis=0)
        chunk = jnp.dot(forward, chunk, preferred_element_type=jnp.float32)
        for s in range(blocks):
            rows = slice(s * BLOCK + h * part, s * BLOCK + (h + 1) * part)
            here = chunk[s * part : (s + 1) * part]
            cosine, sine = cos_ref[rows], sin_ref[rows]

            def rotate(x):
                return (x * cosine + pltpu.roll(x, half, 1) * sine).astype(jnp.bfloat16)

            for g in range(GROUP):
                queries[g, rows] = rotate(here[:, g * HEAD_DIM : (g + 1) * HEAD_DIM])
            keys[rows] = rotate(here[:, GROUP * HEAD_DIM : (GROUP + 1) * HEAD_DIM])
            values[rows] = here[:, (GROUP + 1) * HEAD_DIM :].astype(jnp.bfloat16)

    scale = HEAD_DIM ** (-0.5)
    reach = (MOST - 1 + BLOCK - 1) // BLOCK
    for b in range(blocks):
        first = max(0, b - reach)
        width = (b + 1 - first) * BLOCK
        position = b * BLOCK + lax.broadcasted_iota(jnp.int32, (BLOCK, 1), 0)
        begin, end = jnp.zeros_like(position), jnp.int32(0)
        for j in range(lengths_ref.shape[1]):
            end = end + lengths_ref[0, j]
            begin = jnp.where(position >= end, end, begin)
        key_at = first * BLOCK + lax.broadcasted_iota(jnp.int32, (BLOCK, width), 1)
        allowed = (key_at >= begin) & (key_at <= position)
        key_block = keys[first * BLOCK : (b + 1) * BLOCK]
        value_block = values[first * BLOCK : (b + 1) * BLOCK]
        for g in range(GROUP):
            scores = lax.dot_general(
                queries[g, b * BLOCK : (b + 1) * BLOCK],
                key_block,
                (((1,), (1,)), ((), ())),
                preferred_element_type=jnp.float32,
            )
            scores = jnp.where(allowed, scores * scale, -1e30)
            weights = jnp.exp(scores - jnp.max(scores, axis=1, keepdims=True))
            total = jnp.sum(weights, axis=1, keepdims=True)
            weighted = jnp.dot(
                weights.astype(jnp.bfloat16), value_block, preferred_element_type=jnp.float32
            )
            mixed[b * BLOCK : (b + 1) * BLOCK, g * HEAD_DIM : (g + 1) * HEAD_DIM] = (
                weighted / total
            ).astype(jnp.bfloat16)

    left = lax.broadcasted_iota(jnp.int32, (BLOCK, BLOCK), 0)
    source = ((left // 2) % blocks) * part + (left // (2 * blocks)) * 2 + left % 2
    backward = jnp.where(taken == source, 1.0, 0.0).astype(jnp.bfloat16)
    for h in range(blocks):
        chunk = jnp.concatenate(
            [mixed[s * BLOCK + h * part : s * BLOCK + (h + 1) * part] for s in range(blocks)], axis=0
        )
        out_ref[h * BLOCK : (h + 1) * BLOCK] = jnp.dot(
            backward, chunk, preferred_element_type=jnp.float32
        ).astype(jnp.bfloat16)


def attend(member, lengths, lanes, cosine, sine):
    count = cosine.shape[0]
    whole = pl.BlockSpec(memory_space=pltpu.VMEM)
    scalars = pl.BlockSpec(memory_space=pltpu.SMEM)
    return pl.pallas_call(
        attention_kernel,
        out_shape=jax.ShapeDtypeStruct((count, GROUP * HEAD_DIM), jnp.bfloat16),
        in_specs=[scalars, scalars] + [whole] * 6,
        out_specs=whole,
        scratch_shapes=[
            pltpu.VMEM((GROUP, count, HEAD_DIM), jnp.bfloat16),
            pltpu.VMEM((count, HEAD_DIM), jnp.bfloat16),
            pltpu.VMEM((count, HEAD_DIM), jnp.bfloat16),
            pltpu.VMEM((count, GROUP * HEAD_DIM), jnp.bfloat16),
        ],
        compiler_params=pltpu.CompilerParams(vmem_limit_bytes=24 * 2**20),
        name="attend",
    )(member, lengths, *lanes, cosine, sine)


def on_device(tokens, projection, placement, doc_lengths):
    row_count, width = tokens.shape
    devices = placement.shape[1]
    members = lax.axis_size(CTX)
    groups = devices // members
    piece = row_count // devices
    member = lax.axis_index(CTX)

    mine = lax.all_gather(own_columns(projection, member), ("x", "y"), axis=0, tiled=True)
    theirs = lax.ppermute(own_columns(projection, member ^ 2), ("zh", "zl"), [(0, 3), (3, 0), (1, 2), (2, 1)])
    target = (placement[0][:, None] * piece + jnp.arange(piece, dtype=jnp.int32)[None, :]).reshape(row_count)
    outgoing = sort_rows(tokens, target, groups)
    arrived = lax.all_to_all(outgoing, DP, 0, 0, tiled=True).reshape(row_count, width)
    arrived, theirs = lax.optimization_barrier((arrived, theirs))
    places, pieces = gather_weights(mine, theirs, projection.shape[0])
    across = [(0, 1), (1, 0)]
    far = lax.ppermute(arrived, "zl", across)
    near = lax.ppermute(arrived, "core", across)
    lanes = [project(places, pieces, arrived)]
    tables = rotary_tables(doc_lengths[0], members * row_count)
    far, lanes, tables = lax.optimization_barrier((far, lanes, tables))
    last = lax.ppermute(far, "core", across)
    lanes = lanes + [project(places, pieces, rows) for rows in (near, far, last)]
    mixed = attend(member.reshape(1), doc_lengths, lanes, *tables)
    returned = lax.all_to_all(
        mixed.reshape(devices, members * piece, GROUP * HEAD_DIM), EVERY, 0, 0, tiled=True
    )
    return unsort_rows(returned.reshape(groups, members, members * piece, GROUP * HEAD_DIM), target)


def solution(mesh):
    sizes = {"x": 4, "y": 4, "zh": 2, "zl": 2, "core": 2}
    fine = Mesh(mesh.devices.reshape(tuple(sizes.values())), tuple(sizes))
    return jax.shard_map(
        on_device,
        mesh=fine,
        in_specs=(P(EVERY, None), P(DP, None), P(EVERY, None), P(DP, None)),
        out_specs=P(EVERY, None),
        check_vma=False,
    )
```

```python
import functools
import math

import jax
import jax.numpy as jnp
import numpy as np
from jax import lax
from jax.experimental import pallas as pl
from jax.experimental.pallas import tpu as pltpu
from jax.sharding import Mesh, PartitionSpec as P

HEAD_DIM = 128
HEADS = 16
KV_HEADS = 4
GROUP = HEADS // KV_HEADS
THETA = 500000.0
MOST = 512
DP = ("x", "y", "zh")
CTX = ("zl", "core")
EVERY = DP + CTX
BLOCK = 256


def tables_kernel(lengths_ref, frequency_ref, cos_ref, sin_ref):
    count, width = cos_ref.shape
    step = 128

    @pl.loop(0, count // step)
    def _(i):
        position = i * step + lax.broadcasted_iota(jnp.int32, (step, width), 0)
        begin, end = jnp.zeros_like(position), jnp.int32(0)
        for j in range(lengths_ref.shape[1]):
            end = end + lengths_ref[0, j]
            begin = jnp.where(position >= end, end, begin)
        angle = (position - begin).astype(jnp.float32) * frequency_ref[...]
        rows = pl.ds(pl.multiple_of(i * step, step), step)
        cos_ref[rows] = jnp.cos(angle)
        sine = jnp.sin(angle)
        first = lax.broadcasted_iota(jnp.int32, (step, width), 1) < width // 2
        sin_ref[rows] = jnp.where(first, -sine, sine)


def rotary_tables(lengths, count):
    frequency = THETA ** (-2.0 * np.arange(HEAD_DIM // 2) / HEAD_DIM)
    frequency = np.concatenate([frequency, frequency])[None].astype(np.float32)
    whole = pl.BlockSpec(memory_space=pltpu.VMEM)
    shape = jax.ShapeDtypeStruct((count, HEAD_DIM), jnp.float32)
    return pl.pallas_call(
        tables_kernel,
        out_shape=[shape] * 2,
        in_specs=[pl.BlockSpec(memory_space=pltpu.SMEM), whole],
        out_specs=[pl.BlockSpec((count, HEAD_DIM), lambda: (0, 0))] * 2,
        compiler_params=pltpu.CompilerParams(vmem_limit_bytes=60 * 2**20),
        name="rotary_tables",
    )(lengths, frequency)


def sort_kernel(target_ref, rows_ref, out_ref, held, moved, in_sems, out_sems):
    count = held.shape[0]
    arriving, leaving = [], []
    for i in range(8):
        rows = pl.ds(i * (count // 8), count // 8)
        arriving.append(pltpu.make_async_copy(rows_ref.at[rows], held.at[rows], in_sems.at[i]))
        arriving[-1].start()
    order = lax.broadcasted_iota(jnp.int32, (count, count), 0)
    one_hot = jnp.where(order == target_ref[...], 1.0, 0.0).astype(jnp.bfloat16)
    for copy in arriving:
        copy.wait()
    for i in range(2):
        half = slice(i * (count // 2), (i + 1) * (count // 2))
        moved[half] = jnp.dot(one_hot[half], held[...], preferred_element_type=jnp.float32).astype(jnp.bfloat16)
        for j in range(4):
            rows = pl.ds((i * 4 + j) * (count // 8), count // 8)
            leaving.append(pltpu.make_async_copy(moved.at[rows], out_ref.at[rows], out_sems.at[i * 4 + j]))
            leaving[-1].start()
    for copy in leaving:
        copy.wait()


def sort_rows(tokens, target, groups):
    count, width = tokens.shape
    anywhere = pl.BlockSpec(memory_space=pl.ANY)
    moved = pl.pallas_call(
        sort_kernel,
        out_shape=jax.ShapeDtypeStruct(tokens.shape, tokens.dtype),
        in_specs=[pl.BlockSpec(memory_space=pltpu.VMEM), anywhere],
        out_specs=anywhere,
        scratch_shapes=[
            pltpu.VMEM(tokens.shape, tokens.dtype),
            pltpu.VMEM(tokens.shape, tokens.dtype),
            pltpu.SemaphoreType.DMA((8,)),
            pltpu.SemaphoreType.DMA((8,)),
        ],
        compiler_params=pltpu.CompilerParams(vmem_limit_bytes=60 * 2**20),
        name="sort_rows",
    )(target.reshape(1, count), tokens)
    return moved.reshape(groups, count // groups, width)


def unsort_kernel(target_ref, rows_ref, out_ref):
    count = out_ref.shape[0]
    order = lax.broadcasted_iota(jnp.int32, (count, count), 1)
    one_hot = jnp.where(order == target_ref[...], 1.0, 0.0).astype(jnp.bfloat16)
    rows = rows_ref[...].reshape(count, out_ref.shape[1])
    out_ref[...] = jnp.dot(one_hot, rows, preferred_element_type=jnp.float32).astype(jnp.bfloat16)


def unsort_rows(returned, target):
    groups, blocks, rows, width = returned.shape
    count = groups * rows
    return pl.pallas_call(
        unsort_kernel,
        out_shape=jax.ShapeDtypeStruct((count, blocks * width), returned.dtype),
        grid=(blocks,),
        in_specs=[
            pl.BlockSpec((count, 1), lambda i: (0, 0)),
            pl.BlockSpec((groups, None, rows, width), lambda i: (0, i, 0, 0)),
        ],
        out_specs=pl.BlockSpec((count, width), lambda i: (0, i)),
        compiler_params=pltpu.CompilerParams(vmem_limit_bytes=32 * 2**20),
        name="unsort_rows",
    )(target.reshape(count, 1), returned)


def own_columns(projection, member):
    query_width, key_width = HEADS * HEAD_DIM, KV_HEADS * HEAD_DIM
    return jnp.concatenate(
        [
            lax.dynamic_slice_in_dim(projection, member * GROUP * HEAD_DIM, GROUP * HEAD_DIM, 1),
            lax.dynamic_slice_in_dim(projection, query_width + member * HEAD_DIM, HEAD_DIM, 1),
            lax.dynamic_slice_in_dim(projection, query_width + key_width + member * HEAD_DIM, HEAD_DIM, 1),
        ],
        axis=1,
    )


def ring_blocks(block, axis):
    ways = [[(i, (i + d) % 4) for i in range(4)] for d in (1, 3, 2)]
    return jnp.concatenate([block] + [lax.ppermute(block, axis, way) for way in ways], axis=0)


def spread(block, axis):
    up, down = [(i, (i + 1) % 4) for i in range(4)], [(i, (i + 3) % 4) for i in range(4)]
    half = block.shape[0] // 2
    below, above = lax.ppermute(block, axis, up), lax.ppermute(block, axis, down)
    far_low = lax.ppermute(below[:half], axis, up)
    far_high = lax.ppermute(above[half:], axis, down)
    return [block, below, above, far_low, far_high]


RING = (0, 3, 1, 2)
SPAN = ((0, (0, 1, 2, 3)), (3, (0, 1, 2, 3)), (1, (0, 1, 2, 3)), (2, (0, 1)), (2, (2, 3)))


def gather_weights(mine, theirs, rows):
    x, y, zh = lax.axis_index("x"), lax.axis_index("y"), lax.axis_index("zh")
    half = theirs.shape[1] // 2
    pieces = [mine]
    places = [(i * 2 + zh) * rows for i in range(16)]
    ready = lax.optimization_barrier([ring_blocks(theirs[:, :half], "y"), ring_blocks(theirs[:, half:], "x")])
    for side, two in enumerate(("x", "y")):
        pieces += spread(ready[side], two)
        for outer, inners in SPAN:
            for inner in inners:
                near, far = (outer, RING[inner]) if side == 0 else (RING[inner], outer)
                places.append(((x + near) % 4 * 8 + (y + far) % 4 * 2 + 1 - zh) * rows)
    return jnp.stack(places), pieces


def project_kernel(parts, places_ref, *refs):
    row_refs, refs = refs[:parts], refs[parts:]
    pieces, out_refs, ordered = refs[: -parts - 1], refs[-parts - 1 : -1], refs[-1]
    half = out_refs[0].shape[1] // 2
    step = 128

    def take(first, count):
        for i in range(count):
            column = pl.multiple_of(places_ref[first + i], step)
            at = 0
            for rows in row_refs:
                ordered[at : at + rows.shape[0], i * step : (i + 1) * step] = rows[:, pl.ds(column, step)]
                at += rows.shape[0]

    def product(pieces):
        total, at = None, 0
        for piece in pieces:
            depth = piece.shape[0]
            term = jnp.dot(ordered[:, at : at + depth], piece[...], preferred_element_type=jnp.float32)
            total = term if total is None else total + term
            at += depth
        return total

    take(0, 16)
    out = product(pieces[:1])
    for side in range(2):
        take(16 + side * 16, 16)
        columns = slice(side * half, (side + 1) * half)
        here = (out[:, columns] + product(pieces[1 + side * 5 : 6 + side * 5])).astype(jnp.bfloat16)
        at = 0
        for out_ref in out_refs:
            out_ref[:, columns] = here[at : at + out_ref.shape[0]]
            at += out_ref.shape[0]


def project(places, pieces, rows):
    count, depth = sum(r.shape[0] for r in rows), rows[0].shape[1]
    width = pieces[0].shape[1]
    whole = pl.BlockSpec(memory_space=pltpu.VMEM)
    return pl.pallas_call(
        functools.partial(project_kernel, len(rows)),
        out_shape=[jax.ShapeDtypeStruct((r.shape[0], width), jnp.bfloat16) for r in rows],
        in_specs=[pl.BlockSpec(memory_space=pltpu.SMEM)] + [whole] * (len(rows) + len(pieces)),
        out_specs=[whole] * len(rows),
        scratch_shapes=[pltpu.VMEM((count, depth // 2), jnp.bfloat16)],
        compiler_params=pltpu.CompilerParams(vmem_limit_bytes=24 * 2**20),
        cost_estimate=pl.CostEstimate(
            flops=2 * count * depth * width, bytes_accessed=2 * depth * (width + count), transcendentals=0
        ),
        name="project",
    )(places, *rows, *pieces)


def attention_kernel(member_ref, lengths_ref, *refs):
    lanes = refs[:4]
    cos_ref, sin_ref, out_ref, queries, keys, values, mixed = refs[4:]
    count = cos_ref.shape[0]
    blocks = count // BLOCK
    part = BLOCK // blocks
    half = HEAD_DIM // 2
    member = member_ref[0]

    taken = lax.broadcasted_iota(jnp.int32, (BLOCK, BLOCK), 1)
    lane, rest = taken // part, taken % part
    group, slot, row = rest // (2 * blocks), (rest // 2) % blocks, rest % 2
    placed = slot * part + (group * 4 + (lane ^ member)) * 2 + row
    wanted = lax.broadcasted_iota(jnp.int32, (BLOCK, BLOCK), 0)
    forward = jnp.where(wanted == placed, 1.0, 0.0).astype(jnp.bfloat16)
    for h in range(blocks):
        chunk = jnp.concatenate([lane_ref[h * part : (h + 1) * part] for lane_ref in lanes], axis=0)
        chunk = jnp.dot(forward, chunk, preferred_element_type=jnp.float32)
        for s in range(blocks):
            rows = slice(s * BLOCK + h * part, s * BLOCK + (h + 1) * part)
            here = chunk[s * part : (s + 1) * part]
            cosine, sine = cos_ref[rows], sin_ref[rows]

            def rotate(x):
                return (x * cosine + pltpu.roll(x, half, 1) * sine).astype(jnp.bfloat16)

            for g in range(GROUP):
                queries[g, rows] = rotate(here[:, g * HEAD_DIM : (g + 1) * HEAD_DIM])
            keys[rows] = rotate(here[:, GROUP * HEAD_DIM : (GROUP + 1) * HEAD_DIM])
            values[rows] = here[:, (GROUP + 1) * HEAD_DIM :].astype(jnp.bfloat16)

    scale = HEAD_DIM ** (-0.5) * math.log2(math.e)
    reach = (MOST - 1 + BLOCK - 1) // BLOCK
    for b in range(blocks):
        first = max(0, b - reach)
        width = (b + 1 - first) * BLOCK
        position = b * BLOCK + lax.broadcasted_iota(jnp.int32, (BLOCK, 1), 0)
        begin, end = jnp.zeros_like(position), jnp.int32(0)
        for j in range(lengths_ref.shape[1]):
            end = end + lengths_ref[0, j]
            begin = jnp.where(position >= end, end, begin)
        key_at = first * BLOCK + lax.broadcasted_iota(jnp.int32, (BLOCK, width), 1)
        allowed = (key_at >= begin) & (key_at <= position)
        key_block = keys[first * BLOCK : (b + 1) * BLOCK]
        value_block = values[first * BLOCK : (b + 1) * BLOCK]
        for g in range(GROUP):
            scores = lax.dot_general(
                queries[g, b * BLOCK : (b + 1) * BLOCK],
                key_block,
                (((1,), (1,)), ((), ())),
                preferred_element_type=jnp.float32,
            )
            scores = jnp.where(allowed, scores, -1e30)
            weights = jnp.exp2((scores - jnp.max(scores, axis=1, keepdims=True)) * scale)
            total = jnp.sum(weights, axis=1, keepdims=True)
            weighted = jnp.dot(
                weights.astype(jnp.bfloat16), value_block, preferred_element_type=jnp.float32
            )
            mixed[b * BLOCK : (b + 1) * BLOCK, g * HEAD_DIM : (g + 1) * HEAD_DIM] = (
                weighted / total
            ).astype(jnp.bfloat16)

    left = lax.broadcasted_iota(jnp.int32, (BLOCK, BLOCK), 0)
    source = ((left // 2) % blocks) * part + (left // (2 * blocks)) * 2 + left % 2
    backward = jnp.where(taken == source, 1.0, 0.0).astype(jnp.bfloat16)
    for h in range(blocks):
        chunk = jnp.concatenate(
            [mixed[s * BLOCK + h * part : s * BLOCK + (h + 1) * part] for s in range(blocks)], axis=0
        )
        out_ref[h * BLOCK : (h + 1) * BLOCK] = jnp.dot(
            backward, chunk, preferred_element_type=jnp.float32
        ).astype(jnp.bfloat16)


def attend(member, lengths, lanes, cosine, sine):
    count = cosine.shape[0]
    whole = pl.BlockSpec(memory_space=pltpu.VMEM)
    scalars = pl.BlockSpec(memory_space=pltpu.SMEM)
    return pl.pallas_call(
        attention_kernel,
        out_shape=jax.ShapeDtypeStruct((count, GROUP * HEAD_DIM), jnp.bfloat16),
        in_specs=[scalars, scalars] + [whole] * 6,
        out_specs=whole,
        scratch_shapes=[
            pltpu.VMEM((GROUP, count, HEAD_DIM), jnp.bfloat16),
            pltpu.VMEM((count, HEAD_DIM), jnp.bfloat16),
            pltpu.VMEM((count, HEAD_DIM), jnp.bfloat16),
            pltpu.VMEM((count, GROUP * HEAD_DIM), jnp.bfloat16),
        ],
        compiler_params=pltpu.CompilerParams(vmem_limit_bytes=24 * 2**20),
        name="attend",
    )(member, lengths, *lanes, cosine, sine)


def on_device(tokens, projection, placement, doc_lengths):
    row_count, width = tokens.shape
    devices = placement.shape[1]
    members = lax.axis_size(CTX)
    groups = devices // members
    piece = row_count // devices
    member = lax.axis_index(CTX)

    mine = lax.all_gather(own_columns(projection, member), ("x", "y"), axis=0, tiled=True)
    theirs = lax.ppermute(own_columns(projection, member ^ 2), ("zh", "zl"), [(0, 3), (3, 0), (1, 2), (2, 1)])
    target = (placement[0][:, None] * piece + jnp.arange(piece, dtype=jnp.int32)[None, :]).reshape(row_count)
    outgoing = sort_rows(tokens, target, groups)
    arrived = lax.all_to_all(outgoing, DP, 0, 0, tiled=True).reshape(row_count, width)
    tables = rotary_tables(doc_lengths, members * row_count)
    arrived, theirs, tables = lax.optimization_barrier((arrived, theirs, tables))
    places, pieces = gather_weights(mine, theirs, projection.shape[0])
    across = [(0, 1), (1, 0)]
    far = lax.ppermute(arrived, "zl", across)
    near = lax.ppermute(arrived, "core", across)
    lanes = project(places, pieces, [arrived])
    far, lanes = lax.optimization_barrier((far, lanes))
    last = lax.ppermute(far, "core", across)
    lanes = lanes + project(places, pieces, [near, far]) + project(places, pieces, [last])
    mixed = attend(member.reshape(1), doc_lengths, lanes, *tables)
    returned = lax.all_to_all(
        mixed.reshape(devices, members * piece, GROUP * HEAD_DIM), EVERY, 0, 0, tiled=True
    )
    return unsort_rows(returned.reshape(groups, members, members * piece, GROUP * HEAD_DIM), target)


def solution(mesh):
    sizes = {"x": 4, "y": 4, "zh": 2, "zl": 2, "core": 2}
    fine = Mesh(mesh.devices.reshape(tuple(sizes.values())), tuple(sizes))
    return jax.shard_map(
        on_device,
        mesh=fine,
        in_specs=(P(EVERY, None), P(DP, None), P(EVERY, None), P(DP, None)),
        out_specs=P(EVERY, None),
        check_vma=False,
    )
```

```python
import functools
import math

import jax
import jax.numpy as jnp
import numpy as np
from jax import lax
from jax.experimental import pallas as pl
from jax.experimental.pallas import tpu as pltpu
from jax.sharding import Mesh, PartitionSpec as P

HEAD_DIM = 128
HEADS = 16
KV_HEADS = 4
GROUP = HEADS // KV_HEADS
THETA = 500000.0
MOST = 512
DP = ("x", "y", "zh")
CTX = ("zl", "core")
EVERY = DP + CTX
BLOCK = 256


def tables_kernel(lengths_ref, frequency_ref, cos_ref, sin_ref):
    count, width = cos_ref.shape
    step = 128

    @pl.loop(0, count // step)
    def _(i):
        position = i * step + lax.broadcasted_iota(jnp.int32, (step, width), 0)
        begin, end = jnp.zeros_like(position), jnp.int32(0)
        for j in range(lengths_ref.shape[1]):
            end = end + lengths_ref[0, j]
            begin = jnp.where(position >= end, end, begin)
        angle = (position - begin).astype(jnp.float32) * frequency_ref[...]
        rows = pl.ds(pl.multiple_of(i * step, step), step)
        cos_ref[rows] = jnp.cos(angle)
        sine = jnp.sin(angle)
        first = lax.broadcasted_iota(jnp.int32, (step, width), 1) < width // 2
        sin_ref[rows] = jnp.where(first, -sine, sine)


def rotary_tables(lengths, count):
    frequency = THETA ** (-2.0 * np.arange(HEAD_DIM // 2) / HEAD_DIM)
    frequency = np.concatenate([frequency, frequency])[None].astype(np.float32)
    whole = pl.BlockSpec(memory_space=pltpu.VMEM)
    shape = jax.ShapeDtypeStruct((count, HEAD_DIM), jnp.float32)
    return pl.pallas_call(
        tables_kernel,
        out_shape=[shape] * 2,
        in_specs=[pl.BlockSpec(memory_space=pltpu.SMEM), whole],
        out_specs=[pl.BlockSpec((count, HEAD_DIM), lambda: (0, 0))] * 2,
        compiler_params=pltpu.CompilerParams(vmem_limit_bytes=63 * 2**20),
        name="rotary_tables",
    )(lengths, frequency)


def sort_kernel(member_ref, placement_ref, rows_ref, projection_ref, out_ref, mine_ref, theirs_ref, held, moved, columns, *sems):
    in_sems, out_sems, column_sems, head_sems = sems
    count, devices = held.shape[0], placement_ref.shape[1]
    piece = count // devices
    arriving, leaving = [], []
    for i in range(8):
        rows = pl.ds(i * (count // 8), count // 8)
        arriving.append(pltpu.make_async_copy(rows_ref.at[rows], held.at[rows], in_sems.at[i]))
        arriving[-1].start()
    taking = []
    for i, member in enumerate((member_ref[0], member_ref[0] ^ 2)):
        at, source = 0, 0
        for heads, width in ((KV_HEADS, GROUP * HEAD_DIM), (KV_HEADS, HEAD_DIM), (KV_HEADS, HEAD_DIM)):
            copy = pltpu.make_async_copy(
                projection_ref.at[:, pl.ds(pl.multiple_of(source + member * width, HEAD_DIM), width)],
                columns.at[i, :, pl.ds(at, width)],
                column_sems.at[len(taking)],
            )
            copy.start()
            taking.append(copy)
            at, source = at + width, source + heads * width

    device = lax.broadcasted_iota(jnp.int32, (devices, devices), 0)
    pieces = jnp.where(device == placement_ref[...], 1.0, 0.0).astype(jnp.bfloat16)
    down = lax.broadcasted_iota(jnp.int32, (count, devices), 0) // piece
    tall = jnp.where(down == lax.broadcasted_iota(jnp.int32, (count, devices), 1), 1.0, 0.0).astype(jnp.bfloat16)
    along = lax.broadcasted_iota(jnp.int32, (devices, count), 1) // piece
    wide = jnp.where(along == lax.broadcasted_iota(jnp.int32, (devices, count), 0), 1.0, 0.0).astype(jnp.bfloat16)
    tall = jnp.dot(tall, pieces, preferred_element_type=jnp.float32).astype(jnp.bfloat16)
    both = jnp.dot(tall, wide, preferred_element_type=jnp.float32)
    row = lax.broadcasted_iota(jnp.int32, (count, count), 0) % piece
    same = row == lax.broadcasted_iota(jnp.int32, (count, count), 1) % piece
    one_hot = jnp.where(same, both, 0.0).astype(jnp.bfloat16)

    for copy in taking:
        copy.wait()
    for i, out in enumerate((mine_ref, theirs_ref)):
        leaving.append(pltpu.make_async_copy(columns.at[i], out, head_sems.at[i]))
        leaving[-1].start()
    for copy in arriving:
        copy.wait()
    for i in range(2):
        half = slice(i * (count // 2), (i + 1) * (count // 2))
        moved[half] = jnp.dot(one_hot[half], held[...], preferred_element_type=jnp.float32).astype(jnp.bfloat16)
        for j in range(4):
            rows = pl.ds((i * 4 + j) * (count // 8), count // 8)
            leaving.append(pltpu.make_async_copy(moved.at[rows], out_ref.at[rows], out_sems.at[i * 4 + j]))
            leaving[-1].start()
    for copy in leaving:
        copy.wait()


def sort_rows(tokens, placement, projection, member):
    anywhere = pl.BlockSpec(memory_space=pl.ANY)
    columns = (projection.shape[0], (GROUP + 2) * HEAD_DIM)
    return pl.pallas_call(
        sort_kernel,
        out_shape=[jax.ShapeDtypeStruct(shape, tokens.dtype) for shape in (tokens.shape, columns, columns)],
        in_specs=[
            pl.BlockSpec(memory_space=pltpu.SMEM),
            pl.BlockSpec(memory_space=pltpu.VMEM),
            anywhere,
            anywhere,
        ],
        out_specs=[anywhere] * 3,
        scratch_shapes=[
            pltpu.VMEM(tokens.shape, tokens.dtype),
            pltpu.VMEM(tokens.shape, tokens.dtype),
            pltpu.VMEM((2,) + columns, tokens.dtype),
            pltpu.SemaphoreType.DMA((8,)),
            pltpu.SemaphoreType.DMA((8,)),
            pltpu.SemaphoreType.DMA((6,)),
            pltpu.SemaphoreType.DMA((2,)),
        ],
        compiler_params=pltpu.CompilerParams(vmem_limit_bytes=60 * 2**20),
        name="sort_rows",
    )(member.reshape(1), placement, tokens, projection)


def unsort_kernel(target_ref, rows_ref, out_ref):
    count = out_ref.shape[0]
    order = lax.broadcasted_iota(jnp.int32, (count, count), 1)
    one_hot = jnp.where(order == target_ref[...], 1.0, 0.0).astype(jnp.bfloat16)
    rows = rows_ref[...].reshape(count, out_ref.shape[1])
    out_ref[...] = jnp.dot(one_hot, rows, preferred_element_type=jnp.float32).astype(jnp.bfloat16)


def unsort_rows(returned, target):
    groups, blocks, rows, width = returned.shape
    count = groups * rows
    return pl.pallas_call(
        unsort_kernel,
        out_shape=jax.ShapeDtypeStruct((count, blocks * width), returned.dtype),
        grid=(blocks,),
        in_specs=[
            pl.BlockSpec((count, 1), lambda i: (0, 0)),
            pl.BlockSpec((groups, None, rows, width), lambda i: (0, i, 0, 0)),
        ],
        out_specs=pl.BlockSpec((count, width), lambda i: (0, i)),
        compiler_params=pltpu.CompilerParams(vmem_limit_bytes=32 * 2**20),
        name="unsort_rows",
    )(target.reshape(count, 1), returned)


def ring_blocks(block, axis):
    ways = [[(i, (i + d) % 4) for i in range(4)] for d in (1, 3, 2)]
    return jnp.concatenate([block] + [lax.ppermute(block, axis, way) for way in ways], axis=0)


UP, DOWN = [(i, (i + 1) % 4) for i in range(4)], [(i, (i + 3) % 4) for i in range(4)]


def spread(blocks):
    pairs = [(lax.ppermute(b, axis, UP), lax.ppermute(b, axis, DOWN)) for b, axis in zip(blocks, ("x", "y"))]
    half = blocks[0].shape[0] // 2
    halves = [h for below, above in pairs for h in (below[:half], above[half:])]
    far = [lax.ppermute(h, axis, way) for h, axis, way in zip(halves, ("x", "x", "y", "y"), (UP, DOWN, UP, DOWN))]
    return [[blocks[i], *pairs[i], *far[2 * i : 2 * i + 2]] for i in range(2)]


RING = (0, 3, 1, 2)
SPAN = ((0, (0, 1, 2, 3)), (3, (0, 1, 2, 3)), (1, (0, 1, 2, 3)), (2, (0, 1)), (2, (2, 3)))


def gather_weights(mine, theirs, rows):
    x, y, zh = lax.axis_index("x"), lax.axis_index("y"), lax.axis_index("zh")
    half = theirs.shape[1] // 2
    pieces = [mine]
    places = [(i * 2 + zh) * rows for i in range(16)]
    ready = lax.optimization_barrier([ring_blocks(theirs[:, :half], "y"), ring_blocks(theirs[:, half:], "x")])
    for side, spreads in enumerate(spread(ready)):
        pieces += spreads
        for outer, inners in SPAN:
            for inner in inners:
                near, far = (outer, RING[inner]) if side == 0 else (RING[inner], outer)
                places.append(((x + near) % 4 * 8 + (y + far) % 4 * 2 + 1 - zh) * rows)
    return jnp.stack(places), pieces


def project_kernel(parts, places_ref, *refs):
    row_refs, refs = refs[:parts], refs[parts:]
    pieces, out_refs, ordered = refs[: -parts - 1], refs[-parts - 1 : -1], refs[-1]
    half = out_refs[0].shape[1] // 2
    step = 128

    def take(first, count):
        for i in range(count):
            column = pl.multiple_of(places_ref[first + i], step)
            at = 0
            for rows in row_refs:
                ordered[at : at + rows.shape[0], i * step : (i + 1) * step] = rows[:, pl.ds(column, step)]
                at += rows.shape[0]

    def product(pieces):
        total, at = None, 0
        for piece in pieces:
            depth = piece.shape[0]
            term = jnp.dot(ordered[:, at : at + depth], piece[...], preferred_element_type=jnp.float32)
            total = term if total is None else total + term
            at += depth
        return total

    take(0, 16)
    out = product(pieces[:1])
    for side in range(2):
        take(16 + side * 16, 16)
        columns = slice(side * half, (side + 1) * half)
        here = (out[:, columns] + product(pieces[1 + side * 5 : 6 + side * 5])).astype(jnp.bfloat16)
        at = 0
        for out_ref in out_refs:
            out_ref[:, columns] = here[at : at + out_ref.shape[0]]
            at += out_ref.shape[0]


def project(places, pieces, rows):
    count, depth = sum(r.shape[0] for r in rows), rows[0].shape[1]
    width = pieces[0].shape[1]
    whole = pl.BlockSpec(memory_space=pltpu.VMEM)
    return pl.pallas_call(
        functools.partial(project_kernel, len(rows)),
        out_shape=[jax.ShapeDtypeStruct((r.shape[0], width), jnp.bfloat16) for r in rows],
        in_specs=[pl.BlockSpec(memory_space=pltpu.SMEM)] + [whole] * (len(rows) + len(pieces)),
        out_specs=[whole] * len(rows),
        scratch_shapes=[pltpu.VMEM((count, depth // 2), jnp.bfloat16)],
        compiler_params=pltpu.CompilerParams(vmem_limit_bytes=24 * 2**20),
        cost_estimate=pl.CostEstimate(
            flops=2 * count * depth * width, bytes_accessed=2 * depth * (width + count), transcendentals=0
        ),
        name="project",
    )(places, *rows, *pieces)


def attention_kernel(member_ref, lengths_ref, *refs):
    lanes = refs[:4]
    cos_ref, sin_ref, out_ref, queries, keys, values, mixed = refs[4:]
    count = cos_ref.shape[0]
    blocks = count // BLOCK
    part = BLOCK // blocks
    half = HEAD_DIM // 2
    member = member_ref[0]

    taken = lax.broadcasted_iota(jnp.int32, (BLOCK, BLOCK), 1)
    lane, rest = taken // part, taken % part
    group, slot, row = rest // (2 * blocks), (rest // 2) % blocks, rest % 2
    placed = slot * part + (group * 4 + (lane ^ member)) * 2 + row
    wanted = lax.broadcasted_iota(jnp.int32, (BLOCK, BLOCK), 0)
    forward = jnp.where(wanted == placed, 1.0, 0.0).astype(jnp.bfloat16)
    for h in range(blocks):
        chunk = jnp.concatenate([lane_ref[h * part : (h + 1) * part] for lane_ref in lanes], axis=0)
        chunk = jnp.dot(forward, chunk, preferred_element_type=jnp.float32)
        for s in range(blocks):
            rows = slice(s * BLOCK + h * part, s * BLOCK + (h + 1) * part)
            here = chunk[s * part : (s + 1) * part]
            cosine, sine = cos_ref[rows], sin_ref[rows]

            def rotate(x):
                return (x * cosine + pltpu.roll(x, half, 1) * sine).astype(jnp.bfloat16)

            for g in range(GROUP):
                queries[g, rows] = rotate(here[:, g * HEAD_DIM : (g + 1) * HEAD_DIM])
            keys[rows] = rotate(here[:, GROUP * HEAD_DIM : (GROUP + 1) * HEAD_DIM])
            values[rows] = here[:, (GROUP + 1) * HEAD_DIM :].astype(jnp.bfloat16)

    scale = HEAD_DIM ** (-0.5) * math.log2(math.e)
    reach = (MOST - 1 + BLOCK - 1) // BLOCK
    for b in range(blocks):
        first = max(0, b - reach)
        width = (b + 1 - first) * BLOCK
        position = b * BLOCK + lax.broadcasted_iota(jnp.int32, (BLOCK, 1), 0)
        begin, end = jnp.zeros_like(position), jnp.int32(0)
        for j in range(lengths_ref.shape[1]):
            end = end + lengths_ref[0, j]
            begin = jnp.where(position >= end, end, begin)
        key_at = first * BLOCK + lax.broadcasted_iota(jnp.int32, (BLOCK, width), 1)
        allowed = (key_at >= begin) & (key_at <= position)
        key_block = keys[first * BLOCK : (b + 1) * BLOCK]
        value_block = values[first * BLOCK : (b + 1) * BLOCK]
        for g in range(GROUP):
            scores = lax.dot_general(
                queries[g, b * BLOCK : (b + 1) * BLOCK],
                key_block,
                (((1,), (1,)), ((), ())),
                preferred_element_type=jnp.float32,
            )
            scores = jnp.where(allowed, scores, -1e30)
            weights = jnp.exp2((scores - jnp.max(scores, axis=1, keepdims=True)) * scale)
            total = jnp.sum(weights, axis=1, keepdims=True)
            weighted = jnp.dot(
                weights.astype(jnp.bfloat16), value_block, preferred_element_type=jnp.float32
            )
            mixed[b * BLOCK : (b + 1) * BLOCK, g * HEAD_DIM : (g + 1) * HEAD_DIM] = (
                weighted / total
            ).astype(jnp.bfloat16)

    left = lax.broadcasted_iota(jnp.int32, (BLOCK, BLOCK), 0)
    source = ((left // 2) % blocks) * part + (left // (2 * blocks)) * 2 + left % 2
    backward = jnp.where(taken == source, 1.0, 0.0).astype(jnp.bfloat16)
    for h in range(blocks):
        chunk = jnp.concatenate(
            [mixed[s * BLOCK + h * part : s * BLOCK + (h + 1) * part] for s in range(blocks)], axis=0
        )
        out_ref[h * BLOCK : (h + 1) * BLOCK] = jnp.dot(
            backward, chunk, preferred_element_type=jnp.float32
        ).astype(jnp.bfloat16)


def attend(member, lengths, lanes, cosine, sine):
    count = cosine.shape[0]
    whole = pl.BlockSpec(memory_space=pltpu.VMEM)
    scalars = pl.BlockSpec(memory_space=pltpu.SMEM)
    return pl.pallas_call(
        attention_kernel,
        out_shape=jax.ShapeDtypeStruct((count, GROUP * HEAD_DIM), jnp.bfloat16),
        in_specs=[scalars, scalars] + [whole] * 6,
        out_specs=whole,
        scratch_shapes=[
            pltpu.VMEM((GROUP, count, HEAD_DIM), jnp.bfloat16),
            pltpu.VMEM((count, HEAD_DIM), jnp.bfloat16),
            pltpu.VMEM((count, HEAD_DIM), jnp.bfloat16),
            pltpu.VMEM((count, GROUP * HEAD_DIM), jnp.bfloat16),
        ],
        compiler_params=pltpu.CompilerParams(vmem_limit_bytes=24 * 2**20),
        name="attend",
    )(member, lengths, *lanes, cosine, sine)


def on_device(tokens, projection, placement, doc_lengths):
    row_count, width = tokens.shape
    devices = placement.shape[1]
    members = lax.axis_size(CTX)
    groups = devices // members
    piece = row_count // devices
    member = lax.axis_index(CTX)

    outgoing, mine, theirs = sort_rows(tokens, placement, projection, member)
    outgoing = outgoing.reshape(groups, row_count // groups, width)
    mine = lax.all_gather(mine, ("x", "y"), axis=0, tiled=True)
    theirs = lax.ppermute(theirs, ("zh", "zl"), [(0, 3), (3, 0), (1, 2), (2, 1)])
    target = (placement[0][:, None] * piece + jnp.arange(piece, dtype=jnp.int32)[None, :]).reshape(row_count)
    arrived = lax.all_to_all(outgoing, DP, 0, 0, tiled=True).reshape(row_count, width)
    tables = rotary_tables(doc_lengths, members * row_count)
    arrived, theirs, tables = lax.optimization_barrier((arrived, theirs, tables))
    places, pieces = gather_weights(mine, theirs, projection.shape[0])
    across = [(0, 1), (1, 0)]
    far = lax.ppermute(arrived, "zl", across)
    near = lax.ppermute(arrived, "core", across)
    lanes = project(places, pieces, [arrived])
    far, lanes = lax.optimization_barrier((far, lanes))
    last = lax.ppermute(far, "core", across)
    lanes = lanes + project(places, pieces, [near, far]) + project(places, pieces, [last])
    mixed = attend(member.reshape(1), doc_lengths, lanes, *tables)
    returned = lax.all_to_all(
        mixed.reshape(devices, members * piece, GROUP * HEAD_DIM), EVERY, 0, 0, tiled=True
    )
    return unsort_rows(returned.reshape(groups, members, members * piece, GROUP * HEAD_DIM), target)


def solution(mesh):
    sizes = {"x": 4, "y": 4, "zh": 2, "zl": 2, "core": 2}
    fine = Mesh(mesh.devices.reshape(tuple(sizes.values())), tuple(sizes))
    return jax.shard_map(
        on_device,
        mesh=fine,
        in_specs=(P(EVERY, None), P(DP, None), P(EVERY, None), P(DP, None)),
        out_specs=P(EVERY, None),
        check_vma=False,
    )
```

```python
import functools
import math

import jax
import jax.numpy as jnp
import numpy as np
from jax import lax
from jax.experimental import pallas as pl
from jax.experimental.pallas import tpu as pltpu
from jax.sharding import Mesh, PartitionSpec as P

HEAD_DIM = 128
HEADS = 16
KV_HEADS = 4
GROUP = HEADS // KV_HEADS
THETA = 500000.0
MOST = 512
DP = ("x", "y", "zh")
CTX = ("zl", "core")
EVERY = DP + CTX
BLOCK = 256


def tables_kernel(lengths_ref, frequency_ref, cos_ref, sin_ref):
    count, width = cos_ref.shape
    step = 128

    @pl.loop(0, count // step)
    def _(i):
        position = i * step + lax.broadcasted_iota(jnp.int32, (step, width), 0)
        begin, end = jnp.zeros_like(position), jnp.int32(0)
        for j in range(lengths_ref.shape[1]):
            end = end + lengths_ref[0, j]
            begin = jnp.where(position >= end, end, begin)
        angle = (position - begin).astype(jnp.float32) * frequency_ref[...]
        rows = pl.ds(pl.multiple_of(i * step, step), step)
        cos_ref[rows] = jnp.cos(angle)
        sine = jnp.sin(angle)
        first = lax.broadcasted_iota(jnp.int32, (step, width), 1) < width // 2
        sin_ref[rows] = jnp.where(first, -sine, sine)


def rotary_tables(lengths, count):
    frequency = THETA ** (-2.0 * np.arange(HEAD_DIM // 2) / HEAD_DIM)
    frequency = np.concatenate([frequency, frequency])[None].astype(np.float32)
    whole = pl.BlockSpec(memory_space=pltpu.VMEM)
    shape = jax.ShapeDtypeStruct((count, HEAD_DIM), jnp.float32)
    return pl.pallas_call(
        tables_kernel,
        out_shape=[shape] * 2,
        in_specs=[pl.BlockSpec(memory_space=pltpu.SMEM), whole],
        out_specs=[pl.BlockSpec((count, HEAD_DIM), lambda: (0, 0))] * 2,
        compiler_params=pltpu.CompilerParams(vmem_limit_bytes=63 * 2**20),
        name="rotary_tables",
    )(lengths, frequency)


def sort_kernel(member_ref, placement_ref, rows_ref, projection_ref, out_ref, mine_ref, theirs_ref, held, moved, columns, *sems):
    in_sems, out_sems, column_sems, head_sems = sems
    count, devices = held.shape[0], placement_ref.shape[1]
    piece = count // devices
    arriving, leaving = [], []
    for i in range(8):
        rows = pl.ds(i * (count // 8), count // 8)
        arriving.append(pltpu.make_async_copy(rows_ref.at[rows], held.at[rows], in_sems.at[i]))
        arriving[-1].start()
    taking = []
    for i, member in enumerate((member_ref[0], member_ref[0] ^ 2)):
        at, source = 0, 0
        for heads, width in ((KV_HEADS, GROUP * HEAD_DIM), (KV_HEADS, HEAD_DIM), (KV_HEADS, HEAD_DIM)):
            copy = pltpu.make_async_copy(
                projection_ref.at[:, pl.ds(pl.multiple_of(source + member * width, HEAD_DIM), width)],
                columns.at[i, :, pl.ds(at, width)],
                column_sems.at[len(taking)],
            )
            copy.start()
            taking.append(copy)
            at, source = at + width, source + heads * width

    device = lax.broadcasted_iota(jnp.int32, (devices, devices), 0)
    pieces = jnp.where(device == placement_ref[...], 1.0, 0.0).astype(jnp.bfloat16)
    down = lax.broadcasted_iota(jnp.int32, (count, devices), 0) // piece
    tall = jnp.where(down == lax.broadcasted_iota(jnp.int32, (count, devices), 1), 1.0, 0.0).astype(jnp.bfloat16)
    along = lax.broadcasted_iota(jnp.int32, (devices, count), 1) // piece
    wide = jnp.where(along == lax.broadcasted_iota(jnp.int32, (devices, count), 0), 1.0, 0.0).astype(jnp.bfloat16)
    tall = jnp.dot(tall, pieces, preferred_element_type=jnp.float32).astype(jnp.bfloat16)
    both = jnp.dot(tall, wide, preferred_element_type=jnp.float32)
    row = lax.broadcasted_iota(jnp.int32, (count, count), 0) % piece
    same = row == lax.broadcasted_iota(jnp.int32, (count, count), 1) % piece
    one_hot = jnp.where(same, both, 0.0).astype(jnp.bfloat16)

    for copy in taking:
        copy.wait()
    for i, out in enumerate((mine_ref, theirs_ref)):
        leaving.append(pltpu.make_async_copy(columns.at[i], out, head_sems.at[i]))
        leaving[-1].start()
    for copy in arriving:
        copy.wait()
    for i in range(2):
        half = slice(i * (count // 2), (i + 1) * (count // 2))
        moved[half] = jnp.dot(one_hot[half], held[...], preferred_element_type=jnp.float32).astype(jnp.bfloat16)
        for j in range(4):
            rows = pl.ds((i * 4 + j) * (count // 8), count // 8)
            leaving.append(pltpu.make_async_copy(moved.at[rows], out_ref.at[rows], out_sems.at[i * 4 + j]))
            leaving[-1].start()
    for copy in leaving:
        copy.wait()


def sort_rows(tokens, placement, projection, member):
    anywhere = pl.BlockSpec(memory_space=pl.ANY)
    columns = (projection.shape[0], (GROUP + 2) * HEAD_DIM)
    return pl.pallas_call(
        sort_kernel,
        out_shape=[jax.ShapeDtypeStruct(shape, tokens.dtype) for shape in (tokens.shape, columns, columns)],
        in_specs=[
            pl.BlockSpec(memory_space=pltpu.SMEM),
            pl.BlockSpec(memory_space=pltpu.VMEM),
            anywhere,
            anywhere,
        ],
        out_specs=[anywhere] * 3,
        scratch_shapes=[
            pltpu.VMEM(tokens.shape, tokens.dtype),
            pltpu.VMEM(tokens.shape, tokens.dtype),
            pltpu.VMEM((2,) + columns, tokens.dtype),
            pltpu.SemaphoreType.DMA((8,)),
            pltpu.SemaphoreType.DMA((8,)),
            pltpu.SemaphoreType.DMA((6,)),
            pltpu.SemaphoreType.DMA((2,)),
        ],
        compiler_params=pltpu.CompilerParams(vmem_limit_bytes=60 * 2**20),
        name="sort_rows",
    )(member.reshape(1), placement, tokens, projection)


def unsort_kernel(target_ref, rows_ref, out_ref):
    count = out_ref.shape[0]
    order = lax.broadcasted_iota(jnp.int32, (count, count), 1)
    one_hot = jnp.where(order == target_ref[...], 1.0, 0.0).astype(jnp.bfloat16)
    rows = rows_ref[...].reshape(count, out_ref.shape[1])
    out_ref[...] = jnp.dot(one_hot, rows, preferred_element_type=jnp.float32).astype(jnp.bfloat16)


def unsort_rows(returned, target):
    groups, blocks, rows, width = returned.shape
    count = groups * rows
    return pl.pallas_call(
        unsort_kernel,
        out_shape=jax.ShapeDtypeStruct((count, blocks * width), returned.dtype),
        grid=(blocks,),
        in_specs=[
            pl.BlockSpec((count, 1), lambda i: (0, 0)),
            pl.BlockSpec((groups, None, rows, width), lambda i: (0, i, 0, 0)),
        ],
        out_specs=pl.BlockSpec((count, width), lambda i: (0, i)),
        compiler_params=pltpu.CompilerParams(vmem_limit_bytes=32 * 2**20),
        name="unsort_rows",
    )(target.reshape(count, 1), returned)


def ring_blocks(block, axis):
    ways = [[(i, (i + d) % 4) for i in range(4)] for d in (1, 3, 2)]
    return jnp.concatenate([block] + [lax.ppermute(block, axis, way) for way in ways], axis=0)


UP, DOWN = [(i, (i + 1) % 4) for i in range(4)], [(i, (i + 3) % 4) for i in range(4)]


def spread(blocks):
    pairs = [(lax.ppermute(b, axis, UP), lax.ppermute(b, axis, DOWN)) for b, axis in zip(blocks, ("x", "y"))]
    half = blocks[0].shape[0] // 2
    halves = [h for below, above in pairs for h in (below[:half], above[half:])]
    far = [lax.ppermute(h, axis, way) for h, axis, way in zip(halves, ("x", "x", "y", "y"), (UP, DOWN, UP, DOWN))]
    return [[blocks[i], *pairs[i], *far[2 * i : 2 * i + 2]] for i in range(2)]


RING = (0, 3, 1, 2)
SPAN = ((0, (0, 1, 2, 3)), (3, (0, 1, 2, 3)), (1, (0, 1, 2, 3)), (2, (0, 1)), (2, (2, 3)))


def gather_weights(mine, theirs, rows):
    x, y, zh = lax.axis_index("x"), lax.axis_index("y"), lax.axis_index("zh")
    half = theirs.shape[1] // 2
    pieces = [mine]
    places = [(i * 2 + zh) * rows for i in range(16)]
    ready = lax.optimization_barrier([ring_blocks(theirs[:, :half], "y"), ring_blocks(theirs[:, half:], "x")])
    for side, spreads in enumerate(spread(ready)):
        pieces += spreads
        for outer, inners in SPAN:
            for inner in inners:
                near, far = (outer, RING[inner]) if side == 0 else (RING[inner], outer)
                places.append(((x + near) % 4 * 8 + (y + far) % 4 * 2 + 1 - zh) * rows)
    return jnp.stack(places), pieces


def project_kernel(parts, places_ref, *refs):
    row_refs, refs = refs[:parts], refs[parts:]
    pieces, out_refs, ordered = refs[: -parts - 1], refs[-parts - 1 : -1], refs[-1]
    half = out_refs[0].shape[1] // 2
    step = 128

    def take(first, count):
        for i in range(count):
            column = pl.multiple_of(places_ref[first + i], step)
            at = 0
            for rows in row_refs:
                ordered[at : at + rows.shape[0], i * step : (i + 1) * step] = rows[:, pl.ds(column, step)]
                at += rows.shape[0]

    def product(pieces):
        total, at = None, 0
        for piece in pieces:
            depth = piece.shape[0]
            term = jnp.dot(ordered[:, at : at + depth], piece[...], preferred_element_type=jnp.float32)
            total = term if total is None else total + term
            at += depth
        return total

    take(0, 16)
    out = product(pieces[:1])
    for side in range(2):
        take(16 + side * 16, 16)
        columns = slice(side * half, (side + 1) * half)
        here = (out[:, columns] + product(pieces[1 + side * 5 : 6 + side * 5])).astype(jnp.bfloat16)
        at = 0
        for out_ref in out_refs:
            out_ref[:, columns] = here[at : at + out_ref.shape[0]]
            at += out_ref.shape[0]


def project(places, pieces, rows):
    count, depth = sum(r.shape[0] for r in rows), rows[0].shape[1]
    width = pieces[0].shape[1]
    whole = pl.BlockSpec(memory_space=pltpu.VMEM)
    return pl.pallas_call(
        functools.partial(project_kernel, len(rows)),
        out_shape=[jax.ShapeDtypeStruct((r.shape[0], width), jnp.bfloat16) for r in rows],
        in_specs=[pl.BlockSpec(memory_space=pltpu.SMEM)] + [whole] * (len(rows) + len(pieces)),
        out_specs=[whole] * len(rows),
        scratch_shapes=[pltpu.VMEM((count, depth // 2), jnp.bfloat16)],
        compiler_params=pltpu.CompilerParams(vmem_limit_bytes=24 * 2**20),
        cost_estimate=pl.CostEstimate(
            flops=2 * count * depth * width, bytes_accessed=2 * depth * (width + count), transcendentals=0
        ),
        name="project",
    )(places, *rows, *pieces)


def attention_kernel(member_ref, lengths_ref, *refs):
    lanes = refs[:4]
    cos_ref, sin_ref, out_ref, queries, keys, values, mixed = refs[4:]
    count = cos_ref.shape[0]
    blocks = count // BLOCK
    part = BLOCK // blocks
    half = HEAD_DIM // 2
    member = member_ref[0]

    taken = lax.broadcasted_iota(jnp.int32, (BLOCK, BLOCK), 1)
    lane, rest = taken // part, taken % part
    group, slot, row = rest // (2 * blocks), (rest // 2) % blocks, rest % 2
    placed = slot * part + (group * 4 + (lane ^ member)) * 2 + row
    wanted = lax.broadcasted_iota(jnp.int32, (BLOCK, BLOCK), 0)
    forward = jnp.where(wanted == placed, 1.0, 0.0).astype(jnp.bfloat16)
    for h in range(blocks):
        chunk = jnp.concatenate([lane_ref[h * part : (h + 1) * part] for lane_ref in lanes], axis=0)
        chunk = jnp.dot(forward, chunk, preferred_element_type=jnp.float32)
        for s in range(blocks):
            rows = slice(s * BLOCK + h * part, s * BLOCK + (h + 1) * part)
            here = chunk[s * part : (s + 1) * part]
            cosine, sine = cos_ref[rows], sin_ref[rows]

            def rotate(x):
                return (x * cosine + pltpu.roll(x, half, 1) * sine).astype(jnp.bfloat16)

            for g in range(GROUP):
                queries[g, rows] = rotate(here[:, g * HEAD_DIM : (g + 1) * HEAD_DIM])
            keys[rows] = rotate(here[:, GROUP * HEAD_DIM : (GROUP + 1) * HEAD_DIM])
            values[rows] = here[:, (GROUP + 1) * HEAD_DIM :].astype(jnp.bfloat16)

    scale = HEAD_DIM ** (-0.5) * math.log2(math.e)
    tile = 128
    reach = (MOST - 1 + tile - 1) // tile
    for b in range(count // tile):
        first = max(0, b - reach)
        width = (b + 1 - first) * tile
        position = b * tile + lax.broadcasted_iota(jnp.int32, (tile, 1), 0)
        begin, end = jnp.zeros_like(position), jnp.int32(0)
        for j in range(lengths_ref.shape[1]):
            end = end + lengths_ref[0, j]
            begin = jnp.where(position >= end, end, begin)
        key_at = first * tile + lax.broadcasted_iota(jnp.int32, (tile, width), 1)
        allowed = (key_at >= begin) & (key_at <= position)
        key_block = keys[first * tile : (b + 1) * tile]
        value_block = values[first * tile : (b + 1) * tile]
        rows = slice(b * tile, (b + 1) * tile)
        stacked = jnp.concatenate([queries[g, rows] for g in range(GROUP)], axis=0)
        all_scores = lax.dot_general(
            stacked, key_block, (((1,), (1,)), ((), ())), preferred_element_type=jnp.float32
        )
        stacked_weights, totals = [], []
        for g in range(GROUP):
            scores = jnp.where(allowed, all_scores[g * tile : (g + 1) * tile], -1e30)
            weights = jnp.exp2((scores - jnp.max(scores, axis=1, keepdims=True)) * scale)
            totals.append(jnp.sum(weights, axis=1, keepdims=True))
            stacked_weights.append(weights.astype(jnp.bfloat16))
        weighted = jnp.dot(
            jnp.concatenate(stacked_weights, axis=0), value_block, preferred_element_type=jnp.float32
        )
        for g in range(GROUP):
            mixed[rows, g * HEAD_DIM : (g + 1) * HEAD_DIM] = (
                weighted[g * tile : (g + 1) * tile] / totals[g]
            ).astype(jnp.bfloat16)

    left = lax.broadcasted_iota(jnp.int32, (BLOCK, BLOCK), 0)
    source = ((left // 2) % blocks) * part + (left // (2 * blocks)) * 2 + left % 2
    backward = jnp.where(taken == source, 1.0, 0.0).astype(jnp.bfloat16)
    for h in range(blocks):
        chunk = jnp.concatenate(
            [mixed[s * BLOCK + h * part : s * BLOCK + (h + 1) * part] for s in range(blocks)], axis=0
        )
        out_ref[h * BLOCK : (h + 1) * BLOCK] = jnp.dot(
            backward, chunk, preferred_element_type=jnp.float32
        ).astype(jnp.bfloat16)


def attend(member, lengths, lanes, cosine, sine):
    count = cosine.shape[0]
    whole = pl.BlockSpec(memory_space=pltpu.VMEM)
    scalars = pl.BlockSpec(memory_space=pltpu.SMEM)
    return pl.pallas_call(
        attention_kernel,
        out_shape=jax.ShapeDtypeStruct((count, GROUP * HEAD_DIM), jnp.bfloat16),
        in_specs=[scalars, scalars] + [whole] * 6,
        out_specs=whole,
        scratch_shapes=[
            pltpu.VMEM((GROUP, count, HEAD_DIM), jnp.bfloat16),
            pltpu.VMEM((count, HEAD_DIM), jnp.bfloat16),
            pltpu.VMEM((count, HEAD_DIM), jnp.bfloat16),
            pltpu.VMEM((count, GROUP * HEAD_DIM), jnp.bfloat16),
        ],
        compiler_params=pltpu.CompilerParams(vmem_limit_bytes=24 * 2**20),
        name="attend",
    )(member, lengths, *lanes, cosine, sine)


def on_device(tokens, projection, placement, doc_lengths):
    row_count, width = tokens.shape
    devices = placement.shape[1]
    members = lax.axis_size(CTX)
    groups = devices // members
    piece = row_count // devices
    member = lax.axis_index(CTX)

    outgoing, mine, theirs = sort_rows(tokens, placement, projection, member)
    outgoing = outgoing.reshape(groups, row_count // groups, width)
    mine = lax.all_gather(mine, ("x", "y"), axis=0, tiled=True)
    theirs = lax.ppermute(theirs, ("zh", "zl"), [(0, 3), (3, 0), (1, 2), (2, 1)])
    target = (placement[0][:, None] * piece + jnp.arange(piece, dtype=jnp.int32)[None, :]).reshape(row_count)
    arrived = lax.all_to_all(outgoing, DP, 0, 0, tiled=True).reshape(row_count, width)
    tables = rotary_tables(doc_lengths, members * row_count)
    arrived, theirs, tables = lax.optimization_barrier((arrived, theirs, tables))
    places, pieces = gather_weights(mine, theirs, projection.shape[0])
    across = [(0, 1), (1, 0)]
    far = lax.ppermute(arrived, "zl", across)
    near = lax.ppermute(arrived, "core", across)
    lanes = project(places, pieces, [arrived, near])
    far, lanes = lax.optimization_barrier((far, lanes))
    last = lax.ppermute(far, "core", across)
    lanes = lanes + project(places, pieces, [far]) + project(places, pieces, [last])
    mixed = attend(member.reshape(1), doc_lengths, lanes, *tables)
    returned = lax.all_to_all(
        mixed.reshape(devices, members * piece, GROUP * HEAD_DIM), EVERY, 0, 0, tiled=True
    )
    return unsort_rows(returned.reshape(groups, members, members * piece, GROUP * HEAD_DIM), target)


def solution(mesh):
    sizes = {"x": 4, "y": 4, "zh": 2, "zl": 2, "core": 2}
    fine = Mesh(mesh.devices.reshape(tuple(sizes.values())), tuple(sizes))
    return jax.shard_map(
        on_device,
        mesh=fine,
        in_specs=(P(EVERY, None), P(DP, None), P(EVERY, None), P(DP, None)),
        out_specs=P(EVERY, None),
        check_vma=False,
    )
```

```python
import functools
import math

import jax
import jax.numpy as jnp
import numpy as np
from jax import lax
from jax.experimental import pallas as pl
from jax.experimental.pallas import tpu as pltpu
from jax.sharding import Mesh, PartitionSpec as P

HEAD_DIM = 128
HEADS = 16
KV_HEADS = 4
GROUP = HEADS // KV_HEADS
THETA = 500000.0
MOST = 512
DP = ("x", "y", "zh")
CTX = ("zl", "core")
EVERY = DP + CTX
BLOCK = 256


def tables_kernel(lengths_ref, frequency_ref, cos_ref, sin_ref):
    count, width = cos_ref.shape
    step = 128

    @pl.loop(0, count // step)
    def _(i):
        position = i * step + lax.broadcasted_iota(jnp.int32, (step, width), 0)
        begin, end = jnp.zeros_like(position), jnp.int32(0)
        for j in range(lengths_ref.shape[1]):
            end = end + lengths_ref[0, j]
            begin = jnp.where(position >= end, end, begin)
        angle = (position - begin).astype(jnp.float32) * frequency_ref[...]
        rows = pl.ds(pl.multiple_of(i * step, step), step)
        cos_ref[rows] = jnp.cos(angle)
        sine = jnp.sin(angle)
        first = lax.broadcasted_iota(jnp.int32, (step, width), 1) < width // 2
        sin_ref[rows] = jnp.where(first, -sine, sine)


def rotary_tables(lengths, count):
    frequency = THETA ** (-2.0 * np.arange(HEAD_DIM // 2) / HEAD_DIM)
    frequency = np.concatenate([frequency, frequency])[None].astype(np.float32)
    whole = pl.BlockSpec(memory_space=pltpu.VMEM)
    shape = jax.ShapeDtypeStruct((count, HEAD_DIM), jnp.float32)
    return pl.pallas_call(
        tables_kernel,
        out_shape=[shape] * 2,
        in_specs=[pl.BlockSpec(memory_space=pltpu.SMEM), whole],
        out_specs=[pl.BlockSpec((count, HEAD_DIM), lambda: (0, 0))] * 2,
        compiler_params=pltpu.CompilerParams(vmem_limit_bytes=63 * 2**20),
        name="rotary_tables",
    )(lengths, frequency)


def sort_kernel(member_ref, placement_ref, rows_ref, projection_ref, out_ref, mine_ref, theirs_ref, held, moved, columns, *sems):
    in_sems, out_sems, column_sems, head_sems = sems
    count, devices = held.shape[0], placement_ref.shape[1]
    piece = count // devices
    arriving, leaving = [], []
    parts = [
        (pl.ds(half * (count // 2), count // 2), pl.ds(block * (held.shape[1] // 4), held.shape[1] // 4))
        for block in range(4)
        for half in range(2)
    ]
    for i, part in enumerate(parts):
        arriving.append(pltpu.make_async_copy(rows_ref.at[part], held.at[part], in_sems.at[i]))
        arriving[-1].start()
    taking = []
    for i, member in enumerate((member_ref[0], member_ref[0] ^ 2)):
        at, source = 0, 0
        for heads, width in ((KV_HEADS, GROUP * HEAD_DIM), (KV_HEADS, HEAD_DIM), (KV_HEADS, HEAD_DIM)):
            copy = pltpu.make_async_copy(
                projection_ref.at[:, pl.ds(pl.multiple_of(source + member * width, HEAD_DIM), width)],
                columns.at[i, :, pl.ds(at, width)],
                column_sems.at[len(taking)],
            )
            copy.start()
            taking.append(copy)
            at, source = at + width, source + heads * width

    device = lax.broadcasted_iota(jnp.int32, (devices, devices), 0)
    pieces = jnp.where(device == placement_ref[...], 1.0, 0.0).astype(jnp.bfloat16)
    down = lax.broadcasted_iota(jnp.int32, (count, devices), 0) // piece
    tall = jnp.where(down == lax.broadcasted_iota(jnp.int32, (count, devices), 1), 1.0, 0.0).astype(jnp.bfloat16)
    along = lax.broadcasted_iota(jnp.int32, (devices, count), 1) // piece
    wide = jnp.where(along == lax.broadcasted_iota(jnp.int32, (devices, count), 0), 1.0, 0.0).astype(jnp.bfloat16)
    tall = jnp.dot(tall, pieces, preferred_element_type=jnp.float32).astype(jnp.bfloat16)
    both = jnp.dot(tall, wide, preferred_element_type=jnp.float32)
    row = lax.broadcasted_iota(jnp.int32, (count, count), 0) % piece
    same = row == lax.broadcasted_iota(jnp.int32, (count, count), 1) % piece
    one_hot = jnp.where(same, both, 0.0).astype(jnp.bfloat16)

    for copy in taking:
        copy.wait()
    for i, out in enumerate((mine_ref, theirs_ref)):
        leaving.append(pltpu.make_async_copy(columns.at[i], out, head_sems.at[i]))
        leaving[-1].start()
    for block in range(4):
        columns_here = parts[2 * block][1]
        for copy in arriving[2 * block : 2 * block + 2]:
            copy.wait()
        moved[:, columns_here] = jnp.dot(
            one_hot, held[:, columns_here], preferred_element_type=jnp.float32
        ).astype(jnp.bfloat16)
        for i in (2 * block, 2 * block + 1):
            leaving.append(pltpu.make_async_copy(moved.at[parts[i]], out_ref.at[parts[i]], out_sems.at[i]))
            leaving[-1].start()
    for copy in leaving:
        copy.wait()


def sort_rows(tokens, placement, projection, member):
    anywhere = pl.BlockSpec(memory_space=pl.ANY)
    columns = (projection.shape[0], (GROUP + 2) * HEAD_DIM)
    return pl.pallas_call(
        sort_kernel,
        out_shape=[jax.ShapeDtypeStruct(shape, tokens.dtype) for shape in (tokens.shape, columns, columns)],
        in_specs=[
            pl.BlockSpec(memory_space=pltpu.SMEM),
            pl.BlockSpec(memory_space=pltpu.VMEM),
            anywhere,
            anywhere,
        ],
        out_specs=[anywhere] * 3,
        scratch_shapes=[
            pltpu.VMEM(tokens.shape, tokens.dtype),
            pltpu.VMEM(tokens.shape, tokens.dtype),
            pltpu.VMEM((2,) + columns, tokens.dtype),
            pltpu.SemaphoreType.DMA((8,)),
            pltpu.SemaphoreType.DMA((8,)),
            pltpu.SemaphoreType.DMA((6,)),
            pltpu.SemaphoreType.DMA((2,)),
        ],
        compiler_params=pltpu.CompilerParams(vmem_limit_bytes=60 * 2**20),
        name="sort_rows",
    )(member.reshape(1), placement, tokens, projection)


def unsort_kernel(target_ref, rows_ref, out_ref):
    count = out_ref.shape[0]
    order = lax.broadcasted_iota(jnp.int32, (count, count), 1)
    one_hot = jnp.where(order == target_ref[...], 1.0, 0.0).astype(jnp.bfloat16)
    rows = rows_ref[...].reshape(count, out_ref.shape[1])
    out_ref[...] = jnp.dot(one_hot, rows, preferred_element_type=jnp.float32).astype(jnp.bfloat16)


def unsort_rows(returned, target):
    groups, blocks, rows, width = returned.shape
    count = groups * rows
    return pl.pallas_call(
        unsort_kernel,
        out_shape=jax.ShapeDtypeStruct((count, blocks * width), returned.dtype),
        grid=(blocks,),
        in_specs=[
            pl.BlockSpec((count, 1), lambda i: (0, 0)),
            pl.BlockSpec((groups, None, rows, width), lambda i: (0, i, 0, 0)),
        ],
        out_specs=pl.BlockSpec((count, width), lambda i: (0, i)),
        compiler_params=pltpu.CompilerParams(vmem_limit_bytes=32 * 2**20),
        name="unsort_rows",
    )(target.reshape(count, 1), returned)


def ring_blocks(block, axis):
    ways = [[(i, (i + d) % 4) for i in range(4)] for d in (1, 3, 2)]
    return jnp.concatenate([block] + [lax.ppermute(block, axis, way) for way in ways], axis=0)


UP, DOWN = [(i, (i + 1) % 4) for i in range(4)], [(i, (i + 3) % 4) for i in range(4)]


def spread(blocks):
    pairs = [(lax.ppermute(b, axis, UP), lax.ppermute(b, axis, DOWN)) for b, axis in zip(blocks, ("x", "y"))]
    half = blocks[0].shape[0] // 2
    halves = [h for below, above in pairs for h in (below[:half], above[half:])]
    far = [lax.ppermute(h, axis, way) for h, axis, way in zip(halves, ("x", "x", "y", "y"), (UP, DOWN, UP, DOWN))]
    return [[blocks[i], *pairs[i], *far[2 * i : 2 * i + 2]] for i in range(2)]


RING = (0, 3, 1, 2)
SPAN = ((0, (0, 1, 2, 3)), (3, (0, 1, 2, 3)), (1, (0, 1, 2, 3)), (2, (0, 1)), (2, (2, 3)))


def gather_weights(mine, theirs, rows):
    x, y, zh = lax.axis_index("x"), lax.axis_index("y"), lax.axis_index("zh")
    half = theirs.shape[1] // 2
    pieces = [mine]
    places = [(i * 2 + zh) * rows for i in range(16)]
    ready = lax.optimization_barrier([ring_blocks(theirs[:, :half], "y"), ring_blocks(theirs[:, half:], "x")])
    for side, spreads in enumerate(spread(ready)):
        pieces += spreads
        for outer, inners in SPAN:
            for inner in inners:
                near, far = (outer, RING[inner]) if side == 0 else (RING[inner], outer)
                places.append(((x + near) % 4 * 8 + (y + far) % 4 * 2 + 1 - zh) * rows)
    return jnp.stack(places), pieces


def project_kernel(parts, places_ref, *refs):
    row_refs, refs = refs[:parts], refs[parts:]
    pieces, out_refs, ordered = refs[: -parts - 1], refs[-parts - 1 : -1], refs[-1]
    half = out_refs[0].shape[1] // 2
    step = 128

    def take(first, count):
        for i in range(count):
            column = pl.multiple_of(places_ref[first + i], step)
            at = 0
            for rows in row_refs:
                ordered[at : at + rows.shape[0], i * step : (i + 1) * step] = rows[:, pl.ds(column, step)]
                at += rows.shape[0]

    def product(pieces):
        total, at = None, 0
        for piece in pieces:
            depth = piece.shape[0]
            term = jnp.dot(ordered[:, at : at + depth], piece[...], preferred_element_type=jnp.float32)
            total = term if total is None else total + term
            at += depth
        return total

    take(0, 16)
    out = product(pieces[:1])
    for side in range(2):
        take(16 + side * 16, 16)
        columns = slice(side * half, (side + 1) * half)
        here = (out[:, columns] + product(pieces[1 + side * 5 : 6 + side * 5])).astype(jnp.bfloat16)
        at = 0
        for out_ref in out_refs:
            out_ref[:, columns] = here[at : at + out_ref.shape[0]]
            at += out_ref.shape[0]


def project(places, pieces, rows):
    count, depth = sum(r.shape[0] for r in rows), rows[0].shape[1]
    width = pieces[0].shape[1]
    whole = pl.BlockSpec(memory_space=pltpu.VMEM)
    return pl.pallas_call(
        functools.partial(project_kernel, len(rows)),
        out_shape=[jax.ShapeDtypeStruct((r.shape[0], width), jnp.bfloat16) for r in rows],
        in_specs=[pl.BlockSpec(memory_space=pltpu.SMEM)] + [whole] * (len(rows) + len(pieces)),
        out_specs=[whole] * len(rows),
        scratch_shapes=[pltpu.VMEM((count, depth // 2), jnp.bfloat16)],
        compiler_params=pltpu.CompilerParams(vmem_limit_bytes=24 * 2**20),
        cost_estimate=pl.CostEstimate(
            flops=2 * count * depth * width, bytes_accessed=2 * depth * (width + count), transcendentals=0
        ),
        name="project",
    )(places, *rows, *pieces)


def attention_kernel(member_ref, lengths_ref, *refs):
    lanes = refs[:4]
    cos_ref, sin_ref, out_ref, queries, keys, values, mixed = refs[4:]
    count = cos_ref.shape[0]
    blocks = count // BLOCK
    part = BLOCK // blocks
    half = HEAD_DIM // 2
    member = member_ref[0]

    taken = lax.broadcasted_iota(jnp.int32, (BLOCK, BLOCK), 1)
    lane, rest = taken // part, taken % part
    group, slot, row = rest // (2 * blocks), (rest // 2) % blocks, rest % 2
    placed = slot * part + (group * 4 + (lane ^ member)) * 2 + row
    wanted = lax.broadcasted_iota(jnp.int32, (BLOCK, BLOCK), 0)
    forward = jnp.where(wanted == placed, 1.0, 0.0).astype(jnp.bfloat16)
    for h in range(blocks):
        chunk = jnp.concatenate([lane_ref[h * part : (h + 1) * part] for lane_ref in lanes], axis=0)
        chunk = jnp.dot(forward, chunk, preferred_element_type=jnp.float32)
        for s in range(blocks):
            rows = slice(s * BLOCK + h * part, s * BLOCK + (h + 1) * part)
            here = chunk[s * part : (s + 1) * part]
            cosine, sine = cos_ref[rows], sin_ref[rows]

            def rotate(x):
                return (x * cosine + pltpu.roll(x, half, 1) * sine).astype(jnp.bfloat16)

            for g in range(GROUP):
                queries[g, rows] = rotate(here[:, g * HEAD_DIM : (g + 1) * HEAD_DIM])
            keys[rows] = rotate(here[:, GROUP * HEAD_DIM : (GROUP + 1) * HEAD_DIM])
            values[rows] = here[:, (GROUP + 1) * HEAD_DIM :].astype(jnp.bfloat16)

    scale = HEAD_DIM ** (-0.5) * math.log2(math.e)
    tile = 128
    reach = (MOST - 1 + tile - 1) // tile
    for b in range(count // tile):
        first = max(0, b - reach)
        width = (b + 1 - first) * tile
        position = b * tile + lax.broadcasted_iota(jnp.int32, (tile, 1), 0)
        begin, end = jnp.zeros_like(position), jnp.int32(0)
        for j in range(lengths_ref.shape[1]):
            end = end + lengths_ref[0, j]
            begin = jnp.where(position >= end, end, begin)
        key_at = first * tile + lax.broadcasted_iota(jnp.int32, (tile, width), 1)
        allowed = (key_at >= begin) & (key_at <= position)
        key_block = keys[first * tile : (b + 1) * tile]
        value_block = values[first * tile : (b + 1) * tile]
        rows = slice(b * tile, (b + 1) * tile)
        stacked = jnp.concatenate([queries[g, rows] for g in range(GROUP)], axis=0)
        all_scores = lax.dot_general(
            stacked, key_block, (((1,), (1,)), ((), ())), preferred_element_type=jnp.float32
        )
        stacked_weights, totals = [], []
        for g in range(GROUP):
            scores = jnp.where(allowed, all_scores[g * tile : (g + 1) * tile], -1e30)
            weights = jnp.exp2((scores - jnp.max(scores, axis=1, keepdims=True)) * scale)
            totals.append(jnp.sum(weights, axis=1, keepdims=True))
            stacked_weights.append(weights.astype(jnp.bfloat16))
        weighted = jnp.dot(
            jnp.concatenate(stacked_weights, axis=0), value_block, preferred_element_type=jnp.float32
        )
        for g in range(GROUP):
            mixed[rows, g * HEAD_DIM : (g + 1) * HEAD_DIM] = (
                weighted[g * tile : (g + 1) * tile] / totals[g]
            ).astype(jnp.bfloat16)

    left = lax.broadcasted_iota(jnp.int32, (BLOCK, BLOCK), 0)
    source = ((left // 2) % blocks) * part + (left // (2 * blocks)) * 2 + left % 2
    backward = jnp.where(taken == source, 1.0, 0.0).astype(jnp.bfloat16)
    for h in range(blocks):
        chunk = jnp.concatenate(
            [mixed[s * BLOCK + h * part : s * BLOCK + (h + 1) * part] for s in range(blocks)], axis=0
        )
        out_ref[h * BLOCK : (h + 1) * BLOCK] = jnp.dot(
            backward, chunk, preferred_element_type=jnp.float32
        ).astype(jnp.bfloat16)


def attend(member, lengths, lanes, cosine, sine):
    count = cosine.shape[0]
    whole = pl.BlockSpec(memory_space=pltpu.VMEM)
    scalars = pl.BlockSpec(memory_space=pltpu.SMEM)
    return pl.pallas_call(
        attention_kernel,
        out_shape=jax.ShapeDtypeStruct((count, GROUP * HEAD_DIM), jnp.bfloat16),
        in_specs=[scalars, scalars] + [whole] * 6,
        out_specs=whole,
        scratch_shapes=[
            pltpu.VMEM((GROUP, count, HEAD_DIM), jnp.bfloat16),
            pltpu.VMEM((count, HEAD_DIM), jnp.bfloat16),
            pltpu.VMEM((count, HEAD_DIM), jnp.bfloat16),
            pltpu.VMEM((count, GROUP * HEAD_DIM), jnp.bfloat16),
        ],
        compiler_params=pltpu.CompilerParams(vmem_limit_bytes=24 * 2**20),
        name="attend",
    )(member, lengths, *lanes, cosine, sine)


def on_device(tokens, projection, placement, doc_lengths):
    row_count, width = tokens.shape
    devices = placement.shape[1]
    members = lax.axis_size(CTX)
    groups = devices // members
    piece = row_count // devices
    member = lax.axis_index(CTX)

    outgoing, mine, theirs = sort_rows(tokens, placement, projection, member)
    outgoing = outgoing.reshape(groups, row_count // groups, width)
    mine = lax.all_gather(mine, ("x", "y"), axis=0, tiled=True)
    theirs = lax.ppermute(theirs, ("zh", "zl"), [(0, 3), (3, 0), (1, 2), (2, 1)])
    target = (placement[0][:, None] * piece + jnp.arange(piece, dtype=jnp.int32)[None, :]).reshape(row_count)
    arrived = lax.all_to_all(outgoing, DP, 0, 0, tiled=True).reshape(row_count, width)
    tables = rotary_tables(doc_lengths, members * row_count)
    arrived, theirs, tables = lax.optimization_barrier((arrived, theirs, tables))
    places, pieces = gather_weights(mine, theirs, projection.shape[0])
    across = [(0, 1), (1, 0)]
    far = lax.ppermute(arrived, "zl", across)
    near = lax.ppermute(arrived, "core", across)
    lanes = project(places, pieces, [arrived])
    far, lanes = lax.optimization_barrier((far, lanes))
    last = lax.ppermute(far, "core", across)
    lanes = lanes + project(places, pieces, [near, far]) + project(places, pieces, [last])
    mixed = attend(member.reshape(1), doc_lengths, lanes, *tables)
    returned = lax.all_to_all(
        mixed.reshape(devices, members * piece, GROUP * HEAD_DIM), EVERY, 0, 0, tiled=True
    )
    return unsort_rows(returned.reshape(groups, members, members * piece, GROUP * HEAD_DIM), target)


def solution(mesh):
    sizes = {"x": 4, "y": 4, "zh": 2, "zl": 2, "core": 2}
    fine = Mesh(mesh.devices.reshape(tuple(sizes.values())), tuple(sizes))
    return jax.shard_map(
        on_device,
        mesh=fine,
        in_specs=(P(EVERY, None), P(DP, None), P(EVERY, None), P(DP, None)),
        out_specs=P(EVERY, None),
        check_vma=False,
    )
```

```python
import functools
import math

import jax
import jax.numpy as jnp
import numpy as np
from jax import lax
from jax.experimental import pallas as pl
from jax.experimental.pallas import tpu as pltpu
from jax.sharding import Mesh, PartitionSpec as P

HEAD_DIM = 128
HEADS = 16
KV_HEADS = 4
GROUP = HEADS // KV_HEADS
THETA = 500000.0
MOST = 512
DP = ("x", "y", "zh")
CTX = ("zl", "core")
EVERY = DP + CTX
BLOCK = 256


def tables_kernel(lengths_ref, frequency_ref, cos_ref, sin_ref):
    count, width = cos_ref.shape
    step = 128

    @pl.loop(0, count // step)
    def _(i):
        position = i * step + lax.broadcasted_iota(jnp.int32, (step, width), 0)
        begin, end = jnp.zeros_like(position), jnp.int32(0)
        for j in range(lengths_ref.shape[1]):
            end = end + lengths_ref[0, j]
            begin = jnp.where(position >= end, end, begin)
        angle = (position - begin).astype(jnp.float32) * frequency_ref[...]
        rows = pl.ds(pl.multiple_of(i * step, step), step)
        cos_ref[rows] = jnp.cos(angle)
        sine = jnp.sin(angle)
        first = lax.broadcasted_iota(jnp.int32, (step, width), 1) < width // 2
        sin_ref[rows] = jnp.where(first, -sine, sine)


def rotary_tables(lengths, count):
    frequency = THETA ** (-2.0 * np.arange(HEAD_DIM // 2) / HEAD_DIM)
    frequency = np.concatenate([frequency, frequency])[None].astype(np.float32)
    whole = pl.BlockSpec(memory_space=pltpu.VMEM)
    shape = jax.ShapeDtypeStruct((count, HEAD_DIM), jnp.float32)
    return pl.pallas_call(
        tables_kernel,
        out_shape=[shape] * 2,
        in_specs=[pl.BlockSpec(memory_space=pltpu.SMEM), whole],
        out_specs=[pl.BlockSpec((count, HEAD_DIM), lambda: (0, 0))] * 2,
        compiler_params=pltpu.CompilerParams(vmem_limit_bytes=63 * 2**20),
        name="rotary_tables",
    )(lengths, frequency)


def sort_kernel(member_ref, placement_ref, rows_ref, projection_ref, out_ref, mine_ref, theirs_ref, held, moved, columns, *sems):
    in_sems, out_sems, column_sems, head_sems = sems
    count, devices = held.shape[0], placement_ref.shape[1]
    piece = count // devices
    arriving, leaving = [], []
    parts = [
        (pl.ds(half * (count // 2), count // 2), pl.ds(block * (held.shape[1] // 4), held.shape[1] // 4))
        for block in range(4)
        for half in range(2)
    ]
    for i, part in enumerate(parts):
        arriving.append(pltpu.make_async_copy(rows_ref.at[part], held.at[part], in_sems.at[i]))
        arriving[-1].start()
    taking = []
    for i, member in enumerate((member_ref[0], member_ref[0] ^ 2)):
        at, source = 0, 0
        for heads, width in ((KV_HEADS, GROUP * HEAD_DIM), (KV_HEADS, HEAD_DIM), (KV_HEADS, HEAD_DIM)):
            copy = pltpu.make_async_copy(
                projection_ref.at[:, pl.ds(pl.multiple_of(source + member * width, HEAD_DIM), width)],
                columns.at[i, :, pl.ds(at, width)],
                column_sems.at[len(taking)],
            )
            copy.start()
            taking.append(copy)
            at, source = at + width, source + heads * width

    device = lax.broadcasted_iota(jnp.int32, (devices, devices), 0)
    pieces = jnp.where(device == placement_ref[...], 1.0, 0.0).astype(jnp.bfloat16)
    down = lax.broadcasted_iota(jnp.int32, (count, devices), 0) // piece
    tall = jnp.where(down == lax.broadcasted_iota(jnp.int32, (count, devices), 1), 1.0, 0.0).astype(jnp.bfloat16)
    along = lax.broadcasted_iota(jnp.int32, (devices, count), 1) // piece
    wide = jnp.where(along == lax.broadcasted_iota(jnp.int32, (devices, count), 0), 1.0, 0.0).astype(jnp.bfloat16)
    tall = jnp.dot(tall, pieces, preferred_element_type=jnp.float32).astype(jnp.bfloat16)
    both = jnp.dot(tall, wide, preferred_element_type=jnp.float32)
    row = lax.broadcasted_iota(jnp.int32, (count, count), 0) % piece
    same = row == lax.broadcasted_iota(jnp.int32, (count, count), 1) % piece
    one_hot = jnp.where(same, both, 0.0).astype(jnp.bfloat16)

    for block in range(4):
        columns_here = parts[2 * block][1]
        for copy in arriving[2 * block : 2 * block + 2]:
            copy.wait()
        moved[:, columns_here] = jnp.dot(
            one_hot, held[:, columns_here], preferred_element_type=jnp.float32
        ).astype(jnp.bfloat16)
        for i in (2 * block, 2 * block + 1):
            leaving.append(pltpu.make_async_copy(moved.at[parts[i]], out_ref.at[parts[i]], out_sems.at[i]))
            leaving[-1].start()
    for copy in taking:
        copy.wait()
    for i, out in enumerate((mine_ref, theirs_ref)):
        leaving.append(pltpu.make_async_copy(columns.at[i], out, head_sems.at[i]))
        leaving[-1].start()
    for copy in leaving:
        copy.wait()


def sort_rows(tokens, placement, projection, member):
    anywhere = pl.BlockSpec(memory_space=pl.ANY)
    columns = (projection.shape[0], (GROUP + 2) * HEAD_DIM)
    return pl.pallas_call(
        sort_kernel,
        out_shape=[jax.ShapeDtypeStruct(shape, tokens.dtype) for shape in (tokens.shape, columns, columns)],
        in_specs=[
            pl.BlockSpec(memory_space=pltpu.SMEM),
            pl.BlockSpec(memory_space=pltpu.VMEM),
            anywhere,
            anywhere,
        ],
        out_specs=[anywhere] * 3,
        scratch_shapes=[
            pltpu.VMEM(tokens.shape, tokens.dtype),
            pltpu.VMEM(tokens.shape, tokens.dtype),
            pltpu.VMEM((2,) + columns, tokens.dtype),
            pltpu.SemaphoreType.DMA((8,)),
            pltpu.SemaphoreType.DMA((8,)),
            pltpu.SemaphoreType.DMA((6,)),
            pltpu.SemaphoreType.DMA((2,)),
        ],
        compiler_params=pltpu.CompilerParams(vmem_limit_bytes=60 * 2**20),
        name="sort_rows",
    )(member.reshape(1), placement, tokens, projection)


def unsort_kernel(target_ref, rows_ref, out_ref):
    count = out_ref.shape[0]
    blocks, width = rows_ref.shape[1], rows_ref.shape[3]
    order = lax.broadcasted_iota(jnp.int32, (count, count), 1)
    one_hot = jnp.where(order == target_ref[...], 1.0, 0.0).astype(jnp.bfloat16)
    for i in range(blocks):
        rows = rows_ref[:, i].reshape(count, width)
        out_ref[:, i * width : (i + 1) * width] = jnp.dot(
            one_hot, rows, preferred_element_type=jnp.float32
        ).astype(jnp.bfloat16)


def unsort_rows(returned, target):
    groups, blocks, rows, width = returned.shape
    count = groups * rows
    whole = pl.BlockSpec(memory_space=pltpu.VMEM)
    return pl.pallas_call(
        unsort_kernel,
        out_shape=jax.ShapeDtypeStruct((count, blocks * width), returned.dtype),
        in_specs=[whole, whole],
        out_specs=pl.BlockSpec((count, blocks * width), lambda: (0, 0)),
        compiler_params=pltpu.CompilerParams(vmem_limit_bytes=16 * 2**20),
        name="unsort_rows",
    )(target.reshape(count, 1), returned)


def ring_blocks(block, axis):
    ways = [[(i, (i + d) % 4) for i in range(4)] for d in (1, 3, 2)]
    return jnp.concatenate([block] + [lax.ppermute(block, axis, way) for way in ways], axis=0)


UP, DOWN = [(i, (i + 1) % 4) for i in range(4)], [(i, (i + 3) % 4) for i in range(4)]


def spread(blocks):
    pairs = [(lax.ppermute(b, axis, UP), lax.ppermute(b, axis, DOWN)) for b, axis in zip(blocks, ("x", "y"))]
    half = blocks[0].shape[0] // 2
    halves = [h for below, above in pairs for h in (below[:half], above[half:])]
    far = [lax.ppermute(h, axis, way) for h, axis, way in zip(halves, ("x", "x", "y", "y"), (UP, DOWN, UP, DOWN))]
    return [[blocks[i], *pairs[i], *far[2 * i : 2 * i + 2]] for i in range(2)]


RING = (0, 3, 1, 2)
SPAN = ((0, (0, 1, 2, 3)), (3, (0, 1, 2, 3)), (1, (0, 1, 2, 3)), (2, (0, 1)), (2, (2, 3)))


def gather_weights(mine, theirs, rows):
    x, y, zh = lax.axis_index("x"), lax.axis_index("y"), lax.axis_index("zh")
    half = theirs.shape[1] // 2
    pieces = [mine]
    places = [(i * 2 + zh) * rows for i in range(16)]
    ready = lax.optimization_barrier([ring_blocks(theirs[:, :half], "y"), ring_blocks(theirs[:, half:], "x")])
    for side, spreads in enumerate(spread(ready)):
        pieces += spreads
        for outer, inners in SPAN:
            for inner in inners:
                near, far = (outer, RING[inner]) if side == 0 else (RING[inner], outer)
                places.append(((x + near) % 4 * 8 + (y + far) % 4 * 2 + 1 - zh) * rows)
    return jnp.stack(places), pieces


def project_kernel(parts, places_ref, *refs):
    row_refs, refs = refs[:parts], refs[parts:]
    pieces, out_refs, ordered = refs[: -parts - 1], refs[-parts - 1 : -1], refs[-1]
    half = out_refs[0].shape[1] // 2
    step = 128

    def take(first, count):
        for i in range(count):
            column = pl.multiple_of(places_ref[first + i], step)
            at = 0
            for rows in row_refs:
                ordered[at : at + rows.shape[0], i * step : (i + 1) * step] = rows[:, pl.ds(column, step)]
                at += rows.shape[0]

    def product(pieces):
        total, at = None, 0
        for piece in pieces:
            depth = piece.shape[0]
            term = jnp.dot(ordered[:, at : at + depth], piece[...], preferred_element_type=jnp.float32)
            total = term if total is None else total + term
            at += depth
        return total

    take(0, 16)
    out = product(pieces[:1])
    for side in range(2):
        take(16 + side * 16, 16)
        columns = slice(side * half, (side + 1) * half)
        here = (out[:, columns] + product(pieces[1 + side * 5 : 6 + side * 5])).astype(jnp.bfloat16)
        at = 0
        for out_ref in out_refs:
            out_ref[:, columns] = here[at : at + out_ref.shape[0]]
            at += out_ref.shape[0]


def project(places, pieces, rows):
    count, depth = sum(r.shape[0] for r in rows), rows[0].shape[1]
    width = pieces[0].shape[1]
    whole = pl.BlockSpec(memory_space=pltpu.VMEM)
    return pl.pallas_call(
        functools.partial(project_kernel, len(rows)),
        out_shape=[jax.ShapeDtypeStruct((r.shape[0], width), jnp.bfloat16) for r in rows],
        in_specs=[pl.BlockSpec(memory_space=pltpu.SMEM)] + [whole] * (len(rows) + len(pieces)),
        out_specs=[whole] * len(rows),
        scratch_shapes=[pltpu.VMEM((count, depth // 2), jnp.bfloat16)],
        compiler_params=pltpu.CompilerParams(vmem_limit_bytes=24 * 2**20),
        cost_estimate=pl.CostEstimate(
            flops=2 * count * depth * width, bytes_accessed=2 * depth * (width + count), transcendentals=0
        ),
        name="project",
    )(places, *rows, *pieces)


def attention_kernel(member_ref, lengths_ref, *refs):
    lanes = refs[:4]
    cos_ref, sin_ref, out_ref, queries, keys, values, mixed = refs[4:]
    count = cos_ref.shape[0]
    blocks = count // BLOCK
    part = BLOCK // blocks
    half = HEAD_DIM // 2
    member = member_ref[0]

    taken = lax.broadcasted_iota(jnp.int32, (BLOCK, BLOCK), 1)
    lane, rest = taken // part, taken % part
    group, slot, row = rest // (2 * blocks), (rest // 2) % blocks, rest % 2
    placed = slot * part + (group * 4 + (lane ^ member)) * 2 + row
    wanted = lax.broadcasted_iota(jnp.int32, (BLOCK, BLOCK), 0)
    forward = jnp.where(wanted == placed, 1.0, 0.0).astype(jnp.bfloat16)
    for h in range(blocks):
        chunk = jnp.concatenate([lane_ref[h * part : (h + 1) * part] for lane_ref in lanes], axis=0)
        chunk = jnp.dot(forward, chunk, preferred_element_type=jnp.float32)
        for s in range(blocks):
            rows = slice(s * BLOCK + h * part, s * BLOCK + (h + 1) * part)
            here = chunk[s * part : (s + 1) * part]
            cosine, sine = cos_ref[rows], sin_ref[rows]

            def rotate(x):
                return (x * cosine + pltpu.roll(x, half, 1) * sine).astype(jnp.bfloat16)

            for g in range(GROUP):
                queries[g, rows] = rotate(here[:, g * HEAD_DIM : (g + 1) * HEAD_DIM])
            keys[rows] = rotate(here[:, GROUP * HEAD_DIM : (GROUP + 1) * HEAD_DIM])
            values[rows] = here[:, (GROUP + 1) * HEAD_DIM :].astype(jnp.bfloat16)

    scale = HEAD_DIM ** (-0.5) * math.log2(math.e)
    tile = 128
    reach = (MOST - 1 + tile - 1) // tile
    for b in range(count // tile):
        first = max(0, b - reach)
        width = (b + 1 - first) * tile
        position = b * tile + lax.broadcasted_iota(jnp.int32, (tile, 1), 0)
        begin, end = jnp.zeros_like(position), jnp.int32(0)
        for j in range(lengths_ref.shape[1]):
            end = end + lengths_ref[0, j]
            begin = jnp.where(position >= end, end, begin)
        key_at = first * tile + lax.broadcasted_iota(jnp.int32, (tile, width), 1)
        allowed = (key_at >= begin) & (key_at <= position)
        key_block = keys[first * tile : (b + 1) * tile]
        value_block = values[first * tile : (b + 1) * tile]
        rows = slice(b * tile, (b + 1) * tile)
        stacked = jnp.concatenate([queries[g, rows] for g in range(GROUP)], axis=0)
        all_scores = lax.dot_general(
            stacked, key_block, (((1,), (1,)), ((), ())), preferred_element_type=jnp.float32
        )
        stacked_weights, totals = [], []
        for g in range(GROUP):
            scores = jnp.where(allowed, all_scores[g * tile : (g + 1) * tile], -1e30)
            weights = jnp.exp2((scores - jnp.max(scores, axis=1, keepdims=True)) * scale)
            totals.append(jnp.sum(weights, axis=1, keepdims=True))
            stacked_weights.append(weights.astype(jnp.bfloat16))
        weighted = jnp.dot(
            jnp.concatenate(stacked_weights, axis=0), value_block, preferred_element_type=jnp.float32
        )
        for g in range(GROUP):
            mixed[rows, g * HEAD_DIM : (g + 1) * HEAD_DIM] = (
                weighted[g * tile : (g + 1) * tile] / totals[g]
            ).astype(jnp.bfloat16)

    left = lax.broadcasted_iota(jnp.int32, (BLOCK, BLOCK), 0)
    source = ((left // 2) % blocks) * part + (left // (2 * blocks)) * 2 + left % 2
    backward = jnp.where(taken == source, 1.0, 0.0).astype(jnp.bfloat16)
    for h in range(blocks):
        chunk = jnp.concatenate(
            [mixed[s * BLOCK + h * part : s * BLOCK + (h + 1) * part] for s in range(blocks)], axis=0
        )
        out_ref[h * BLOCK : (h + 1) * BLOCK] = jnp.dot(
            backward, chunk, preferred_element_type=jnp.float32
        ).astype(jnp.bfloat16)


def attend(member, lengths, lanes, cosine, sine):
    count = cosine.shape[0]
    whole = pl.BlockSpec(memory_space=pltpu.VMEM)
    scalars = pl.BlockSpec(memory_space=pltpu.SMEM)
    return pl.pallas_call(
        attention_kernel,
        out_shape=jax.ShapeDtypeStruct((count, GROUP * HEAD_DIM), jnp.bfloat16),
        in_specs=[scalars, scalars] + [whole] * 6,
        out_specs=whole,
        scratch_shapes=[
            pltpu.VMEM((GROUP, count, HEAD_DIM), jnp.bfloat16),
            pltpu.VMEM((count, HEAD_DIM), jnp.bfloat16),
            pltpu.VMEM((count, HEAD_DIM), jnp.bfloat16),
            pltpu.VMEM((count, GROUP * HEAD_DIM), jnp.bfloat16),
        ],
        compiler_params=pltpu.CompilerParams(vmem_limit_bytes=24 * 2**20),
        name="attend",
    )(member, lengths, *lanes, cosine, sine)


def on_device(tokens, projection, placement, doc_lengths):
    row_count, width = tokens.shape
    devices = placement.shape[1]
    members = lax.axis_size(CTX)
    groups = devices // members
    piece = row_count // devices
    member = lax.axis_index(CTX)

    outgoing, mine, theirs = sort_rows(tokens, placement, projection, member)
    outgoing = outgoing.reshape(groups, row_count // groups, width)
    mine = lax.all_gather(mine, ("x", "y"), axis=0, tiled=True)
    theirs = lax.ppermute(theirs, ("zh", "zl"), [(0, 3), (3, 0), (1, 2), (2, 1)])
    target = (placement[0][:, None] * piece + jnp.arange(piece, dtype=jnp.int32)[None, :]).reshape(row_count)
    arrived = lax.all_to_all(outgoing, DP, 0, 0, tiled=True).reshape(row_count, width)
    tables = rotary_tables(doc_lengths, members * row_count)
    arrived, theirs, tables = lax.optimization_barrier((arrived, theirs, tables))
    places, pieces = gather_weights(mine, theirs, projection.shape[0])
    across = [(0, 1), (1, 0)]
    far = lax.ppermute(arrived, "zl", across)
    near = lax.ppermute(arrived, "core", across)
    lanes = project(places, pieces, [arrived])
    far, lanes = lax.optimization_barrier((far, lanes))
    last = lax.ppermute(far, "core", across)
    lanes = lanes + project(places, pieces, [near, far]) + project(places, pieces, [last])
    mixed = attend(member.reshape(1), doc_lengths, lanes, *tables)
    returned = lax.all_to_all(
        mixed.reshape(devices, members * piece, GROUP * HEAD_DIM), EVERY, 0, 0, tiled=True
    )
    return unsort_rows(returned.reshape(groups, members, members * piece, GROUP * HEAD_DIM), target)


def solution(mesh):
    sizes = {"x": 4, "y": 4, "zh": 2, "zl": 2, "core": 2}
    fine = Mesh(mesh.devices.reshape(tuple(sizes.values())), tuple(sizes))
    return jax.shard_map(
        on_device,
        mesh=fine,
        in_specs=(P(EVERY, None), P(DP, None), P(EVERY, None), P(DP, None)),
        out_specs=P(EVERY, None),
        check_vma=False,
    )
```

```python
import functools
import math

import jax
import jax.numpy as jnp
import numpy as np
from jax import lax
from jax.experimental import pallas as pl
from jax.experimental.pallas import tpu as pltpu
from jax.sharding import Mesh, PartitionSpec as P

HEAD_DIM = 128
HEADS = 16
KV_HEADS = 4
GROUP = HEADS // KV_HEADS
THETA = 500000.0
MOST = 512
DP = ("x", "y", "zh")
CTX = ("zl", "core")
EVERY = DP + CTX
BLOCK = 256


def tables_kernel(lengths_ref, frequency_ref, cos_ref, sin_ref):
    count, width = cos_ref.shape
    step = 128

    @pl.loop(0, count // step)
    def _(i):
        position = i * step + lax.broadcasted_iota(jnp.int32, (step, width), 0)
        begin, end = jnp.zeros_like(position), jnp.int32(0)
        for j in range(lengths_ref.shape[1]):
            end = end + lengths_ref[0, j]
            begin = jnp.where(position >= end, end, begin)
        angle = (position - begin).astype(jnp.float32) * frequency_ref[...]
        rows = pl.ds(pl.multiple_of(i * step, step), step)
        cos_ref[rows] = jnp.cos(angle)
        sine = jnp.sin(angle)
        first = lax.broadcasted_iota(jnp.int32, (step, width), 1) < width // 2
        sin_ref[rows] = jnp.where(first, -sine, sine)


def rotary_tables(lengths, count):
    frequency = THETA ** (-2.0 * np.arange(HEAD_DIM // 2) / HEAD_DIM)
    frequency = np.concatenate([frequency, frequency])[None].astype(np.float32)
    whole = pl.BlockSpec(memory_space=pltpu.VMEM)
    shape = jax.ShapeDtypeStruct((count, HEAD_DIM), jnp.float32)
    return pl.pallas_call(
        tables_kernel,
        out_shape=[shape] * 2,
        in_specs=[pl.BlockSpec(memory_space=pltpu.SMEM), whole],
        out_specs=[pl.BlockSpec((count, HEAD_DIM), lambda: (0, 0))] * 2,
        compiler_params=pltpu.CompilerParams(vmem_limit_bytes=63 * 2**20),
        name="rotary_tables",
    )(lengths, frequency)


def sort_kernel(member_ref, placement_ref, rows_ref, projection_ref, out_ref, mine_ref, theirs_ref, held, moved, columns, *sems):
    in_sems, out_sems, column_sems, head_sems = sems
    count, devices = held.shape[0], placement_ref.shape[1]
    piece = count // devices
    arriving, leaving = [], []
    taking = []
    for i, member in enumerate((member_ref[0], member_ref[0] ^ 2)):
        at, source = 0, 0
        for heads, width in ((KV_HEADS, GROUP * HEAD_DIM), (KV_HEADS, HEAD_DIM), (KV_HEADS, HEAD_DIM)):
            copy = pltpu.make_async_copy(
                projection_ref.at[:, pl.ds(pl.multiple_of(source + member * width, HEAD_DIM), width)],
                columns.at[i, :, pl.ds(at, width)],
                column_sems.at[len(taking)],
            )
            copy.start()
            taking.append(copy)
            at, source = at + width, source + heads * width

    parts = [
        (pl.ds(half * (count // 2), count // 2), pl.ds(block * (held.shape[1] // 4), held.shape[1] // 4))
        for block in range(4)
        for half in range(2)
    ]
    for i, part in enumerate(parts):
        arriving.append(pltpu.make_async_copy(rows_ref.at[part], held.at[part], in_sems.at[i]))
        arriving[-1].start()
    device = lax.broadcasted_iota(jnp.int32, (devices, devices), 0)
    pieces = jnp.where(device == placement_ref[...], 1.0, 0.0).astype(jnp.bfloat16)
    down = lax.broadcasted_iota(jnp.int32, (count, devices), 0) // piece
    tall = jnp.where(down == lax.broadcasted_iota(jnp.int32, (count, devices), 1), 1.0, 0.0).astype(jnp.bfloat16)
    along = lax.broadcasted_iota(jnp.int32, (devices, count), 1) // piece
    wide = jnp.where(along == lax.broadcasted_iota(jnp.int32, (devices, count), 0), 1.0, 0.0).astype(jnp.bfloat16)
    tall = jnp.dot(tall, pieces, preferred_element_type=jnp.float32).astype(jnp.bfloat16)
    both = jnp.dot(tall, wide, preferred_element_type=jnp.float32)
    row = lax.broadcasted_iota(jnp.int32, (count, count), 0) % piece
    same = row == lax.broadcasted_iota(jnp.int32, (count, count), 1) % piece
    one_hot = jnp.where(same, both, 0.0).astype(jnp.bfloat16)

    for block in range(4):
        columns_here = parts[2 * block][1]
        for copy in arriving[2 * block : 2 * block + 2]:
            copy.wait()
        moved[:, columns_here] = jnp.dot(
            one_hot, held[:, columns_here], preferred_element_type=jnp.float32
        ).astype(jnp.bfloat16)
        for i in (2 * block, 2 * block + 1):
            leaving.append(pltpu.make_async_copy(moved.at[parts[i]], out_ref.at[parts[i]], out_sems.at[i]))
            leaving[-1].start()
    for copy in taking:
        copy.wait()
    for i, out in enumerate((mine_ref, theirs_ref)):
        leaving.append(pltpu.make_async_copy(columns.at[i], out, head_sems.at[i]))
        leaving[-1].start()
    for copy in leaving:
        copy.wait()


def sort_rows(tokens, placement, projection, member):
    anywhere = pl.BlockSpec(memory_space=pl.ANY)
    columns = (projection.shape[0], (GROUP + 2) * HEAD_DIM)
    return pl.pallas_call(
        sort_kernel,
        out_shape=[jax.ShapeDtypeStruct(shape, tokens.dtype) for shape in (tokens.shape, columns, columns)],
        in_specs=[
            pl.BlockSpec(memory_space=pltpu.SMEM),
            pl.BlockSpec(memory_space=pltpu.VMEM),
            anywhere,
            anywhere,
        ],
        out_specs=[anywhere] * 3,
        scratch_shapes=[
            pltpu.VMEM(tokens.shape, tokens.dtype),
            pltpu.VMEM(tokens.shape, tokens.dtype),
            pltpu.VMEM((2,) + columns, tokens.dtype),
            pltpu.SemaphoreType.DMA((8,)),
            pltpu.SemaphoreType.DMA((8,)),
            pltpu.SemaphoreType.DMA((6,)),
            pltpu.SemaphoreType.DMA((2,)),
        ],
        compiler_params=pltpu.CompilerParams(vmem_limit_bytes=60 * 2**20),
        name="sort_rows",
    )(member.reshape(1), placement, tokens, projection)


def unsort_kernel(target_ref, rows_ref, out_ref):
    count = out_ref.shape[0]
    blocks, width = rows_ref.shape[1], rows_ref.shape[3]
    order = lax.broadcasted_iota(jnp.int32, (count, count), 1)
    one_hot = jnp.where(order == target_ref[...], 1.0, 0.0).astype(jnp.bfloat16)
    for i in range(blocks):
        rows = rows_ref[:, i].reshape(count, width)
        out_ref[:, i * width : (i + 1) * width] = jnp.dot(
            one_hot, rows, preferred_element_type=jnp.float32
        ).astype(jnp.bfloat16)


def unsort_rows(returned, target):
    groups, blocks, rows, width = returned.shape
    count = groups * rows
    whole = pl.BlockSpec(memory_space=pltpu.VMEM)
    return pl.pallas_call(
        unsort_kernel,
        out_shape=jax.ShapeDtypeStruct((count, blocks * width), returned.dtype),
        in_specs=[whole, whole],
        out_specs=pl.BlockSpec((count, blocks * width), lambda: (0, 0)),
        compiler_params=pltpu.CompilerParams(vmem_limit_bytes=16 * 2**20),
        name="unsort_rows",
    )(target.reshape(count, 1), returned)


def ring_blocks(block, axis):
    ways = [[(i, (i + d) % 4) for i in range(4)] for d in (1, 3, 2)]
    return jnp.concatenate([block] + [lax.ppermute(block, axis, way) for way in ways], axis=0)


UP, DOWN = [(i, (i + 1) % 4) for i in range(4)], [(i, (i + 3) % 4) for i in range(4)]


def spread(blocks):
    pairs = [(lax.ppermute(b, axis, UP), lax.ppermute(b, axis, DOWN)) for b, axis in zip(blocks, ("x", "y"))]
    half = blocks[0].shape[0] // 2
    halves = [h for below, above in pairs for h in (below[:half], above[half:])]
    far = [lax.ppermute(h, axis, way) for h, axis, way in zip(halves, ("x", "x", "y", "y"), (UP, DOWN, UP, DOWN))]
    return [[blocks[i], *pairs[i], *far[2 * i : 2 * i + 2]] for i in range(2)]


RING = (0, 3, 1, 2)
SPAN = ((0, (0, 1, 2, 3)), (3, (0, 1, 2, 3)), (1, (0, 1, 2, 3)), (2, (0, 1)), (2, (2, 3)))


def gather_weights(mine, theirs, rows):
    x, y, zh = lax.axis_index("x"), lax.axis_index("y"), lax.axis_index("zh")
    half = theirs.shape[1] // 2
    pieces = [mine]
    places = [(i * 2 + zh) * rows for i in range(16)]
    ready = lax.optimization_barrier([ring_blocks(theirs[:, :half], "y"), ring_blocks(theirs[:, half:], "x")])
    for side, spreads in enumerate(spread(ready)):
        pieces += spreads
        for outer, inners in SPAN:
            for inner in inners:
                near, far = (outer, RING[inner]) if side == 0 else (RING[inner], outer)
                places.append(((x + near) % 4 * 8 + (y + far) % 4 * 2 + 1 - zh) * rows)
    return jnp.stack(places), pieces


def project_kernel(parts, places_ref, *refs):
    row_refs, refs = refs[:parts], refs[parts:]
    pieces, out_refs, ordered = refs[: -parts - 1], refs[-parts - 1 : -1], refs[-1]
    half = out_refs[0].shape[1] // 2
    step = 128

    def take(first, count):
        for i in range(count):
            column = pl.multiple_of(places_ref[first + i], step)
            at = 0
            for rows in row_refs:
                ordered[at : at + rows.shape[0], i * step : (i + 1) * step] = rows[:, pl.ds(column, step)]
                at += rows.shape[0]

    def product(pieces):
        total, at = None, 0
        for piece in pieces:
            depth = piece.shape[0]
            term = jnp.dot(ordered[:, at : at + depth], piece[...], preferred_element_type=jnp.float32)
            total = term if total is None else total + term
            at += depth
        return total

    take(0, 16)
    out = product(pieces[:1])
    for side in range(2):
        take(16 + side * 16, 16)
        columns = slice(side * half, (side + 1) * half)
        here = (out[:, columns] + product(pieces[1 + side * 5 : 6 + side * 5])).astype(jnp.bfloat16)
        at = 0
        for out_ref in out_refs:
            out_ref[:, columns] = here[at : at + out_ref.shape[0]]
            at += out_ref.shape[0]


def project(places, pieces, rows):
    count, depth = sum(r.shape[0] for r in rows), rows[0].shape[1]
    width = pieces[0].shape[1]
    whole = pl.BlockSpec(memory_space=pltpu.VMEM)
    return pl.pallas_call(
        functools.partial(project_kernel, len(rows)),
        out_shape=[jax.ShapeDtypeStruct((r.shape[0], width), jnp.bfloat16) for r in rows],
        in_specs=[pl.BlockSpec(memory_space=pltpu.SMEM)] + [whole] * (len(rows) + len(pieces)),
        out_specs=[whole] * len(rows),
        scratch_shapes=[pltpu.VMEM((count, depth // 2), jnp.bfloat16)],
        compiler_params=pltpu.CompilerParams(vmem_limit_bytes=24 * 2**20),
        cost_estimate=pl.CostEstimate(
            flops=2 * count * depth * width, bytes_accessed=2 * depth * (width + count), transcendentals=0
        ),
        name="project",
    )(places, *rows, *pieces)


def attention_kernel(member_ref, lengths_ref, *refs):
    lanes = refs[:4]
    cos_ref, sin_ref, out_ref, queries, keys, values, mixed = refs[4:]
    count = cos_ref.shape[0]
    blocks = count // BLOCK
    part = BLOCK // blocks
    half = HEAD_DIM // 2
    member = member_ref[0]

    taken = lax.broadcasted_iota(jnp.int32, (BLOCK, BLOCK), 1)
    lane, rest = taken // part, taken % part
    group, slot, row = rest // (2 * blocks), (rest // 2) % blocks, rest % 2
    placed = slot * part + (group * 4 + (lane ^ member)) * 2 + row
    wanted = lax.broadcasted_iota(jnp.int32, (BLOCK, BLOCK), 0)
    forward = jnp.where(wanted == placed, 1.0, 0.0).astype(jnp.bfloat16)
    for h in range(blocks):
        chunk = jnp.concatenate([lane_ref[h * part : (h + 1) * part] for lane_ref in lanes], axis=0)
        chunk = jnp.dot(forward, chunk, preferred_element_type=jnp.float32)
        for s in range(blocks):
            rows = slice(s * BLOCK + h * part, s * BLOCK + (h + 1) * part)
            here = chunk[s * part : (s + 1) * part]
            cosine, sine = cos_ref[rows], sin_ref[rows]

            def rotate(x):
                return (x * cosine + pltpu.roll(x, half, 1) * sine).astype(jnp.bfloat16)

            for g in range(GROUP):
                queries[g, rows] = rotate(here[:, g * HEAD_DIM : (g + 1) * HEAD_DIM])
            keys[rows] = rotate(here[:, GROUP * HEAD_DIM : (GROUP + 1) * HEAD_DIM])
            values[rows] = here[:, (GROUP + 1) * HEAD_DIM :].astype(jnp.bfloat16)

    scale = HEAD_DIM ** (-0.5) * math.log2(math.e)
    tile = 128
    reach = (MOST - 1 + tile - 1) // tile
    for b in range(count // tile):
        first = max(0, b - reach)
        width = (b + 1 - first) * tile
        position = b * tile + lax.broadcasted_iota(jnp.int32, (tile, 1), 0)
        begin, end = jnp.zeros_like(position), jnp.int32(0)
        for j in range(lengths_ref.shape[1]):
            end = end + lengths_ref[0, j]
            begin = jnp.where(position >= end, end, begin)
        key_at = first * tile + lax.broadcasted_iota(jnp.int32, (tile, width), 1)
        allowed = (key_at >= begin) & (key_at <= position)
        key_block = keys[first * tile : (b + 1) * tile]
        value_block = values[first * tile : (b + 1) * tile]
        rows = slice(b * tile, (b + 1) * tile)
        stacked = jnp.concatenate([queries[g, rows] for g in range(GROUP)], axis=0)
        all_scores = lax.dot_general(
            stacked, key_block, (((1,), (1,)), ((), ())), preferred_element_type=jnp.float32
        )
        stacked_weights, totals = [], []
        for g in range(GROUP):
            scores = jnp.where(allowed, all_scores[g * tile : (g + 1) * tile], -1e30)
            weights = jnp.exp2((scores - jnp.max(scores, axis=1, keepdims=True)) * scale)
            totals.append(jnp.sum(weights, axis=1, keepdims=True))
            stacked_weights.append(weights.astype(jnp.bfloat16))
        weighted = jnp.dot(
            jnp.concatenate(stacked_weights, axis=0), value_block, preferred_element_type=jnp.float32
        )
        for g in range(GROUP):
            mixed[rows, g * HEAD_DIM : (g + 1) * HEAD_DIM] = (
                weighted[g * tile : (g + 1) * tile] / totals[g]
            ).astype(jnp.bfloat16)

    left = lax.broadcasted_iota(jnp.int32, (BLOCK, BLOCK), 0)
    source = ((left // 2) % blocks) * part + (left // (2 * blocks)) * 2 + left % 2
    backward = jnp.where(taken == source, 1.0, 0.0).astype(jnp.bfloat16)
    for h in range(blocks):
        chunk = jnp.concatenate(
            [mixed[s * BLOCK + h * part : s * BLOCK + (h + 1) * part] for s in range(blocks)], axis=0
        )
        out_ref[h * BLOCK : (h + 1) * BLOCK] = jnp.dot(
            backward, chunk, preferred_element_type=jnp.float32
        ).astype(jnp.bfloat16)


def attend(member, lengths, lanes, cosine, sine):
    count = cosine.shape[0]
    whole = pl.BlockSpec(memory_space=pltpu.VMEM)
    scalars = pl.BlockSpec(memory_space=pltpu.SMEM)
    return pl.pallas_call(
        attention_kernel,
        out_shape=jax.ShapeDtypeStruct((count, GROUP * HEAD_DIM), jnp.bfloat16),
        in_specs=[scalars, scalars] + [whole] * 6,
        out_specs=whole,
        scratch_shapes=[
            pltpu.VMEM((GROUP, count, HEAD_DIM), jnp.bfloat16),
            pltpu.VMEM((count, HEAD_DIM), jnp.bfloat16),
            pltpu.VMEM((count, HEAD_DIM), jnp.bfloat16),
            pltpu.VMEM((count, GROUP * HEAD_DIM), jnp.bfloat16),
        ],
        compiler_params=pltpu.CompilerParams(vmem_limit_bytes=24 * 2**20),
        name="attend",
    )(member, lengths, *lanes, cosine, sine)


def on_device(tokens, projection, placement, doc_lengths):
    row_count, width = tokens.shape
    devices = placement.shape[1]
    members = lax.axis_size(CTX)
    groups = devices // members
    piece = row_count // devices
    member = lax.axis_index(CTX)

    outgoing, mine, theirs = sort_rows(tokens, placement, projection, member)
    outgoing = outgoing.reshape(groups, row_count // groups, width)
    mine = lax.all_gather(mine, ("x", "y"), axis=0, tiled=True)
    theirs = lax.ppermute(theirs, ("zh", "zl"), [(0, 3), (3, 0), (1, 2), (2, 1)])
    target = (placement[0][:, None] * piece + jnp.arange(piece, dtype=jnp.int32)[None, :]).reshape(row_count)
    arrived = lax.all_to_all(outgoing, DP, 0, 0, tiled=True).reshape(row_count, width)
    tables = rotary_tables(doc_lengths, members * row_count)
    arrived, theirs, tables = lax.optimization_barrier((arrived, theirs, tables))
    places, pieces = gather_weights(mine, theirs, projection.shape[0])
    across = [(0, 1), (1, 0)]
    far = lax.ppermute(arrived, "zl", across)
    near = lax.ppermute(arrived, "core", across)
    lanes = project(places, pieces, [arrived])
    far, lanes = lax.optimization_barrier((far, lanes))
    last = lax.ppermute(far, "core", across)
    lanes = lanes + project(places, pieces, [near, far]) + project(places, pieces, [last])
    mixed = attend(member.reshape(1), doc_lengths, lanes, *tables)
    returned = lax.all_to_all(
        mixed.reshape(devices, members * piece, GROUP * HEAD_DIM), EVERY, 0, 0, tiled=True
    )
    return unsort_rows(returned.reshape(groups, members, members * piece, GROUP * HEAD_DIM), target)


def solution(mesh):
    sizes = {"x": 4, "y": 4, "zh": 2, "zl": 2, "core": 2}
    fine = Mesh(mesh.devices.reshape(tuple(sizes.values())), tuple(sizes))
    return jax.shard_map(
        on_device,
        mesh=fine,
        in_specs=(P(EVERY, None), P(DP, None), P(EVERY, None), P(DP, None)),
        out_specs=P(EVERY, None),
        check_vma=False,
    )
```
